512 devices in a mesh: row: 32 (over z_lo, y), col: 16 (over z_hi, x, core).
Axes of the slice: x: 4, y: 4, z: 16 (z_hi: 2, z_lo: 8; z = z_hi * 8 + z_lo), core: 2. Of those that a mesh axis runs over, the one named last changes fastest.
Arguments:
- water_depth: float32 [2048, 2048], P('row', 'col'), may hold values from 1 to 2
- discharge: float32 [2, 2048, 2048], P(None, 'row', 'col'), may hold values from -1.5 to 1.5
- sediment: float32 [4, 2048, 2048], P(None, 'row', 'col'), may hold values from 0.01 to 0.1
- bed_level: float32 [512, 512], P(('row', 'col')), may hold values from -3 to 3
- cell_map: int32 [2048, 2048], P('row', 'col'), may hold values from 0 to 8191, as said below
- wet_mask: int32 [2048, 2048], P('row', 'col'), may hold values 0 or 1
- sediment_params: float32 [3, 4], replicated, may hold values from 0.5 to 2
Outputs:
- depth_out: float32 [2048, 2048], P('row', 'col')
- discharge_out: float32 [2, 2048, 2048], P(None, 'row', 'col')
- sediment_out: float32 [4, 2048, 2048], P(None, 'row', 'col')
- fine_bed: float32 [2048, 2048], P('row', 'col')
- bed_out: float32 [512, 512], P(('row', 'col'))
- deposit: float32 [4, 512, 512], P(None, ('row', 'col'))
The draws below stay inside these ranges and needn't reach their ends.
Inputs may be any that keep to these rules, and one draw needn't show every extreme that they name: cell_map[i, j] = r * 512 + c with r within 1 of (i % 64) // 4 and 0 <= r < 16, and c within 3 of j // 4.
All inputs are finite; a program needn't handle non-finite values. No bound on the sum of `wet_mask` on one device may be relied on, other than what follows from the above.
Results may differ from the reference program's by a relative error of at most 0.0003.
Values sent between devices are 32-bit elements; how exact they have to be, the bound alone decides.
A program may use at most 64 MiB of HBM per device.

```python
import math
import jax
import jax.numpy as jnp
from jax import lax

CX = 64
FRACTIONS = 4
SUBSTEPS = 4
NX = 2048
NY = 2048
NXC = 512
NYC = 512


def draw_cell_map(key, part):
    row_ids = jnp.arange(NX, dtype=jnp.int32)[:, None] % CX
    col_ids = jnp.arange(NY, dtype=jnp.int32)[None, :]
    shift_row = jax.random.randint(jax.random.fold_in(key, 11), (NX, NY), -1, 2, dtype=jnp.int32)
    shift_col = jax.random.randint(jax.random.fold_in(key, 12), (NX, NY), -3, 4, dtype=jnp.int32)
    band_row = jnp.clip(row_ids // 4 + shift_row, 0, CX // 4 - 1)
    coarse_col = jnp.clip(col_ids // 4 + shift_col, 0, NY // 4 - 1)
    return (band_row * (NY // 4) + coarse_col).astype(jnp.int32)


def plant(array, rng, smallest, high):
    index_at = [jax.random.randint(jax.random.fold_in(rng, axis), (), 0, length) for axis, length in enumerate(array.shape)]
    widest = array.shape.index(max(array.shape))
    beside = index_at[:widest] + [(index_at[widest] + 1) % array.shape[widest]] + index_at[widest + 1:]
    return array.at[tuple(index_at)].set(smallest).at[tuple(beside)].set(high)


def level_of(stream_key, shape, split, least, top_value):
    def one(axis_at, shards_of):
        heights = jax.random.uniform(jax.random.fold_in(jax.random.fold_in(stream_key, 6), axis_at), (shards_of,), jnp.float32, least / len(split), top_value / len(split))
        return jnp.repeat(jnp.exp(heights), shape[axis_at] // shards_of).reshape((-1,) + (1,) * (len(shape) - axis_at - 1))

    gain = one(*split[0])
    for cut in split[1:]:
        gain = gain * one(*cut)
    return gain


def noise(own_key, extent, width, reach, shards=(), kind=jnp.bfloat16):
    gain = level_of(own_key, extent, shards, -0.22, 0.18) if shards else 1.0
    drawn = jax.random.normal(own_key, extent, jnp.float32) * width * gain
    return jnp.minimum(jnp.maximum(drawn, -reach), reach).astype(kind)


def setup_inputs(seed: int = 0) -> dict:
    arg_keys = jax.random.split(jax.random.key(seed), 8)
    water_depth = jnp.clip(1.0 + 1.0 * jax.random.uniform(arg_keys[0], (NX, NY), jnp.float32) ** level_of(arg_keys[0], (NX, NY), ((0, 32), (1, 16)), -0.2, 0.2), 1.0, 2.0)
    discharge = noise(arg_keys[1], (2, NX, NY), 0.3, 1.5, ((1, 32), (2, 16)), jnp.float32)
    sediment = jnp.clip(jnp.exp(math.log(0.1) - 2.3025851 * jax.random.uniform(arg_keys[2], (FRACTIONS, NX, NY), jnp.float32) ** level_of(arg_keys[2], (FRACTIONS, NX, NY), ((1, 32), (2, 16)), -0.2, 0.2)), 0.01, 0.1)
    bed_level = noise(arg_keys[3], (NXC, NYC), 0.3, 3.0, ((0, 512),), jnp.float32)
    cell_map = draw_cell_map(jax.random.fold_in(arg_keys[7], 71), 0)
    wet_mask = plant((jax.random.randint(arg_keys[5], (NX, NY), 0, 10) < 9).astype(jnp.int32), jax.random.fold_in(arg_keys[5], 1), 0, 1)
    sediment_params = jnp.clip(jnp.exp(jax.random.uniform(arg_keys[6], (3, FRACTIONS), jnp.float32, math.log(0.5), math.log(2.0))), 0.5, 2.0)
    return {"water_depth": water_depth, "discharge": discharge, "sediment": sediment, "bed_level": bed_level, "cell_map": cell_map, "wet_mask": wet_mask, "sediment_params": sediment_params}


gravity = 1.0
time_step = 0.2
depth_floor = 1.25
drag_coeff = 0.02
settle_base = 0.05
critical_base = 0.05
erode_base = 0.002
exner_factor = 400.0

def minmod(lower_diff, upper_diff):
    return 0.5 * (jnp.sign(lower_diff) + jnp.sign(upper_diff)) * jnp.minimum(jnp.abs(lower_diff), jnp.abs(upper_diff))

def physical(fields, normal):
    depths = fields[0]
    speed = fields[normal] / jnp.maximum(depths, depth_floor)
    fluxes = fields * speed[None]
    fluxes = fluxes.at[normal].add(0.5 * gravity * depths * depths)
    celerity = jnp.abs(speed) + jnp.sqrt(gravity * depths)
    return (fluxes, celerity)

def face_flux(left_state, right_state, normal):
    left_flux, left_wave = physical(left_state, normal)
    right_flux, right_wave = physical(right_state, normal)
    fastest = jnp.maximum(left_wave, right_wave)
    return 0.5 * (left_flux + right_flux) - 0.5 * fastest[None] * (right_state - left_state)

def advance(fields, bed_pad, wet_pad, params):
    center = fields[:, 2:-2, 2:-2]
    along_rows = fields[:, :, 2:-2]
    slopes = minmod(along_rows[:, 1:-1] - along_rows[:, :-2], along_rows[:, 2:] - along_rows[:, 1:-1])
    middle = along_rows[:, 1:-1]
    left_state = (middle + 0.5 * slopes)[:, :-1]
    right_state = (middle - 0.5 * slopes)[:, 1:]
    open_x = wet_pad[1:-2, 2:-2] * wet_pad[2:-1, 2:-2]
    fluxes = face_flux(left_state, right_state, 1) * open_x[None]
    net_x = fluxes[:, 1:] - fluxes[:, :-1]
    along_cols = fields[:, 2:-2, :]
    slopes = minmod(along_cols[:, :, 1:-1] - along_cols[:, :, :-2], along_cols[:, :, 2:] - along_cols[:, :, 1:-1])
    middle = along_cols[:, :, 1:-1]
    left_state = (middle + 0.5 * slopes)[:, :, :-1]
    right_state = (middle - 0.5 * slopes)[:, :, 1:]
    open_y = wet_pad[2:-2, 1:-2] * wet_pad[2:-2, 2:-1]
    fluxes = face_flux(left_state, right_state, 2) * open_y[None]
    net_y = fluxes[:, :, 1:] - fluxes[:, :, :-1]
    depths = center[0]
    floored = jnp.maximum(depths, depth_floor)
    along_x = center[1] / floored
    along_y = center[2] / floored
    velocity_mag = jnp.sqrt(along_x * along_x + along_y * along_y + 1e-06)
    bed_x = 0.5 * (bed_pad[3:-1, 2:-2] - bed_pad[1:-3, 2:-2])
    bed_y = 0.5 * (bed_pad[2:-2, 3:-1] - bed_pad[2:-2, 1:-3])
    source_x = -gravity * depths * bed_x - drag_coeff * velocity_mag * along_x
    source_y = -gravity * depths * bed_y - drag_coeff * velocity_mag * along_y
    settling = settle_base * params[0][:, None, None] * center[3:] / floored[None]
    critical = critical_base * params[1][:, None, None]
    erosion = erode_base * params[2][:, None, None] * jnp.maximum((velocity_mag * velocity_mag)[None] / critical - 1.0, 0.0)
    exchange = settling - erosion
    sources = jnp.concatenate([jnp.zeros_like(depths)[None], source_x[None], source_y[None], -exchange], axis=0)
    wet_center = wet_pad[2:-2, 2:-2][None]
    updated = center + time_step * wet_center * (sources - net_x - net_y)
    return (updated, time_step * wet_center * exchange)

def reference(water_depth, discharge, sediment, bed_level, cell_map, wet_mask, sediment_params):
    coarse_rows, coarse_cols = bed_level.shape
    row_ids = jnp.arange(NX, dtype=jnp.int32)[:, None]
    band_start = row_ids // CX * (CX // 4)
    coarse_index = ((band_start + cell_map // coarse_cols) * coarse_cols + cell_map % coarse_cols).astype(jnp.int32)
    bed_start = bed_level.reshape(-1)[coarse_index]
    wet = wet_mask.astype(jnp.float32)
    fields = jnp.concatenate([water_depth[None], discharge, sediment], axis=0)
    bed_pad = jnp.pad(bed_start, 2)
    wet_pad = jnp.pad(wet, 2)
    exchanged = jnp.zeros((FRACTIONS, NX, NY), jnp.float32)
    for substep in range(SUBSTEPS):
        fields, change = advance(jnp.pad(fields, ((0, 0), (2, 2), (2, 2))), bed_pad, wet_pad, sediment_params)
        exchanged = exchanged + change
    flat_ids = coarse_index.reshape(-1)
    sums = jax.vmap(lambda column: jax.ops.segment_sum(column, flat_ids, num_segments=coarse_rows * coarse_cols))(exchanged.reshape(FRACTIONS, -1))
    deposit = exner_factor / 16.0 * sums.reshape(FRACTIONS, coarse_rows, coarse_cols)
    bed_new = bed_level + lax.optimization_barrier(jnp.sum(deposit, axis=0))
    fine_bed = bed_new.reshape(-1)[coarse_index]
    return (fields[0], fields[1:3], fields[3:], fine_bed, bed_new, deposit)
```

```python
import jax
import jax.numpy as jnp
from jax import lax
from jax.experimental import pallas as pl
from jax.experimental.pallas import tpu as pltpu
from jax.sharding import PartitionSpec as P

FRACTIONS = 4
SUBSTEPS = 4
ROWS = 32
COLS = 16
SEG = 10

MESH = pl.DeviceIdType.MESH
f32 = jnp.float32
i32 = jnp.int32


def roll(x, shift, axis):
    return pltpu.roll(x, shift % x.shape[axis], axis)


def minmod(a, b):
    return jnp.maximum(jnp.minimum(b, 0.0), jnp.minimum(a, jnp.maximum(b, 0.0)))


def face_factors(h_l, n_l, h_r, n_r, opened):
    w_l = n_l / jnp.maximum(h_l, 2.5)
    w_r = n_r / jnp.maximum(h_r, 2.5)
    c_l = jnp.abs(w_l) + jnp.sqrt(0.5 * h_l)
    c_r = jnp.abs(w_r) + jnp.sqrt(0.5 * h_r)
    fastest = jnp.maximum(c_l, c_r)
    push = (0.25 * opened) * (h_l * h_l + h_r * h_r)
    return opened * (w_l + fastest), opened * (w_r - fastest), push


def kernel(
    depth, disch, sed, bed, cmap, wetm, par,
    o_depth, o_disch, o_sed, o_fine, o_bed, o_dep,
    nat, raw, bedv, pk, rx, strips, band, band2, cn, nbed,
    ibuf, rbuf, kbuf, fld, wet, gx, gy, ox, oy, wd, lc, fc, coef,
    exch, on, exn, sel, mhi, mlo, tot, nsum, nrx, rs, wnew, fineb, depv, bedo,
    in_sem, nb_send, nb_recv, st_send, st_recv, ph_send, ph_recv, ns_send, ns_recv, out_sem,
):
    R = lax.axis_index("row")
    C = lax.axis_index("col")
    barrier = pltpu.get_barrier_semaphore()

    def greet(c, carry):
        near = jnp.abs(c - C) <= 1

        @pl.when(c != C)
        def _():
            pl.semaphore_signal(barrier, inc=1, device_id=(R, c), device_id_type=MESH)

        @pl.when(jnp.logical_and(R > 0, jnp.logical_or(near, c >= COLS - 3)))
        def _():
            pl.semaphore_signal(barrier, inc=1, device_id=(R - 1, c), device_id_type=MESH)

        @pl.when(jnp.logical_and(R < ROWS - 1, jnp.logical_or(near, c <= 2)))
        def _():
            pl.semaphore_signal(barrier, inc=1, device_id=(R + 1, c), device_id_type=MESH)

        return carry

    lax.fori_loop(0, COLS, greet, 0)

    mid = pl.ds(8, 64)
    loads = [
        pltpu.make_async_copy(depth, nat.at[0, mid], in_sem.at[0]),
        pltpu.make_async_copy(disch, nat.at[pl.ds(1, 2), mid], in_sem.at[1]),
        pltpu.make_async_copy(sed, nat.at[pl.ds(3, 4), mid], in_sem.at[2]),
        pltpu.make_async_copy(bed, bedv, in_sem.at[3]),
        pltpu.make_async_copy(cmap, raw.at[0], in_sem.at[4]),
        pltpu.make_async_copy(wetm, raw.at[1], in_sem.at[5]),
    ]
    for copy in loads:
        copy.start()

    lane = lax.broadcasted_iota(i32, (8, 128), 1)
    sub = lax.broadcasted_iota(i32, (8, 128), 0)
    masks = [((lane + 8 - 16 * q) & 127) < 16 for q in range(8)]

    far = f32(1 << 20)

    @pl.when(R == 0)
    def _():
        nat[0:8, 0:8, :] = jnp.zeros((8, 8, 128), f32)
        nat[8, 0:8, :] = jnp.full((8, 128), far)
        band[0:3] = jnp.zeros((3, 1, 128), f32)

    @pl.when(R == ROWS - 1)
    def _():
        nat[0:8, 72:80, :] = jnp.zeros((8, 8, 128), f32)
        nat[8, 72:80, :] = jnp.full((8, 128), far)
        band[19:22] = jnp.zeros((3, 1, 128), f32)

    for side, edge in ((0, C == COLS - 1), (1, C == 0)):

        @pl.when(edge)
        def _(side=side):
            rx[side, 0] = jnp.full((8, 128), far)
            rx[side, 1:9] = jnp.zeros((8, 8, 128), f32)

        @pl.when(jnp.logical_or(edge, R == 0))
        def _(side=side):
            rx[side, 9] = jnp.zeros((8, 128), f32)
            rx[side, 10] = jnp.full((8, 128), far)

        @pl.when(jnp.logical_or(edge, R == ROWS - 1))
        def _(side=side):
            rx[side, 11] = jnp.full((8, 128), far)
            rx[side, 12] = jnp.zeros((8, 128), f32)

    @pl.when(C == COLS - 1)
    def _():
        nrx[0] = jnp.zeros((16, 128), f32)

    @pl.when(C == 0)
    def _():
        nrx[1] = jnp.zeros((16, 128), f32)

    tot[...] = jnp.zeros((128, 128), f32)
    wnew[...] = jnp.zeros((24, 128), f32)

    from_col = lax.broadcasted_iota(i32, (128, 128), 0) // 4
    to_lane = lax.broadcasted_iota(i32, (128, 128), 1)
    for d in range(7):
        sel[128 * d : 128 * d + 128, :] = (
            jnp.where(to_lane - from_col == d + 5, 1.0, 0.0).astype(jnp.bfloat16)
        )

    for k in range(FRACTIONS):
        erode = 0.002 * jnp.full((8, 128), par[2, k], f32)
        coef[0, k] = 0.05 * jnp.full((8, 128), par[0, k], f32)
        coef[1, k] = erode / (0.05 * jnp.full((8, 128), par[1, k], f32))
        coef[2, k] = erode

    for copy in loads:
        copy.wait()
    nat[8, 8:72, :] = raw[0].astype(f32)
    nat[7, 8:72, :] = raw[1].astype(f32)

    at = 32 * lax.broadcasted_iota(i32, (16, 128), 0) - 8 + lax.broadcasted_iota(i32, (16, 128), 1)
    window = jnp.zeros((16, 128), f32)
    for q in range(4):
        chunk = jnp.broadcast_to(bedv[:, 128 * q : 128 * q + 128], (16, 128))
        got = jnp.take_along_axis(chunk, at & 127, axis=1, mode="promise_in_bounds")
        window = jnp.where((at >> 7) == q, got, window)
    for t in range(COLS):
        strips[t] = window[t : t + 1, :]

    map_pack = None
    for g in range(8):
        rows = slice(8 + 8 * g, 16 + 8 * g)
        packed = nat[0, rows, :]
        for q in range(1, 8):
            packed = jnp.where(masks[q], roll(nat[q, rows, :], 16 * q, 1), packed)
        pk[1 + g] = packed
        moved = roll(nat[8, rows, :], 16 * g, 1)
        map_pack = moved if g == 0 else jnp.where(masks[g], moved, map_pack)
    pk[0] = map_pack
    pk[9] = map_pack

    up, down = R > 0, R < ROWS - 1
    left, right = C > 0, C < COLS - 1
    both = jnp.logical_and
    above = jnp.where(C <= 2, COLS, jnp.where(C == COLS - 1, 2, 3))
    below = jnp.where(C >= COLS - 3, COLS, jnp.where(C == 0, 2, 3))
    expected = COLS - 1 + jnp.where(up, above, 0) + jnp.where(down, below, 0)
    pl.semaphore_wait(barrier, expected)

    def remote(src, dst, send, recv, device):
        return pltpu.make_async_remote_copy(
            src_ref=src, dst_ref=dst, send_sem=send, recv_sem=recv,
            device_id=device, device_id_type=MESH,
        )

    plan = [
        (left, pk.at[pl.ds(0, 9)], rx.at[0, pl.ds(0, 9)], (R, C - 1), right),
        (right, pk.at[pl.ds(0, 9)], rx.at[1, pl.ds(0, 9)], (R, C + 1), left),
        (up, nat.at[:, pl.ds(8, 8)], nat.at[:, pl.ds(72, 8)], (R - 1, C), down),
        (down, nat.at[:, pl.ds(64, 8)], nat.at[:, pl.ds(0, 8)], (R + 1, C), up),
        (both(up, left), pk.at[pl.ds(0, 2)], rx.at[0, pl.ds(11, 2)], (R - 1, C - 1), both(down, right)),
        (both(up, right), pk.at[pl.ds(0, 2)], rx.at[1, pl.ds(11, 2)], (R - 1, C + 1), both(down, left)),
        (both(down, left), pk.at[pl.ds(8, 2)], rx.at[0, pl.ds(9, 2)], (R + 1, C - 1), both(up, right)),
        (both(down, right), pk.at[pl.ds(8, 2)], rx.at[1, pl.ds(9, 2)], (R + 1, C + 1), both(up, left)),
    ]
    for n, (sends, src, dst, device, _) in enumerate(plan):

        @pl.when(sends)
        def _(n=n, src=src, dst=dst, device=device):
            remote(src, dst, nb_send.at[n], nb_recv.at[n], device).start()

    def send_strips(t, carry):
        @pl.when(t != C)
        def _():
            remote(strips.at[t], band.at[3 + C], st_send.at[0], st_recv.at[0], (R, t)).start()

        @pl.when(both(C <= 2, up))
        def _():
            remote(strips.at[t], band.at[19 + C], st_send.at[1], st_recv.at[1], (R - 1, t)).start()

        @pl.when(both(C >= COLS - 3, down))
        def _():
            remote(strips.at[t], band.at[C - 13], st_send.at[1], st_recv.at[2], (R + 1, t)).start()

        return carry

    lax.fori_loop(0, COLS, send_strips, 0)
    band[3 + C] = strips[C]

    for n, (_, src, dst, device, gets) in enumerate(plan):

        @pl.when(gets)
        def _(n=n, src=src, dst=dst, device=device):
            pltpu.make_async_copy(src, dst, nb_recv.at[n]).wait()

    lower_half = (lane & 15) < 8
    for g in range(10):
        slot = 9 if g == 0 else (12 if g == 9 else g)
        cn[8 * g : 8 * g + 8, :] = jnp.where(lower_half, rx[0, slot], rx[1, slot])
    for t in range(SEG):
        side = cn[pl.ds(t, 8, stride=SEG), :]
        for q in range(8):
            rolled = roll(side, -16 * q, 1)
            own = nat[q, pl.ds(t, 8, stride=SEG), :]
            if q < 7:
                fld[q, t + 2, :, 0:128] = own
                fld[q, t + 2, :, 128:256] = rolled
            else:
                wet[t + 1, :, 0:128] = own
                wet[t + 1, :, 128:256] = rolled
    wet[0] = roll(wet[SEG], 1, 0)
    wet[SEG + 1] = roll(wet[1], -1, 0)
    for t in range(-1, SEG):
        w = wet[t + 1]
        ox[t + 1] = 0.05 * w * wet[t + 2]
        if t >= 0:
            oy[t] = 0.05 * w * roll(w, -1, 1)
            wd[t] = 0.2 * w

    pltpu.make_async_copy(strips.at[pl.ds(0, 15)], band.at[pl.ds(3, 15)], st_recv.at[0]).wait()

    @pl.when(down)
    def _():
        pltpu.make_async_copy(strips.at[pl.ds(0, 3)], band.at[pl.ds(19, 3)], st_recv.at[1]).wait()

    @pl.when(up)
    def _():
        pltpu.make_async_copy(strips.at[pl.ds(0, 3)], band.at[pl.ds(0, 3)], st_recv.at[2]).wait()

    for e in range(22):
        band2[e : e + 1, :] = band[e]

    map_side = jnp.where(lower_half, rx[0, 0], rx[1, 0])
    map_top = jnp.where(lower_half, rx[0, 10], rx[1, 10])
    map_low = jnp.where(lower_half, rx[0, 11], rx[1, 11])
    top_half = sub < 4

    def looked_up(table, first_row, index, shift):
        rows = [jnp.broadcast_to(table[first_row + n : first_row + n + 1, :], (8, 128)) for n in range(4)]
        result = jnp.zeros((8, 128), f32)
        for n in range(3):
            pair = jnp.where(top_half, rows[n], rows[n + 1])
            got = jnp.take_along_axis(pair, index, axis=1, mode="promise_in_bounds")
            result = jnp.where(shift == n - 1, got, result)
        return result

    for g in range(10):
        rows = slice(8 * g, 8 * g + 8)
        if g == 0:
            beside = roll(map_top, -16 * 7, 1)
        elif g == 9:
            beside = map_low
        else:
            beside = roll(map_side, -16 * (g - 1), 1)
        for tile, values in enumerate((nat[8, rows, :], beside)):
            cells = values.astype(i32)
            base = 2 * g - 2 + (sub >> 2)
            shift = (cells >> 9) - base + (-16 if g == 0 else (16 if g == 9 else 0))
            index = ((cells & 511) - 32 * C + 8) & 127
            nbed[tile, rows, :] = looked_up(band2, 2 * g - 2 - 1 + 3, index, shift)
            if tile == 0:
                ibuf[rows, :] = index
                rbuf[rows, :] = shift
                kbuf[rows, :] = (shift + 1) * 7 + (index - 8 - (lane >> 2) + 3)

    def bed_plane(t):
        return jnp.concatenate(
            [nbed[0, pl.ds(t, 8, stride=SEG), :], nbed[1, pl.ds(t, 8, stride=SEG), :]], axis=1
        )

    for t in range(SEG):
        here = bed_plane(t)
        below_bed = roll(bed_plane(SEG - 1), 1, 0) if t == 0 else bed_plane(t - 1)
        above_bed = roll(bed_plane(0), -1, 0) if t == SEG - 1 else bed_plane(t + 1)
        scale = -0.5 * wd[t]
        gx[t] = scale * (above_bed - below_bed)
        gy[t] = scale * (roll(here, -1, 1) - roll(here, 1, 1))

    exch[...] = jnp.zeros(exch.shape, f32)

    def x_states(q, t):
        q0, q1, q2 = fld[q, t + 2], fld[q, t + 3], fld[q, t + 4]
        s = minmod(q1 - q0, q2 - q1)
        twice = q1 + q1
        return twice + s, twice - s

    def substep(_, carry):
        for q in range(7):
            fld[q, 0] = roll(fld[q, 10], 1, 0)
            fld[q, 1] = roll(fld[q, 11], 1, 0)
            fld[q, 12] = roll(fld[q, 2], -1, 0)
            fld[q, 13] = roll(fld[q, 3], -1, 0)
        for q in range(7):
            q0, q1, q2 = fld[q, 0], fld[q, 1], fld[q, 2]
            s = minmod(q1 - q0, q2 - q1)
            lc[q] = q1 + q1 + s

        def x_faces(t):
            lows = {}
            for q in (0, 1):
                left_new, right_new = x_states(q, t)
                lows[q] = (lc[q], left_new, right_new)
            a, b, push = face_factors(lows[0][0], lows[1][0], lows[0][2], lows[1][2], ox[t + 1])
            net = []
            for q in range(7):
                if q in lows:
                    left_old, left_new, right_new = lows[q]
                else:
                    left_new, right_new = x_states(q, t)
                    left_old = lc[q]
                lc[q] = left_new
                flux = left_old * a + right_new * b
                if q == 1:
                    flux = flux + push
                net.append((flux, q))
            return net

        for flux, q in x_faces(-1):
            fc[q] = flux

        def plane(t, inner):
            net = []
            for flux, q in x_faces(t):
                net.append(flux - fc[q])
                fc[q] = flux
            values = [fld[q, t + 2] for q in range(7)]

            def y_states(q):
                v = values[q]
                d = roll(v, -1, 1) - v
                s = minmod(roll(d, 1, 1), d)
                twice = v + v
                return twice + s, roll(twice - s, -1, 1)

            h_l, h_r = y_states(0)
            n_l, n_r = y_states(2)
            a, b, push = face_factors(h_l, n_l, h_r, n_r, oy[t])
            for q in range(7):
                if q == 0:
                    lo, hi = h_l, h_r
                elif q == 2:
                    lo, hi = n_l, n_r
                else:
                    lo, hi = y_states(q)
                flux = lo * a + hi * b
                if q == 2:
                    flux = flux + push
                net[q] = net[q] + (flux - roll(flux, 1, 1))
            h = values[0]
            inv = 1.0 / jnp.maximum(h, 1.25)
            u, v = values[1] * inv, values[2] * inv
            s2 = u * u + v * v + 1e-6
            w = wd[t]
            drag = (0.02 * w) * jnp.sqrt(s2)
            fld[0, t + 2] = h - net[0]
            fld[1, t + 2] = values[1] - net[1] + (h * gx[t] - drag * u)
            fld[2, t + 2] = values[2] - net[2] + (h * gy[t] - drag * v)
            settle = inv * w
            for k in range(FRACTIONS):
                two = lambda n: jnp.concatenate([coef[n, k], coef[n, k]], axis=1)
                m = values[3 + k]
                erosion = jnp.maximum(s2 * two(1) - two(2), 0.0)
                change = two(0) * m * settle - erosion * w
                exch[k, t] += change[:, 0:128]
                fld[3 + k, t + 2] = m - net[3 + k] - change
            return inner

        lax.fori_loop(0, SEG, plane, 0)
        return carry

    lax.fori_loop(0, SUBSTEPS, substep, 0)

    for t in range(SEG):
        for q in range(7):
            on[q, pl.ds(t, 8, stride=SEG), :] = fld[q, t + 2, :, 0:128]
        for k in range(FRACTIONS):
            exn[k, pl.ds(t, 8, stride=SEG), :] = exch[k, t]
    stores = [
        pltpu.make_async_copy(on.at[0, mid], o_depth, out_sem.at[0]),
        pltpu.make_async_copy(on.at[pl.ds(1, 2), mid], o_disch, out_sem.at[1]),
        pltpu.make_async_copy(on.at[pl.ds(3, 4), mid], o_sed, out_sem.at[2]),
    ]
    for copy in stores:
        copy.start()

    keys = [kbuf[pl.ds(8 + p, 16, stride=4), :] for p in range(4)]
    planes = [[exn[k, pl.ds(8 + p, 16, stride=4), :] for p in range(4)] for k in range(FRACTIONS)]
    for r in range(3):
        for d in range(7):
            hits = [keys[p] == r * 7 + d for p in range(4)]
            for k in range(FRACTIONS):
                acc = jnp.where(hits[0], planes[k][0], 0.0)
                for p in range(1, 4):
                    acc = acc + jnp.where(hits[p], planes[k][p], 0.0)
                high = acc.astype(jnp.bfloat16)
                rows = slice(64 * r + 16 * k, 64 * r + 16 * k + 16)
                mhi[rows, 128 * d : 128 * d + 128] = high
                mlo[rows, 128 * d : 128 * d + 128] = (acc - high.astype(f32)).astype(jnp.bfloat16)
    res = jnp.dot(mhi[...], sel[...], preferred_element_type=f32)
    res = res + jnp.dot(mlo[...], sel[...], preferred_element_type=f32)
    every = None
    for k in range(FRACTIONS):
        part = res[64 + 16 * k : 80 + 16 * k]
        part = part + roll(res[16 * k : 16 * k + 16], -1, 0)
        part = part + roll(res[128 + 16 * k : 144 + 16 * k], 1, 0)
        part = 25.0 * part
        tot[pl.ds(k, 16, stride=8), :] = part
        every = part if k == 0 else every + part
    nsum[...] = every

    @pl.when(left)
    def _():
        remote(nsum, nrx.at[0], ns_send.at[0], ns_recv.at[0], (R, C - 1)).start()

    @pl.when(right)
    def _():
        remote(nsum, nrx.at[1], ns_send.at[1], ns_recv.at[1], (R, C + 1)).start()

    def send_sums(r, carry):
        @pl.when(r != C)
        def _():
            remote(
                tot.at[pl.ds(pl.multiple_of(8 * r, 8), 8)], rs.at[pl.ds(pl.multiple_of(8 * C, 8), 8)],
                ph_send, ph_recv, (R, r),
            ).start()

        return carry

    lax.fori_loop(0, COLS, send_sums, 0)
    own_rows = pl.ds(pl.multiple_of(8 * C, 8), 8)
    rs[own_rows, :] = tot[own_rows, :]

    @pl.when(right)
    def _():
        pltpu.make_async_copy(nsum, nrx.at[0], ns_recv.at[0]).wait()

    @pl.when(left)
    def _():
        pltpu.make_async_copy(nsum, nrx.at[1], ns_recv.at[1]).wait()

    wnew[1:17, :] = band2[3:19, :] + (nsum[...] + roll(nrx[0], 32, 1) + roll(nrx[1], -32, 1))
    for g in range(8):
        rows = slice(8 + 8 * g, 16 + 8 * g)
        fineb[8 * g : 8 * g + 8, :] = looked_up(wnew, 2 * g, ibuf[rows, :], rbuf[rows, :])
    fine_store = pltpu.make_async_copy(fineb, o_fine, out_sem.at[3])
    fine_store.start()

    pltpu.make_async_copy(tot.at[pl.ds(0, 120)], rs.at[pl.ds(0, 120)], ph_recv).wait()
    chunks = [jnp.zeros((8, 128), f32) for _ in range(4)]
    low_lanes = lane < 64
    for s in range(COLS):
        q, m = divmod(s, 4)
        piece = roll(rs[8 * s : 8 * s + 8, :], 32 * m - 8, 1)
        if m == 0:
            chunks[q] = chunks[q] + jnp.where(low_lanes, piece, 0.0)
            if q > 0:
                chunks[q - 1] = chunks[q - 1] + jnp.where(low_lanes, 0.0, piece)
        elif m == 3:
            chunks[q] = chunks[q] + jnp.where(low_lanes, 0.0, piece)
            if q < 3:
                chunks[q + 1] = chunks[q + 1] + jnp.where(low_lanes, piece, 0.0)
        else:
            chunks[q] = chunks[q] + piece
    for q in range(4):
        cols = slice(128 * q, 128 * q + 128)
        total = None
        for k in range(FRACTIONS):
            line = chunks[q][k : k + 1, :]
            depv[k, :, cols] = line
            total = line if k == 0 else total + line
        bedo[:, cols] = bedv[:, cols] + total
    last = [
        pltpu.make_async_copy(depv, o_dep, out_sem.at[4]),
        pltpu.make_async_copy(bedo, o_bed, out_sem.at[5]),
    ]
    for copy in last:
        copy.start()

    for n, (sends, src, dst, device, _) in enumerate(plan):

        @pl.when(sends)
        def _(n=n, src=src, dst=dst, device=device):
            remote(src, dst, nb_send.at[n], nb_recv.at[n], device).wait_send()

    pltpu.make_async_copy(strips.at[pl.ds(0, 15)], band.at[pl.ds(0, 15)], st_send.at[0]).wait()

    @pl.when(jnp.logical_or(both(C <= 2, up), both(C >= COLS - 3, down)))
    def _():
        pltpu.make_async_copy(strips, band.at[pl.ds(0, 16)], st_send.at[1]).wait()

    @pl.when(left)
    def _():
        pltpu.make_async_copy(nsum, nrx.at[0], ns_send.at[0]).wait()

    @pl.when(right)
    def _():
        pltpu.make_async_copy(nsum, nrx.at[1], ns_send.at[1]).wait()

    pltpu.make_async_copy(tot.at[pl.ds(0, 120)], rs.at[pl.ds(0, 120)], ph_send).wait()
    for copy in stores + [fine_store] + last:
        copy.wait()


def local(water_depth, discharge, sediment, bed_level, cell_map, wet_mask, sediment_params):
    hbm = pl.BlockSpec(memory_space=pl.ANY)
    dma = pltpu.SemaphoreType.DMA
    bf16 = jnp.bfloat16
    scratch = [
        ((9, 80, 128), f32),
        ((2, 64, 128), i32),
        ((1, 512), f32),
        ((10, 8, 128), f32),
        ((2, 13, 8, 128), f32),
        ((16, 1, 128), f32),
        ((22, 1, 128), f32),
        ((24, 128), f32),
        ((80, 128), f32),
        ((2, 80, 128), f32),
        ((80, 128), i32),
        ((80, 128), i32),
        ((80, 128), i32),
        ((7, 14, 8, 256), f32),
        ((12, 8, 256), f32),
        ((10, 8, 256), f32),
        ((10, 8, 256), f32),
        ((11, 8, 256), f32),
        ((10, 8, 256), f32),
        ((10, 8, 256), f32),
        ((7, 8, 256), f32),
        ((7, 8, 256), f32),
        ((3, 4, 8, 128), f32),
        ((4, 10, 8, 128), f32),
        ((7, 80, 128), f32),
        ((4, 80, 128), f32),
        ((896, 128), bf16),
        ((192, 896), bf16),
        ((192, 896), bf16),
        ((128, 128), f32),
        ((16, 128), f32),
        ((2, 16, 128), f32),
        ((128, 128), f32),
        ((24, 128), f32),
        ((64, 128), f32),
        ((4, 1, 512), f32),
        ((1, 512), f32),
    ]
    return pl.pallas_call(
        kernel,
        out_shape=(
            jax.ShapeDtypeStruct((64, 128), f32),
            jax.ShapeDtypeStruct((2, 64, 128), f32),
            jax.ShapeDtypeStruct((4, 64, 128), f32),
            jax.ShapeDtypeStruct((64, 128), f32),
            jax.ShapeDtypeStruct((1, 512), f32),
            jax.ShapeDtypeStruct((4, 1, 512), f32),
        ),
        in_specs=[hbm] * 6 + [pl.BlockSpec(memory_space=pltpu.SMEM)],
        out_specs=(hbm,) * 6,
        scratch_shapes=[pltpu.VMEM(shape, dtype) for shape, dtype in scratch]
        + [dma((6,)), dma((8,)), dma((8,)), dma((2,)), dma((3,)), dma(()), dma(()), dma((2,)), dma((2,)), dma((6,))],
        compiler_params=pltpu.CompilerParams(
            collective_id=0, has_side_effects=True, vmem_limit_bytes=32 * 1024 * 1024
        ),
    )(water_depth, discharge, sediment, bed_level, cell_map, wet_mask, sediment_params)


def solution(mesh):
    placed = (
        P("row", "col"),
        P(None, "row", "col"),
        P(None, "row", "col"),
        P(("row", "col"), None),
        P("row", "col"),
        P("row", "col"),
        P(),
    )
    return jax.shard_map(
        local,
        mesh=mesh,
        in_specs=placed,
        out_specs=(
            P("row", "col"),
            P(None, "row", "col"),
            P(None, "row", "col"),
            P("row", "col"),
            P(("row", "col"), None),
            P(None, ("row", "col"), None),
        ),
        check_vma=False,
    )
```

```python
import jax
import jax.numpy as jnp
from jax import lax
from jax.experimental import pallas as pl
from jax.experimental.pallas import tpu as pltpu
from jax.sharding import PartitionSpec as P

FRACTIONS = 4
SUBSTEPS = 4
ROWS = 32
COLS = 16
MAIN, SIDE = 2, 16
SLOTS = 23

MESH = pl.DeviceIdType.MESH
f32 = jnp.float32
i32 = jnp.int32


def roll(x, shift, axis):
    return pltpu.roll(x, shift % x.shape[axis], axis)


def minmod(a, b):
    return jnp.maximum(jnp.minimum(b, 0.0), jnp.minimum(a, jnp.maximum(b, 0.0)))


def inverse(x):
    guess = pl.reciprocal(x, approx=True)
    return guess * (2.0 - x * guess)


def root(x):
    return x * lax.rsqrt(x + 1e-35)


def face_factors(h_l, n_l, h_r, n_r, opened):
    w_l = n_l * inverse(jnp.maximum(h_l, 2.5))
    w_r = n_r * inverse(jnp.maximum(h_r, 2.5))
    c_l = jnp.abs(w_l) + root(0.5 * h_l)
    c_r = jnp.abs(w_r) + root(0.5 * h_r)
    fastest = jnp.maximum(c_l, c_r)
    push = (0.25 * opened) * (h_l * h_l + h_r * h_r)
    return opened * (w_l + fastest), opened * (w_r - fastest), push


def kernel(
    depth, disch, sed, bed, cmap, wetm, par,
    o_depth, o_disch, o_sed, o_fine, o_bed, o_dep,
    nat, raw, bedv, pk, rx, strips, band, band2, cn, nbed,
    ibuf, rbuf, kbuf, fld, wet, bedp, gx, gy, ox, oy, wd, coef,
    exch, on, exn, sel, mhi, mlo, tot, nsum, nrx, rs, wnew, fineb, depv, bedo,
    in_sem, nb_send, nb_recv, st_send, st_recv, ph_send, ph_recv, ns_send, ns_recv, out_sem,
):
    R = lax.axis_index("row")
    C = lax.axis_index("col")
    other_half = jnp.where(C < 8, 8, 0)
    barrier = pltpu.get_barrier_semaphore()

    def greet(n, carry):
        c = (n + other_half) & 15
        near = jnp.abs(c - C) <= 1

        @pl.when(c != C)
        def _():
            pl.semaphore_signal(barrier, inc=1, device_id=(R, c), device_id_type=MESH)

        @pl.when(jnp.logical_and(R > 0, jnp.logical_or(near, c >= COLS - 3)))
        def _():
            pl.semaphore_signal(barrier, inc=1, device_id=(R - 1, c), device_id_type=MESH)

        @pl.when(jnp.logical_and(R < ROWS - 1, jnp.logical_or(near, c <= 2)))
        def _():
            pl.semaphore_signal(barrier, inc=1, device_id=(R + 1, c), device_id_type=MESH)

        return carry

    lax.fori_loop(0, COLS, greet, 0)

    mid = pl.ds(8, 64)
    loads = [
        pltpu.make_async_copy(depth, nat.at[0, mid], in_sem.at[0]),
        pltpu.make_async_copy(disch, nat.at[pl.ds(1, 2), mid], in_sem.at[1]),
        pltpu.make_async_copy(sed, nat.at[pl.ds(3, 4), mid], in_sem.at[2]),
        pltpu.make_async_copy(bed, bedv, in_sem.at[3]),
        pltpu.make_async_copy(cmap, raw.at[0], in_sem.at[4]),
        pltpu.make_async_copy(wetm, raw.at[1], in_sem.at[5]),
    ]
    for copy in loads:
        copy.start()

    lane = lax.broadcasted_iota(i32, (8, 128), 1)
    sub = lax.broadcasted_iota(i32, (8, 128), 0)
    low_lanes = lane < 64

    far = f32(1 << 20)

    @pl.when(R == 0)
    def _():
        nat[0:8, 0:8, :] = jnp.zeros((8, 8, 128), f32)
        nat[8, 0:8, :] = jnp.full((8, 128), far)
        band[0:3] = jnp.zeros((3, 1, 128), f32)

    @pl.when(R == ROWS - 1)
    def _():
        nat[0:8, 72:80, :] = jnp.zeros((8, 8, 128), f32)
        nat[8, 72:80, :] = jnp.full((8, 128), far)
        band[19:22] = jnp.zeros((3, 1, 128), f32)

    for side, edge in ((0, C == COLS - 1), (1, C == 0)):

        @pl.when(edge)
        def _(side=side):
            rx[side, 0] = jnp.full((8, 128), far)
            rx[side, 1:9] = jnp.zeros((8, 8, 128), f32)

        @pl.when(jnp.logical_or(edge, R == 0))
        def _(side=side):
            rx[side, 9] = jnp.zeros((8, 128), f32)
            rx[side, 10] = jnp.full((8, 128), far)

        @pl.when(jnp.logical_or(edge, R == ROWS - 1))
        def _(side=side):
            rx[side, 11] = jnp.full((8, 128), far)
            rx[side, 12] = jnp.zeros((8, 128), f32)

    @pl.when(C == COLS - 1)
    def _():
        nrx[0] = jnp.zeros((16, 128), f32)

    @pl.when(C == 0)
    def _():
        nrx[1] = jnp.zeros((16, 128), f32)

    wnew[...] = jnp.zeros((24, 128), f32)
    exch[...] = jnp.zeros(exch.shape, f32)

    from_col = lax.broadcasted_iota(i32, (128, 128), 0) // 4
    to_lane = lax.broadcasted_iota(i32, (128, 128), 1)
    for d in range(7):
        sel[128 * d : 128 * d + 128, :] = (
            jnp.where(to_lane - from_col == d + 5, 1.0, 0.0).astype(jnp.bfloat16)
        )

    for k in range(FRACTIONS):
        erode = 0.002 * jnp.full((8, 128), par[2, k], f32)
        coef[0, k] = 0.05 * jnp.full((8, 128), par[0, k], f32)
        coef[1, k] = erode / (0.05 * jnp.full((8, 128), par[1, k], f32))
        coef[2, k] = erode

    for copy in loads:
        copy.wait()
    nat[8, 8:72, :] = raw[0].astype(f32)
    nat[7, 8:72, :] = raw[1].astype(f32)

    at = 32 * lax.broadcasted_iota(i32, (16, 128), 0) - 8 + lax.broadcasted_iota(i32, (16, 128), 1)
    window = jnp.zeros((16, 128), f32)
    for q in range(4):
        chunk = jnp.broadcast_to(bedv[:, 128 * q : 128 * q + 128], (16, 128))
        got = jnp.take_along_axis(chunk, at & 127, axis=1, mode="promise_in_bounds")
        window = jnp.where((at >> 7) == q, got, window)
    for t in range(COLS):
        strips[t] = window[t : t + 1, :]

    map_pack = jnp.zeros((8, 128), f32)
    for g in range(8):
        rows = slice(8 + 8 * g, 16 + 8 * g)
        packed = jnp.zeros((8, 128), f32)
        for q in range(8):
            first = (lane >> 3) == 2 * q
            second = (lane >> 3) == 2 * q + 1
            values = nat[q, rows, :]
            packed = jnp.where(first, roll(values, 16 * q, 1), packed)
            packed = jnp.where(second, roll(values, 16 * q + 16, 1), packed)
        pk[1 + g] = packed
        values = nat[8, rows, :]
        map_pack = jnp.where((lane >> 3) == 2 * g, roll(values, 16 * g, 1), map_pack)
        map_pack = jnp.where((lane >> 3) == 2 * g + 1, roll(values, 16 * g + 16, 1), map_pack)
    pk[0] = map_pack
    pk[9] = map_pack

    up, down = R > 0, R < ROWS - 1
    left, right = C > 0, C < COLS - 1
    both = jnp.logical_and
    above = jnp.where(C <= 2, COLS, jnp.where(C == COLS - 1, 2, 3))
    below = jnp.where(C >= COLS - 3, COLS, jnp.where(C == 0, 2, 3))
    expected = COLS - 1 + jnp.where(up, above, 0) + jnp.where(down, below, 0)
    pl.semaphore_wait(barrier, expected)

    def remote(src, dst, send, recv, device):
        return pltpu.make_async_remote_copy(
            src_ref=src, dst_ref=dst, send_sem=send, recv_sem=recv,
            device_id=device, device_id_type=MESH,
        )

    plan = [
        (left, pk.at[pl.ds(0, 9)], rx.at[0, pl.ds(0, 9)], (R, C - 1), right),
        (right, pk.at[pl.ds(0, 9)], rx.at[1, pl.ds(0, 9)], (R, C + 1), left),
        (up, nat.at[:, pl.ds(8, 8)], nat.at[:, pl.ds(72, 8)], (R - 1, C), down),
        (down, nat.at[:, pl.ds(64, 8)], nat.at[:, pl.ds(0, 8)], (R + 1, C), up),
        (both(up, left), pk.at[pl.ds(0, 2)], rx.at[0, pl.ds(11, 2)], (R - 1, C - 1), both(down, right)),
        (both(up, right), pk.at[pl.ds(0, 2)], rx.at[1, pl.ds(11, 2)], (R - 1, C + 1), both(down, left)),
        (both(down, left), pk.at[pl.ds(8, 2)], rx.at[0, pl.ds(9, 2)], (R + 1, C - 1), both(up, right)),
        (both(down, right), pk.at[pl.ds(8, 2)], rx.at[1, pl.ds(9, 2)], (R + 1, C + 1), both(up, left)),
    ]

    def send_to_neighbours(which):
        for n in which:
            sends, src, dst, device, _ = plan[n]

            @pl.when(sends)
            def _(n=n, src=src, dst=dst, device=device):
                remote(src, dst, nb_send.at[n], nb_recv.at[n], device).start()

    def await_neighbours(which):
        for n in which:
            _, src, dst, device, gets = plan[n]

            @pl.when(gets)
            def _(n=n, src=src, dst=dst):
                pltpu.make_async_copy(src, dst, nb_recv.at[n]).wait()

    def send_strips(n, carry):
        t = (n + other_half) & 15

        @pl.when(t != C)
        def _():
            remote(strips.at[t], band.at[3 + C], st_send.at[0], st_recv.at[0], (R, t)).start()

        @pl.when(both(C <= 2, up))
        def _():
            remote(strips.at[t], band.at[19 + C], st_send.at[1], st_recv.at[1], (R - 1, t)).start()

        @pl.when(both(C >= COLS - 3, down))
        def _():
            remote(strips.at[t], band.at[C - 13], st_send.at[1], st_recv.at[2], (R + 1, t)).start()

        return carry

    send_to_neighbours((0, 1))
    lax.fori_loop(0, COLS // 2, send_strips, 0)
    send_to_neighbours(range(2, 8))
    lax.fori_loop(COLS // 2, COLS, send_strips, 0)
    band[3 + C] = strips[C]

    def main_plane(ref, t):
        return ref[pl.ds(t, 8, stride=10), :]

    def side_rows(ref, t):
        return ref[pl.ds(t, 8, stride=5), :], ref[pl.ds(40 + t, 8, stride=5), :]

    def side_inner(ref, t):
        a, b = side_rows(ref, t)
        low = jnp.where(lane < 32, roll(a, 8, 1), roll(a, -72, 1))
        high = jnp.where(lane < 96, roll(b, 72, 1), roll(b, -8, 1))
        return jnp.where(low_lanes, low, high)

    first_eight = (lane & 8) == 0
    seam = both(lane >= 56, lane < 72)
    halo_lanes = both(((lane + 8) & 63) < 16, lane >= 0)

    def side_halo(a, b, q, inner):
        one = roll(jnp.where(first_eight, a, b), 56 - 16 * q, 1)
        two = roll(jnp.where(first_eight, b, a), 120 - 16 * q, 1)
        return jnp.where(halo_lanes, jnp.where(seam, one, two), inner)

    def shifted(value, step, side):
        turned = roll(value, step, 0)
        if side:
            turned = jnp.where(sub == (0 if step == 1 else 7), roll(turned, 64, 1), turned)
        return turned

    def ghosts(ref, side):
        first, count = (SIDE, 5) if side else (MAIN, 10)
        ref[first - 2] = shifted(ref[first + count - 2], 1, side)
        ref[first - 1] = shifted(ref[first + count - 1], 1, side)
        ref[first + count] = shifted(ref[first], -1, side)
        ref[first + count + 1] = shifted(ref[first + 1], -1, side)

    def wet_factors(first, count):
        for s in range(first - 1, first + count):
            ox[s] = 0.05 * wet[s] * wet[s + 1]
        for s in range(first, first + count):
            oy[s] = 0.05 * wet[s] * roll(wet[s], -1, 1)
            wd[s] = 0.2 * wet[s]

    def chunk(src, dst, base, with_bed):
        kept = {}

        def q_at(q, s):
            if (q, s) not in kept:
                kept[q, s] = fld[src, q, base + s]
            return kept[q, s]

        diffs = {}

        def d_at(q, s):
            if (q, s) not in diffs:
                diffs[q, s] = q_at(q, s + 1) - q_at(q, s)
            return diffs[q, s]

        lefts, fluxes, twice = {}, {}, {}
        for s in range(-1, 6):
            rights = {}
            for q in range(7):
                slope = minmod(d_at(q, s - 1), d_at(q, s))
                double = q_at(q, s) + q_at(q, s)
                twice[q, s] = double
                lefts[q, s] = double + slope
                rights[q] = double - slope
            if s < 0:
                continue
            a, b, push = face_factors(
                lefts[0, s - 1], lefts[1, s - 1], rights[0], rights[1], ox[base + s - 1]
            )
            for q in range(7):
                flux = lefts[q, s - 1] * a + rights[q] * b
                fluxes[q, s] = flux + push if q == 1 else flux
            if s < 1:
                continue
            p = s - 1
            y_left, y_right = {}, {}
            for q in range(7):
                v = q_at(q, p)
                d = roll(v, -1, 1) - v
                slope = minmod(roll(d, 1, 1), d)
                y_left[q] = twice[q, p] + slope
                y_right[q] = roll(twice[q, p] - slope, -1, 1)
            a, b, push = face_factors(y_left[0], y_left[2], y_right[0], y_right[2], oy[base + p])
            new = []
            for q in range(7):
                flux = y_left[q] * a + y_right[q] * b
                if q == 2:
                    flux = flux + push
                net = (fluxes[q, s] - fluxes[q, p]) + (flux - roll(flux, 1, 1))
                new.append(q_at(q, p) - net)
            h = q_at(0, p)
            inv = inverse(jnp.maximum(h, 1.25))
            u, v = q_at(1, p) * inv, q_at(2, p) * inv
            s2 = u * u + v * v + 1e-6
            w = wd[base + p]
            drag = (0.02 * w) * root(s2)
            new[1] = new[1] - drag * u
            new[2] = new[2] - drag * v
            if with_bed:
                new[1] = new[1] + h * gx[base + p]
                new[2] = new[2] + h * gy[base + p]
            settle = inv * w
            for k in range(FRACTIONS):
                erosion = jnp.maximum(s2 * coef[1, k] - coef[2, k], 0.0)
                change = coef[0, k] * q_at(3 + k, p) * settle - erosion * w
                exch[k, base + p] += change
                new[3 + k] = new[3 + k] - change
            for q in range(7):
                fld[dst, q, base + p] = new[q]

    await_neighbours((2, 3))
    for t in range(10):
        for q in range(7):
            fld[0, q, MAIN + t] = main_plane(nat.at[q], t)
        wet[MAIN + t] = main_plane(nat.at[7], t)
    ghosts(wet, False)
    wet_factors(MAIN, 10)
    for q in range(7):
        ghosts(fld.at[0, q], False)
    for t in range(5):
        for q in range(7):
            fld[0, q, SIDE + t] = side_inner(nat.at[q], t)
        wet[SIDE + t] = side_inner(nat.at[7], t)

    def early(c, carry):
        chunk(0, 1, MAIN + 5 * c, False)
        return carry

    lax.fori_loop(0, 2, early, 0)

    await_neighbours((0, 1, 4, 5, 6, 7))
    for g in range(10):
        slot = 9 if g == 0 else (12 if g == 9 else g)
        cn[8 * g : 8 * g + 8, :] = jnp.where(first_eight, rx[0, slot], rx[1, slot])
    for t in range(5):
        a, b = side_rows(cn, t)
        for q in range(7):
            fld[0, q, SIDE + t] = side_halo(a, b, q, fld[0, q, SIDE + t])
        wet[SIDE + t] = side_halo(a, b, 7, wet[SIDE + t])
    ghosts(wet, True)
    wet_factors(SIDE, 5)
    for q in range(7):
        ghosts(fld.at[0, q], True)
    chunk(0, 1, SIDE, False)

    pltpu.make_async_copy(strips.at[pl.ds(0, 15)], band.at[pl.ds(3, 15)], st_recv.at[0]).wait()

    @pl.when(down)
    def _():
        pltpu.make_async_copy(strips.at[pl.ds(0, 3)], band.at[pl.ds(19, 3)], st_recv.at[1]).wait()

    @pl.when(up)
    def _():
        pltpu.make_async_copy(strips.at[pl.ds(0, 3)], band.at[pl.ds(0, 3)], st_recv.at[2]).wait()

    for e in range(22):
        band2[e : e + 1, :] = band[e]

    map_side = jnp.where(first_eight, rx[0, 0], rx[1, 0])
    map_top = jnp.where(first_eight, rx[0, 10], rx[1, 10])
    map_low = jnp.where(first_eight, rx[0, 11], rx[1, 11])
    top_half = sub < 4

    def looked_up(table, first_row, index, shift):
        rows = [jnp.broadcast_to(table[first_row + n : first_row + n + 1, :], (8, 128)) for n in range(4)]
        result = jnp.zeros((8, 128), f32)
        for n in range(3):
            pair = jnp.where(top_half, rows[n], rows[n + 1])
            got = jnp.take_along_axis(pair, index, axis=1, mode="promise_in_bounds")
            result = jnp.where(shift == n - 1, got, result)
        return result

    for g in range(10):
        rows = slice(8 * g, 8 * g + 8)
        if g == 0:
            beside = roll(map_top, -16 * 7, 1)
        elif g == 9:
            beside = map_low
        else:
            beside = roll(map_side, -16 * (g - 1), 1)
        for tile, values in enumerate((nat[8, rows, :], beside)):
            cells = values.astype(i32)
            base = 2 * g - 2 + (sub >> 2)
            shift = (cells >> 9) - base + (-16 if g == 0 else (16 if g == 9 else 0))
            index = ((cells & 511) - 32 * C + 8) & 127
            nbed[tile, rows, :] = looked_up(band2, 2 * g - 2 - 1 + 3, index, shift)
            if tile == 0:
                ibuf[rows, :] = index
                rbuf[rows, :] = shift
                kbuf[rows, :] = (shift + 1) * 7 + (index - 8 - (lane >> 2) + 3)

    for t in range(10):
        bedp[MAIN + t] = main_plane(nbed.at[0], t)
    for t in range(5):
        a, b = side_rows(nbed.at[1], t)
        bedp[SIDE + t] = side_halo(a, b, 0, side_inner(nbed.at[0], t))
    ghosts(bedp, False)
    ghosts(bedp, True)
    for first, count in ((MAIN, 10), (SIDE, 5)):
        for s in range(first, first + count):
            here = bedp[s]
            scale = -0.5 * wd[s]
            slope_x = scale * (bedp[s + 1] - bedp[s - 1])
            slope_y = scale * (roll(here, -1, 1) - roll(here, 1, 1))
            gx[s] = slope_x
            gy[s] = slope_y
            h = fld[0, 0, s]
            fld[1, 1, s] += h * slope_x
            fld[1, 2, s] += h * slope_y

    def substep(n, carry):
        src = n & 1
        for q in range(7):
            ghosts(fld.at[src, q], False)
            ghosts(fld.at[src, q], True)

        def part(c, inner):
            chunk(src, 1 - src, MAIN + 5 * c + 4 * (c // 2), True)
            return inner

        lax.fori_loop(0, 3, part, 0)
        return carry

    lax.fori_loop(1, SUBSTEPS, substep, 0)

    edge = jnp.logical_or(lane < 8, lane >= 120)

    def natural(planes, out):
        for t in range(10):
            out[pl.ds(t, 8, stride=10), :] = planes[MAIN + t]
        for t in range(5):
            value = planes[SIDE + t]
            for part, (to_left, to_right) in enumerate(((-8, 72), (-72, 8))):
                rows = pl.ds(40 * part + t, 8, stride=5)
                moved = jnp.where(low_lanes, roll(value, to_left, 1), roll(value, to_right, 1))
                out[rows, :] = jnp.where(edge, moved, out[rows, :])

    for k in range(FRACTIONS):
        natural(exch.at[k], exn.at[k])

    keys = [kbuf[pl.ds(8 + p, 16, stride=4), :] for p in range(4)]
    planes = [[exn[k, pl.ds(8 + p, 16, stride=4), :] for p in range(4)] for k in range(FRACTIONS)]
    for r in range(3):
        for d in range(7):
            hits = [keys[p] == r * 7 + d for p in range(4)]
            for k in range(FRACTIONS):
                acc = jnp.where(hits[0], planes[k][0], 0.0)
                for p in range(1, 4):
                    acc = acc + jnp.where(hits[p], planes[k][p], 0.0)
                high = acc.astype(jnp.bfloat16)
                rows = slice(64 * r + 16 * k, 64 * r + 16 * k + 16)
                mhi[rows, 128 * d : 128 * d + 128] = high
                mlo[rows, 128 * d : 128 * d + 128] = (acc - high.astype(f32)).astype(jnp.bfloat16)
    res = jnp.dot(mhi[...], sel[...], preferred_element_type=f32)
    res = res + jnp.dot(mlo[...], sel[...], preferred_element_type=f32)
    parts = []
    for k in range(FRACTIONS):
        part = res[64 + 16 * k : 80 + 16 * k]
        part = part + roll(res[16 * k : 16 * k + 16], -1, 0)
        part = part + roll(res[128 + 16 * k : 144 + 16 * k], 1, 0)
        parts.append(25.0 * part)
    nsum[...] = (parts[0] + parts[1]) + (parts[2] + parts[3])
    for n in range(2):
        pair = parts[2 * n] + roll(parts[2 * n + 1], 64, 1)
        for r in range(COLS):
            tot[r, :, 128 * n : 128 * n + 128] = pair[r : r + 1, :]

    def send_sums(n, carry):
        r = (n + other_half) & 15

        @pl.when(r != C)
        def _():
            remote(tot.at[r], rs.at[C], ph_send, ph_recv, (R, r)).start()

        return carry

    @pl.when(left)
    def _():
        remote(nsum, nrx.at[0], ns_send.at[0], ns_recv.at[0], (R, C - 1)).start()

    @pl.when(right)
    def _():
        remote(nsum, nrx.at[1], ns_send.at[1], ns_recv.at[1], (R, C + 1)).start()

    lax.fori_loop(0, COLS, send_sums, 0)
    rs[C] = tot[C]

    for q in range(7):
        natural(fld.at[0, q], on.at[q])
    stores = [
        pltpu.make_async_copy(on.at[0, mid], o_depth, out_sem.at[0]),
        pltpu.make_async_copy(on.at[pl.ds(1, 2), mid], o_disch, out_sem.at[1]),
        pltpu.make_async_copy(on.at[pl.ds(3, 4), mid], o_sed, out_sem.at[2]),
    ]
    for copy in stores:
        copy.start()

    for n, (sends, src, dst, device, _) in enumerate(plan):

        @pl.when(sends)
        def _(n=n, src=src, dst=dst, device=device):
            remote(src, dst, nb_send.at[n], nb_recv.at[n], device).wait_send()

    pltpu.make_async_copy(strips.at[pl.ds(0, 15)], band.at[pl.ds(0, 15)], st_send.at[0]).wait()

    @pl.when(jnp.logical_or(both(C <= 2, up), both(C >= COLS - 3, down)))
    def _():
        pltpu.make_async_copy(strips, band.at[pl.ds(0, 16)], st_send.at[1]).wait()

    @pl.when(right)
    def _():
        pltpu.make_async_copy(nsum, nrx.at[0], ns_recv.at[0]).wait()

    @pl.when(left)
    def _():
        pltpu.make_async_copy(nsum, nrx.at[1], ns_recv.at[1]).wait()

    wnew[1:17, :] = band2[3:19, :] + (nsum[...] + roll(nrx[0], 32, 1) + roll(nrx[1], -32, 1))
    for g in range(8):
        rows = slice(8 + 8 * g, 16 + 8 * g)
        fineb[8 * g : 8 * g + 8, :] = looked_up(wnew, 2 * g, ibuf[rows, :], rbuf[rows, :])
    fine_store = pltpu.make_async_copy(fineb, o_fine, out_sem.at[3])
    fine_store.start()

    pltpu.make_async_copy(tot.at[pl.ds(0, 15)], rs.at[pl.ds(0, 15)], ph_recv).wait()
    row_lane = lax.broadcasted_iota(i32, (1, 128), 1)
    row_low = row_lane < 64
    lines = [[jnp.zeros((1, 128), f32) for _ in range(4)] for _ in range(FRACTIONS)]
    for s in range(COLS):
        q, m = divmod(s, 4)
        for n in range(2):
            pair = rs[s, :, 128 * n : 128 * n + 128]
            for half in range(2):
                line = lines[2 * n + half]
                piece = jnp.where(row_low, 0.0, pair) if half else jnp.where(row_low, pair, 0.0)
                piece = roll(piece, 32 * m - 8 - 64 * half, 1)
                if m == 0:
                    line[q] = line[q] + jnp.where(row_low, piece, 0.0)
                    if q > 0:
                        line[q - 1] = line[q - 1] + jnp.where(row_low, 0.0, piece)
                elif m == 3:
                    line[q] = line[q] + jnp.where(row_low, 0.0, piece)
                    if q < 3:
                        line[q + 1] = line[q + 1] + jnp.where(row_low, piece, 0.0)
                else:
                    line[q] = line[q] + piece
    for q in range(4):
        cols = slice(128 * q, 128 * q + 128)
        total = None
        for k in range(FRACTIONS):
            line = lines[k][q]
            depv[k, :, cols] = line
            total = line if k == 0 else total + line
        bedo[:, cols] = bedv[:, cols] + total
    last = [
        pltpu.make_async_copy(depv, o_dep, out_sem.at[4]),
        pltpu.make_async_copy(bedo, o_bed, out_sem.at[5]),
    ]
    for copy in last:
        copy.start()

    @pl.when(left)
    def _():
        pltpu.make_async_copy(nsum, nrx.at[0], ns_send.at[0]).wait()

    @pl.when(right)
    def _():
        pltpu.make_async_copy(nsum, nrx.at[1], ns_send.at[1]).wait()

    pltpu.make_async_copy(tot.at[pl.ds(0, 15)], rs.at[pl.ds(0, 15)], ph_send).wait()
    for copy in stores + [fine_store] + last:
        copy.wait()


def handed_on(*refs):
    count = (len(refs) - 1) // 2
    copies = [pltpu.make_async_copy(refs[n], refs[count + n], refs[-1].at[n]) for n in range(count)]
    for copy in copies:
        copy.start()
    for copy in copies:
        copy.wait()


def local(water_depth, discharge, sediment, bed_level, cell_map, wet_mask, sediment_params):
    hbm = pl.BlockSpec(memory_space=pl.ANY)
    dma = pltpu.SemaphoreType.DMA
    bf16 = jnp.bfloat16
    plane = (SLOTS, 8, 128)
    scratch = [
        ((9, 80, 128), f32),
        ((2, 64, 128), i32),
        ((1, 512), f32),
        ((10, 8, 128), f32),
        ((2, 13, 8, 128), f32),
        ((16, 1, 128), f32),
        ((22, 1, 128), f32),
        ((24, 128), f32),
        ((80, 128), f32),
        ((2, 80, 128), f32),
        ((80, 128), i32),
        ((80, 128), i32),
        ((80, 128), i32),
        ((2, 7, *plane), f32),
        (plane, f32),
        (plane, f32),
        (plane, f32),
        (plane, f32),
        (plane, f32),
        (plane, f32),
        (plane, f32),
        ((3, 4, 8, 128), f32),
        ((4, *plane), f32),
        ((7, 80, 128), f32),
        ((4, 80, 128), f32),
        ((896, 128), bf16),
        ((192, 896), bf16),
        ((192, 896), bf16),
        ((16, 1, 256), f32),
        ((16, 128), f32),
        ((2, 16, 128), f32),
        ((16, 1, 256), f32),
        ((24, 128), f32),
        ((64, 128), f32),
        ((4, 1, 512), f32),
        ((1, 512), f32),
    ]
    results = tuple(
        jax.ShapeDtypeStruct(shape, f32)
        for shape in ((64, 128), (2, 64, 128), (4, 64, 128), (64, 128), (1, 512), (4, 1, 512))
    )
    made = pl.pallas_call(
        kernel,
        out_shape=results,
        in_specs=[hbm] * 6 + [pl.BlockSpec(memory_space=pltpu.SMEM)],
        out_specs=(hbm,) * 6,
        scratch_shapes=[pltpu.VMEM(shape, dtype) for shape, dtype in scratch]
        + [dma((6,)), dma((8,)), dma((8,)), dma((2,)), dma((3,)), dma(()), dma(()), dma((2,)), dma((2,)), dma((6,))],
        compiler_params=pltpu.CompilerParams(
            collective_id=0, has_side_effects=True, vmem_limit_bytes=56 * 1024 * 1024
        ),
    )(water_depth, discharge, sediment, bed_level, cell_map, wet_mask, sediment_params)
    return pl.pallas_call(
        handed_on,
        out_shape=results,
        in_specs=[hbm] * 6,
        out_specs=(hbm,) * 6,
        scratch_shapes=[dma((6,))],
        compiler_params=pltpu.CompilerParams(vmem_limit_bytes=56 * 1024 * 1024),
    )(*made)


def solution(mesh):
    placed = (
        P("row", "col"),
        P(None, "row", "col"),
        P(None, "row", "col"),
        P(("row", "col"), None),
        P("row", "col"),
        P("row", "col"),
        P(),
    )
    return jax.shard_map(
        local,
        mesh=mesh,
        in_specs=placed,
        out_specs=(
            P("row", "col"),
            P(None, "row", "col"),
            P(None, "row", "col"),
            P("row", "col"),
            P(("row", "col"), None),
            P(None, ("row", "col"), None),
        ),
        check_vma=False,
    )
```

```python
import jax
import jax.numpy as jnp
from jax import lax
from jax.experimental import pallas as pl
from jax.experimental.pallas import tpu as pltpu
from jax.sharding import PartitionSpec as P

FRACTIONS = 4
SUBSTEPS = 4
ROWS = 32
COLS = 16
MAIN, SIDE = 2, 16
SLOTS = 23

MESH = pl.DeviceIdType.MESH
f32 = jnp.float32
i32 = jnp.int32


def roll(x, shift, axis):
    return pltpu.roll(x, shift % x.shape[axis], axis)


def minmod(a, b):
    return jnp.maximum(jnp.minimum(b, 0.0), jnp.minimum(a, jnp.maximum(b, 0.0)))


def inverse(x):
    guess = pl.reciprocal(x, approx=True)
    return guess * (2.0 - x * guess)


def root(x):
    return x * lax.rsqrt(x + 1e-35)


def face_factors(h_l, n_l, h_r, n_r, opened):
    w_l = n_l * inverse(jnp.maximum(h_l, 2.5))
    w_r = n_r * inverse(jnp.maximum(h_r, 2.5))
    c_l = jnp.abs(w_l) + root(0.5 * h_l)
    c_r = jnp.abs(w_r) + root(0.5 * h_r)
    fastest = jnp.maximum(c_l, c_r)
    push = (0.25 * opened) * (h_l * h_l + h_r * h_r)
    return opened * (w_l + fastest), opened * (w_r - fastest), push


def kernel(
    depth, disch, sed, bed, cmap, wetm, par,
    o_fields, o_fine, o_bed, o_dep,
    nat, raw, bedv, pk, rx, strips, band, band2, cn, nbed, sidx, sshift,
    ibuf, rbuf, kbuf, one, two, wet, gx, gy, ox, oy, wd, coef,
    exch, nmain, nside, sel, mhi, mlo, tot, nsum, nrx, rs, wnew,
    in_sem, nb_send, nb_recv, st_send, st_recv, ph_send, ph_recv, ns_send, ns_recv,
):
    R = lax.axis_index("row")
    C = lax.axis_index("col")
    other_half = jnp.where(C < 8, 8, 0)
    barrier = pltpu.get_barrier_semaphore()

    def greet(n, carry):
        c = (n + other_half) & 15
        near = jnp.abs(c - C) <= 1

        @pl.when(c != C)
        def _():
            pl.semaphore_signal(barrier, inc=1, device_id=(R, c), device_id_type=MESH)

        @pl.when(jnp.logical_and(R > 0, jnp.logical_or(near, c >= COLS - 3)))
        def _():
            pl.semaphore_signal(barrier, inc=1, device_id=(R - 1, c), device_id_type=MESH)

        @pl.when(jnp.logical_and(R < ROWS - 1, jnp.logical_or(near, c <= 2)))
        def _():
            pl.semaphore_signal(barrier, inc=1, device_id=(R + 1, c), device_id_type=MESH)

        return carry

    lax.fori_loop(0, COLS, greet, 0)

    mid = pl.ds(8, 64)
    loads = [
        pltpu.make_async_copy(depth, nat.at[0, mid], in_sem.at[0]),
        pltpu.make_async_copy(disch, nat.at[pl.ds(1, 2), mid], in_sem.at[1]),
        pltpu.make_async_copy(sed, nat.at[pl.ds(3, 4), mid], in_sem.at[2]),
        pltpu.make_async_copy(bed, bedv, in_sem.at[3]),
        pltpu.make_async_copy(cmap, raw.at[0], in_sem.at[4]),
        pltpu.make_async_copy(wetm, raw.at[1], in_sem.at[5]),
    ]
    for copy in loads:
        copy.start()

    lane = lax.broadcasted_iota(i32, (8, 128), 1)
    sub = lax.broadcasted_iota(i32, (8, 128), 0)
    low_lanes = lane < 64

    far = f32(1 << 20)

    @pl.when(R == 0)
    def _():
        nat[0:8, 0:8, :] = jnp.zeros((8, 8, 128), f32)
        nat[8, 0:8, :] = jnp.full((8, 128), far)
        band[0:3] = jnp.zeros((3, 1, 128), f32)

    @pl.when(R == ROWS - 1)
    def _():
        nat[0:8, 72:80, :] = jnp.zeros((8, 8, 128), f32)
        nat[8, 72:80, :] = jnp.full((8, 128), far)
        band[19:22] = jnp.zeros((3, 1, 128), f32)

    for side, edge in ((0, C == COLS - 1), (1, C == 0)):

        @pl.when(edge)
        def _(side=side):
            rx[side, 0] = jnp.full((8, 128), far)
            rx[side, 1:9] = jnp.zeros((8, 8, 128), f32)

        @pl.when(jnp.logical_or(edge, R == 0))
        def _(side=side):
            rx[side, 9] = jnp.zeros((8, 128), f32)
            rx[side, 10] = jnp.full((8, 128), far)

        @pl.when(jnp.logical_or(edge, R == ROWS - 1))
        def _(side=side):
            rx[side, 11] = jnp.full((8, 128), far)
            rx[side, 12] = jnp.zeros((8, 128), f32)

    @pl.when(C == COLS - 1)
    def _():
        nrx[0] = jnp.zeros((16, 128), f32)

    @pl.when(C == 0)
    def _():
        nrx[1] = jnp.zeros((16, 128), f32)

    wnew[...] = jnp.zeros((24, 128), f32)

    from_col = lax.broadcasted_iota(i32, (128, 128), 0) // 4
    to_lane = lax.broadcasted_iota(i32, (128, 128), 1)
    for d in range(7):
        sel[128 * d : 128 * d + 128, :] = (
            jnp.where(to_lane - from_col == d + 5, 1.0, 0.0).astype(jnp.bfloat16)
        )

    for k in range(FRACTIONS):
        erode = 0.002 * jnp.full((8, 128), par[2, k], f32)
        coef[0, k] = 0.05 * jnp.full((8, 128), par[0, k], f32)
        coef[1, k] = erode / (0.05 * jnp.full((8, 128), par[1, k], f32))
        coef[2, k] = erode

    for copy in loads:
        copy.wait()
    nat[8, 8:72, :] = raw[0].astype(f32)
    nat[7, 8:72, :] = raw[1].astype(f32)

    at = 32 * lax.broadcasted_iota(i32, (16, 128), 0) - 8 + lax.broadcasted_iota(i32, (16, 128), 1)
    window = jnp.zeros((16, 128), f32)
    for q in range(4):
        chunk = jnp.broadcast_to(bedv[:, 128 * q : 128 * q + 128], (16, 128))
        got = jnp.take_along_axis(chunk, at & 127, axis=1, mode="promise_in_bounds")
        window = jnp.where((at >> 7) == q, got, window)
    for t in range(COLS):
        strips[t] = window[t : t + 1, :]

    map_pack = jnp.zeros((8, 128), f32)
    for g in range(8):
        rows = slice(8 + 8 * g, 16 + 8 * g)
        packed = jnp.zeros((8, 128), f32)
        for q in range(8):
            first = (lane >> 3) == 2 * q
            second = (lane >> 3) == 2 * q + 1
            values = nat[q, rows, :]
            packed = jnp.where(first, roll(values, 16 * q, 1), packed)
            packed = jnp.where(second, roll(values, 16 * q + 16, 1), packed)
        pk[1 + g] = packed
        values = nat[8, rows, :]
        map_pack = jnp.where((lane >> 3) == 2 * g, roll(values, 16 * g, 1), map_pack)
        map_pack = jnp.where((lane >> 3) == 2 * g + 1, roll(values, 16 * g + 16, 1), map_pack)
    pk[0] = map_pack
    pk[9] = map_pack

    up, down = R > 0, R < ROWS - 1
    left, right = C > 0, C < COLS - 1
    both = jnp.logical_and
    above = jnp.where(C <= 2, COLS, jnp.where(C == COLS - 1, 2, 3))
    below = jnp.where(C >= COLS - 3, COLS, jnp.where(C == 0, 2, 3))
    expected = COLS - 1 + jnp.where(up, above, 0) + jnp.where(down, below, 0)
    pl.semaphore_wait(barrier, expected)

    def remote(src, dst, send, recv, device):
        return pltpu.make_async_remote_copy(
            src_ref=src, dst_ref=dst, send_sem=send, recv_sem=recv,
            device_id=device, device_id_type=MESH,
        )

    plan = [
        (left, pk.at[pl.ds(0, 9)], rx.at[0, pl.ds(0, 9)], (R, C - 1), right),
        (right, pk.at[pl.ds(0, 9)], rx.at[1, pl.ds(0, 9)], (R, C + 1), left),
        (up, nat.at[:, pl.ds(8, 8)], nat.at[:, pl.ds(72, 8)], (R - 1, C), down),
        (down, nat.at[:, pl.ds(64, 8)], nat.at[:, pl.ds(0, 8)], (R + 1, C), up),
        (both(up, left), pk.at[pl.ds(0, 2)], rx.at[0, pl.ds(11, 2)], (R - 1, C - 1), both(down, right)),
        (both(up, right), pk.at[pl.ds(0, 2)], rx.at[1, pl.ds(11, 2)], (R - 1, C + 1), both(down, left)),
        (both(down, left), pk.at[pl.ds(8, 2)], rx.at[0, pl.ds(9, 2)], (R + 1, C - 1), both(up, right)),
        (both(down, right), pk.at[pl.ds(8, 2)], rx.at[1, pl.ds(9, 2)], (R + 1, C + 1), both(up, left)),
    ]

    def send_to_neighbours(which):
        for n in which:
            sends, src, dst, device, _ = plan[n]

            @pl.when(sends)
            def _(n=n, src=src, dst=dst, device=device):
                remote(src, dst, nb_send.at[n], nb_recv.at[n], device).start()

    def await_neighbours(which):
        for n in which:
            _, src, dst, device, gets = plan[n]

            @pl.when(gets)
            def _(n=n, src=src, dst=dst):
                pltpu.make_async_copy(src, dst, nb_recv.at[n]).wait()

    def send_strips(n, carry):
        t = (n + other_half) & 15

        @pl.when(t != C)
        def _():
            remote(strips.at[t], band.at[3 + C], st_send.at[0], st_recv.at[0], (R, t)).start()

        @pl.when(both(C <= 2, up))
        def _():
            remote(strips.at[t], band.at[19 + C], st_send.at[1], st_recv.at[1], (R - 1, t)).start()

        @pl.when(both(C >= COLS - 3, down))
        def _():
            remote(strips.at[t], band.at[C - 13], st_send.at[1], st_recv.at[2], (R + 1, t)).start()

        return carry

    send_to_neighbours((0, 1))
    lax.fori_loop(0, COLS // 2, send_strips, 0)
    send_to_neighbours(range(2, 8))
    lax.fori_loop(COLS // 2, COLS, send_strips, 0)
    band[3 + C] = strips[C]

    def main_plane(ref, t):
        return ref[pl.ds(t, 8, stride=10), :]

    def side_rows(ref, t):
        return ref[pl.ds(t, 8, stride=5), :], ref[pl.ds(40 + t, 8, stride=5), :]

    def side_inner(ref):
        rows = [side_rows(ref, t) for t in range(5)]
        turned = [(roll(a, 8, 1), roll(a, -72, 1), roll(b, 72, 1), roll(b, -8, 1)) for a, b in rows]
        return [
            jnp.where(low_lanes, jnp.where(lane < 32, a, b), jnp.where(lane < 96, c, d))
            for a, b, c, d in turned
        ]

    first_eight = (lane & 8) == 0
    seam = both(lane >= 56, lane < 72)
    halo_lanes = both(((lane + 8) & 63) < 16, lane >= 0)

    def side_halo(mixed, q, inner):
        turned = [(roll(a, 56 - 16 * q, 1), roll(b, 120 - 16 * q, 1)) for a, b in mixed]
        return [
            jnp.where(halo_lanes, jnp.where(seam, a, b), old) for (a, b), old in zip(turned, inner)
        ]

    def mixed_rows(ref):
        rows = [side_rows(ref, t) for t in range(5)]
        return [(jnp.where(first_eight, a, b), jnp.where(first_eight, b, a)) for a, b in rows]

    def shifted(value, step, side):
        turned = roll(value, step, 0)
        if side:
            turned = jnp.where(sub == (0 if step == 1 else 7), roll(turned, 64, 1), turned)
        return turned

    def around(planes, side):
        return [
            shifted(planes[-2], 1, side), shifted(planes[-1], 1, side),
            shifted(planes[0], -1, side), shifted(planes[1], -1, side),
        ]

    def ghosts(ref, side, channels=range(7)):
        first, count = (SIDE, 5) if side else (MAIN, 10)
        made = [
            around([ref[q, first + n] for n in (0, 1, count - 2, count - 1)], side) for q in channels
        ]
        for q, values in zip(channels, made):
            for slot, value in zip((first - 2, first - 1, first + count, first + count + 1), values):
                ref[q, slot] = value

    def wet_factors(planes, side):
        first, count = (SIDE, 5) if side else (MAIN, 10)
        beyond = around(planes, side)
        padded = [beyond[1]] + planes + [beyond[2]]
        turned = [roll(w, -1, 1) for w in planes]
        for n in range(count + 1):
            ox[first - 1 + n] = 0.05 * padded[n] * padded[n + 1]
        for n in range(count):
            oy[first + n] = 0.05 * planes[n] * turned[n]
            wd[first + n] = 0.2 * planes[n]

    def chunk(src, dst, base, with_bed, start=False):
        kept, diffs = {}, {}

        def q_at(q, s):
            if (q, s) not in kept:
                kept[q, s] = src[q, base + s]
            return kept[q, s]

        def d_at(q, s):
            if (q, s) not in diffs:
                diffs[q, s] = q_at(q, s + 1) - q_at(q, s)
            return diffs[q, s]

        ahead = {}

        def fetch(p):
            for q in range(7):
                q_at(q, p + 2)
            ahead[p] = [
                tuple(roll(q_at(q, p), step, 1) for step in (1, -1, -2)) for q in range(7)
            ]
            if not start:
                ahead[p, "sum"] = [exch[k, base + p] for k in range(FRACTIONS)]

        def finish(p, new, turned, changes):
            for q in range(7):
                dst[q, base + p] = new[q] + turned[q]
            for k in range(FRACTIONS):
                exch[k, base + p] = changes[k]

        for s in range(-2, 2):
            for q in range(7):
                q_at(q, s)
        fetch(0)
        lefts, fluxes, twice = {}, {}, {}
        pending = None
        for s in range(-1, 6):
            if 1 <= s < 5:
                fetch(s)
            elif s == 5:
                for q in range(7):
                    q_at(q, 6)
            rights = {}
            for q in range(7):
                slope = minmod(d_at(q, s - 1), d_at(q, s))
                double = q_at(q, s) + q_at(q, s)
                twice[q, s] = double
                lefts[q, s] = double + slope
                rights[q] = double - slope
            if s < 0:
                continue
            a, b, push = face_factors(
                lefts[0, s - 1], lefts[1, s - 1], rights[0], rights[1], ox[base + s - 1]
            )
            for q in range(7):
                flux = lefts[q, s - 1] * a + rights[q] * b
                fluxes[q, s] = flux + push if q == 1 else flux
            if s < 1:
                continue
            p = s - 1
            y_left, y_right = {}, {}
            for q in range(7):
                v = q_at(q, p)
                lower, upper, second = ahead[p][q]
                d = upper - v
                y_left[q] = twice[q, p] + minmod(v - lower, d)
                y_right[q] = upper + upper - minmod(d, second - upper)
            a, b, push = face_factors(y_left[0], y_left[2], y_right[0], y_right[2], oy[base + p])
            new, turned = [], []
            for q in range(7):
                flux = y_left[q] * a + y_right[q] * b
                if q == 2:
                    flux = flux + push
                turned.append(roll(flux, 1, 1))
                new.append(q_at(q, p) - ((fluxes[q, s] - fluxes[q, p]) + flux))
            h = q_at(0, p)
            inv = inverse(jnp.maximum(h, 1.25))
            u, v = q_at(1, p) * inv, q_at(2, p) * inv
            s2 = u * u + v * v + 1e-6
            w = wd[base + p]
            drag = (0.02 * w) * root(s2)
            new[1] = new[1] - drag * u
            new[2] = new[2] - drag * v
            if with_bed:
                new[1] = new[1] + h * gx[base + p]
                new[2] = new[2] + h * gy[base + p]
            settle = inv * w
            changes = []
            for k in range(FRACTIONS):
                erosion = jnp.maximum(s2 * coef[1, k] - coef[2, k], 0.0)
                change = coef[0, k] * q_at(3 + k, p) * settle - erosion * w
                new[3 + k] = new[3 + k] - change
                changes.append(change if start else ahead[p, "sum"][k] + change)
            if pending is not None:
                finish(*pending)
            pending = (p, new, turned, changes)
        finish(*pending)

    await_neighbours((2, 3))
    wet_main = [main_plane(nat.at[7], t) for t in range(10)]
    wet_factors(wet_main, False)
    for q in range(7):
        planes = [main_plane(nat.at[q], t) for t in range(10)]
        for t in range(10):
            one[q, MAIN + t] = planes[t]
    ghosts(one, False)
    for q in range(8):
        planes = side_inner(nat.at[q])
        for t in range(5):
            if q < 7:
                one[q, SIDE + t] = planes[t]
            else:
                wet[SIDE + t] = planes[t]

    top_half = sub < 4

    def place(values, g):
        cells = values.astype(i32)
        base = 2 * g - 2 + (sub >> 2)
        shift = (cells >> 9) - base + (-16 if g == 0 else (16 if g == 9 else 0))
        return ((cells & 511) - 32 * C + 8) & 127, shift

    places = [place(nat[8, 8 * g : 8 * g + 8, :], g) for g in range(10)]
    for g, (index, shift) in enumerate(places):
        rows = slice(8 * g, 8 * g + 8)
        ibuf[rows, :] = index
        rbuf[rows, :] = shift
        kbuf[rows, :] = (shift + 1) * 7 + (index - 8 - (lane >> 2) + 3)

    def early(c, carry):
        chunk(one, two, MAIN + 5 * c, False, True)
        return carry

    lax.fori_loop(0, 2, early, 0)

    await_neighbours((0, 1, 4, 5, 6, 7))
    slots = [9, *range(1, 9), 12]
    side_values = [jnp.where(first_eight, rx[0, slot], rx[1, slot]) for slot in slots]
    map_side = jnp.where(first_eight, rx[0, 0], rx[1, 0])
    map_top = jnp.where(first_eight, rx[0, 10], rx[1, 10])
    map_low = jnp.where(first_eight, rx[0, 11], rx[1, 11])
    beside = [map_top] + [map_side] * 8 + [map_low]
    beside = [roll(v, -16 * n, 1) for v, n in zip(beside, (7, *range(8), 0))]
    places = [place(values, g) for g, values in enumerate(beside)]
    for g in range(10):
        cn[8 * g : 8 * g + 8, :] = side_values[g]
        sidx[8 * g : 8 * g + 8, :], sshift[8 * g : 8 * g + 8, :] = places[g]
    mixed = mixed_rows(cn)
    wet_side = side_halo(mixed, 7, [wet[SIDE + t] for t in range(5)])
    whole = [side_halo(mixed, q, [one[q, SIDE + t] for t in range(5)]) for q in range(7)]
    wet_factors(wet_side, True)
    for q in range(7):
        for t in range(5):
            one[q, SIDE + t] = whole[q][t]
    ghosts(one, True)
    chunk(one, two, SIDE, False, True)
    ghosts(two, False, (0, 3, 4, 5, 6))
    ghosts(two, True, (0, 3, 4, 5, 6))

    pltpu.make_async_copy(strips.at[pl.ds(0, 15)], band.at[pl.ds(3, 15)], st_recv.at[0]).wait()

    @pl.when(down)
    def _():
        pltpu.make_async_copy(strips.at[pl.ds(0, 3)], band.at[pl.ds(19, 3)], st_recv.at[1]).wait()

    @pl.when(up)
    def _():
        pltpu.make_async_copy(strips.at[pl.ds(0, 3)], band.at[pl.ds(0, 3)], st_recv.at[2]).wait()

    band_rows = [band[e] for e in range(22)]
    for e in range(22):
        band2[e : e + 1, :] = band_rows[e]

    def wide_rows(table, first_row, count):
        return [
            jnp.broadcast_to(table[first_row + n : first_row + n + 1, :], (8, 128)) for n in range(count)
        ]

    def looked_up(rows, places):
        found = []
        for g, (index, shift) in enumerate(places):
            found.append([
                jnp.take_along_axis(
                    jnp.where(top_half, rows[2 * g + n], rows[2 * g + n + 1]),
                    index, axis=1, mode="promise_in_bounds",
                )
                for n in range(3)
            ])
        return [
            jnp.where(
                shift == -1, got[0],
                jnp.where(shift == 0, got[1], jnp.where(shift == 1, got[2], 0.0)),
            )
            for got, (_, shift) in zip(found, places)
        ]

    rows = wide_rows(band2, 0, 22)
    groups = [slice(8 * g, 8 * g + 8) for g in range(10)]
    found = looked_up(rows, [(ibuf[r, :], rbuf[r, :]) for r in groups])
    for r, value in zip(groups, found):
        nbed[0, r, :] = value
    found = looked_up(rows, [(sidx[r, :], sshift[r, :]) for r in groups])
    for r, value in zip(groups, found):
        nbed[1, r, :] = value

    bed_main = [main_plane(nbed.at[0], t) for t in range(10)]
    bed_side = side_halo(mixed_rows(nbed.at[1]), 0, side_inner(nbed.at[0]))
    for planes, side in ((bed_main, False), (bed_side, True)):
        first, count = (SIDE, 5) if side else (MAIN, 10)
        beyond = around(planes, side)
        padded = [beyond[1]] + planes + [beyond[2]]
        turned = [(roll(v, -1, 1), roll(v, 1, 1)) for v in planes]
        scale = [-0.5 * wd[first + n] for n in range(count)]
        slope_x = [scale[n] * (padded[n + 2] - padded[n]) for n in range(count)]
        slope_y = [scale[n] * (turned[n][0] - turned[n][1]) for n in range(count)]
        depths = [one[0, first + n] for n in range(count)]
        new_x = [two[1, first + n] + depths[n] * slope_x[n] for n in range(count)]
        new_y = [two[2, first + n] + depths[n] * slope_y[n] for n in range(count)]
        for n in range(count):
            gx[first + n] = slope_x[n]
            gy[first + n] = slope_y[n]
            two[1, first + n] = new_x[n]
            two[2, first + n] = new_y[n]
    ghosts(two, False, (1, 2))
    ghosts(two, True, (1, 2))

    for substep in range(1, SUBSTEPS):
        src, dst = (two, one) if substep % 2 else (one, two)

        def each(c, carry, src=src, dst=dst):
            chunk(src, dst, MAIN + 5 * c + 4 * (c // 2), True)
            return carry

        lax.fori_loop(0, 3, each, 0)
        if substep < SUBSTEPS - 1:
            ghosts(dst, False)
            ghosts(dst, True)

    edge = jnp.logical_or(lane < 8, lane >= 120)

    def natural(planes, n):
        mains = [planes[MAIN + t] for t in range(10)]
        sides = [planes[SIDE + t] for t in range(5)]
        turned = [tuple(roll(v, step, 1) for step in (-8, 72, -72, 8)) for v in sides]
        for t, value in enumerate(mains):
            nmain[n, pl.ds(t, 8, stride=10), :] = value
        for t, (a, b, c, d) in enumerate(turned):
            nside[n, pl.ds(t, 8, stride=5), :] = jnp.where(low_lanes, a, b)
            nside[n, pl.ds(40 + t, 8, stride=5), :] = jnp.where(low_lanes, c, d)

    for k in range(FRACTIONS):
        natural(exch.at[k], k)
    wide_edge = jnp.concatenate([edge, edge], axis=0)

    keys = [kbuf[pl.ds(8 + p, 16, stride=4), :] for p in range(4)]
    fourth = [pl.ds(8 + p, 16, stride=4) for p in range(4)]
    planes = [
        [jnp.where(wide_edge, nside[k, rows, :], nmain[k, rows, :]) for rows in fourth]
        for k in range(FRACTIONS)
    ]
    for r in range(3):
        for d in range(7):
            hits = [keys[p] == r * 7 + d for p in range(4)]
            for k in range(FRACTIONS):
                acc = jnp.where(hits[0], planes[k][0], 0.0)
                for p in range(1, 4):
                    acc = acc + jnp.where(hits[p], planes[k][p], 0.0)
                high = acc.astype(jnp.bfloat16)
                rows = slice(64 * r + 16 * k, 64 * r + 16 * k + 16)
                mhi[rows, 128 * d : 128 * d + 128] = high
                mlo[rows, 128 * d : 128 * d + 128] = (acc - high.astype(f32)).astype(jnp.bfloat16)
    res = jnp.dot(mhi[...], sel[...], preferred_element_type=f32)
    res = res + jnp.dot(mlo[...], sel[...], preferred_element_type=f32)
    parts = []
    for k in range(FRACTIONS):
        part = res[64 + 16 * k : 80 + 16 * k]
        part = part + roll(res[16 * k : 16 * k + 16], -1, 0)
        part = part + roll(res[128 + 16 * k : 144 + 16 * k], 1, 0)
        parts.append(25.0 * part)
    nsum[...] = (parts[0] + parts[1]) + (parts[2] + parts[3])
    for n in range(2):
        pair = parts[2 * n] + roll(parts[2 * n + 1], 64, 1)
        for r in range(COLS):
            tot[r, :, 128 * n : 128 * n + 128] = pair[r : r + 1, :]

    def send_sums(n, carry):
        r = (n + other_half) & 15

        @pl.when(r != C)
        def _():
            remote(tot.at[r], rs.at[C], ph_send, ph_recv, (R, r)).start()

        return carry

    @pl.when(left)
    def _():
        remote(nsum, nrx.at[0], ns_send.at[0], ns_recv.at[0], (R, C - 1)).start()

    @pl.when(right)
    def _():
        remote(nsum, nrx.at[1], ns_send.at[1], ns_recv.at[1], (R, C + 1)).start()

    lax.fori_loop(0, COLS, send_sums, 0)
    rs[C] = tot[C]

    for q in range(7):
        natural(one.at[q], 4 + q)
    for q in range(7):
        for g in range(1, 9):
            rows = slice(8 * g, 8 * g + 8)
            o_fields[q, rows, :] = jnp.where(edge, nside[4 + q, rows, :], nmain[4 + q, rows, :])

    for n, (sends, src, dst, device, _) in enumerate(plan):

        @pl.when(sends)
        def _(n=n, src=src, dst=dst, device=device):
            remote(src, dst, nb_send.at[n], nb_recv.at[n], device).wait_send()

    pltpu.make_async_copy(strips.at[pl.ds(0, 15)], band.at[pl.ds(0, 15)], st_send.at[0]).wait()

    @pl.when(jnp.logical_or(both(C <= 2, up), both(C >= COLS - 3, down)))
    def _():
        pltpu.make_async_copy(strips, band.at[pl.ds(0, 16)], st_send.at[1]).wait()

    @pl.when(right)
    def _():
        pltpu.make_async_copy(nsum, nrx.at[0], ns_recv.at[0]).wait()

    @pl.when(left)
    def _():
        pltpu.make_async_copy(nsum, nrx.at[1], ns_recv.at[1]).wait()

    wnew[1:17, :] = band2[3:19, :] + (nsum[...] + roll(nrx[0], 32, 1) + roll(nrx[1], -32, 1))
    inner = [slice(8 + 8 * g, 16 + 8 * g) for g in range(8)]
    found = looked_up(wide_rows(wnew, 0, 18), [(ibuf[r, :], rbuf[r, :]) for r in inner])
    for g, value in enumerate(found):
        o_fine[8 * g : 8 * g + 8, :] = value

    pltpu.make_async_copy(tot.at[pl.ds(0, 15)], rs.at[pl.ds(0, 15)], ph_recv).wait()
    row_lane = lax.broadcasted_iota(i32, (1, 128), 1)
    row_low = row_lane < 64
    lines = [[jnp.zeros((1, 128), f32) for _ in range(4)] for _ in range(FRACTIONS)]
    for s in range(COLS):
        q, m = divmod(s, 4)
        for n in range(2):
            pair = rs[s, :, 128 * n : 128 * n + 128]
            for half in range(2):
                line = lines[2 * n + half]
                piece = jnp.where(row_low, 0.0, pair) if half else jnp.where(row_low, pair, 0.0)
                piece = roll(piece, 32 * m - 8 - 64 * half, 1)
                if m == 0:
                    line[q] = line[q] + jnp.where(row_low, piece, 0.0)
                    if q > 0:
                        line[q - 1] = line[q - 1] + jnp.where(row_low, 0.0, piece)
                elif m == 3:
                    line[q] = line[q] + jnp.where(row_low, 0.0, piece)
                    if q < 3:
                        line[q + 1] = line[q + 1] + jnp.where(row_low, piece, 0.0)
                else:
                    line[q] = line[q] + piece
    for q in range(4):
        cols = slice(128 * q, 128 * q + 128)
        total = None
        for k in range(FRACTIONS):
            line = lines[k][q]
            o_dep[k, :, cols] = line
            total = line if k == 0 else total + line
        o_bed[:, cols] = bedv[:, cols] + total
    @pl.when(left)
    def _():
        pltpu.make_async_copy(nsum, nrx.at[0], ns_send.at[0]).wait()

    @pl.when(right)
    def _():
        pltpu.make_async_copy(nsum, nrx.at[1], ns_send.at[1]).wait()

    pltpu.make_async_copy(tot.at[pl.ds(0, 15)], rs.at[pl.ds(0, 15)], ph_send).wait()


def handed_on(fields, fine, bed, dep, o_depth, o_disch, o_sed, o_fine, o_bed, o_dep, sem):
    mid = pl.ds(8, 64)
    pairs = (
        (fields.at[0, mid], o_depth),
        (fields.at[pl.ds(1, 2), mid], o_disch),
        (fields.at[pl.ds(3, 4), mid], o_sed),
        (fine, o_fine),
        (bed, o_bed),
        (dep, o_dep),
    )
    copies = [pltpu.make_async_copy(src, dst, sem.at[n]) for n, (src, dst) in enumerate(pairs)]
    for copy in copies:
        copy.start()
    for copy in copies:
        copy.wait()


def local(water_depth, discharge, sediment, bed_level, cell_map, wet_mask, sediment_params):
    hbm = pl.BlockSpec(memory_space=pl.ANY)
    dma = pltpu.SemaphoreType.DMA
    vmem = pl.BlockSpec(memory_space=pltpu.VMEM)
    bf16 = jnp.bfloat16
    plane = (SLOTS, 8, 128)
    scratch = [
        ((9, 80, 128), f32),
        ((2, 64, 128), i32),
        ((1, 512), f32),
        ((10, 8, 128), f32),
        ((2, 13, 8, 128), f32),
        ((16, 1, 128), f32),
        ((22, 1, 128), f32),
        ((24, 128), f32),
        ((80, 128), f32),
        ((2, 80, 128), f32),
        ((80, 128), i32),
        ((80, 128), i32),
        ((80, 128), i32),
        ((80, 128), i32),
        ((80, 128), i32),
        ((7, *plane), f32),
        ((7, *plane), f32),
        (plane, f32),
        (plane, f32),
        (plane, f32),
        (plane, f32),
        (plane, f32),
        (plane, f32),
        ((3, 4, 8, 128), f32),
        ((4, *plane), f32),
        ((11, 80, 128), f32),
        ((11, 80, 128), f32),
        ((896, 128), bf16),
        ((192, 896), bf16),
        ((192, 896), bf16),
        ((16, 1, 256), f32),
        ((16, 128), f32),
        ((2, 16, 128), f32),
        ((16, 1, 256), f32),
        ((24, 128), f32),
    ]
    results = tuple(
        jax.ShapeDtypeStruct(shape, f32)
        for shape in ((64, 128), (2, 64, 128), (4, 64, 128), (64, 128), (1, 512), (4, 1, 512))
    )
    made = pl.pallas_call(
        kernel,
        out_shape=tuple(
            pltpu.VMEM(shape, f32) for shape in ((7, 80, 128), (64, 128), (1, 512), (4, 1, 512))
        ),
        in_specs=[hbm] * 6 + [pl.BlockSpec(memory_space=pltpu.SMEM)],
        out_specs=(vmem,) * 4,
        scratch_shapes=[pltpu.VMEM(shape, dtype) for shape, dtype in scratch]
        + [dma((6,)), dma((8,)), dma((8,)), dma((2,)), dma((3,)), dma(()), dma(()), dma((2,)), dma((2,))],
        compiler_params=pltpu.CompilerParams(
            collective_id=0, has_side_effects=True, vmem_limit_bytes=56 * 1024 * 1024
        ),
    )(water_depth, discharge, sediment, bed_level, cell_map, wet_mask, sediment_params)
    return pl.pallas_call(
        handed_on,
        out_shape=results,
        in_specs=[hbm] * 4,
        out_specs=(hbm,) * 6,
        scratch_shapes=[dma((6,))],
    )(*(pltpu.with_memory_space_constraint(x, pltpu.VMEM) for x in made))


def solution(mesh):
    placed = (
        P("row", "col"),
        P(None, "row", "col"),
        P(None, "row", "col"),
        P(("row", "col"), None),
        P("row", "col"),
        P("row", "col"),
        P(),
    )
    return jax.shard_map(
        local,
        mesh=mesh,
        in_specs=placed,
        out_specs=(
            P("row", "col"),
            P(None, "row", "col"),
            P(None, "row", "col"),
            P("row", "col"),
            P(("row", "col"), None),
            P(None, ("row", "col"), None),
        ),
        check_vma=False,
    )
```

```python
import jax
import jax.numpy as jnp
from jax import lax
from jax.experimental import pallas as pl
from jax.experimental.pallas import tpu as pltpu
from jax.sharding import PartitionSpec as P

FRACTIONS = 4
SUBSTEPS = 4
ROWS = 32
COLS = 16
MAIN, SIDE = 2, 16
SLOTS = 23

MESH = pl.DeviceIdType.MESH
f32 = jnp.float32
i32 = jnp.int32


def roll(x, shift, axis):
    return pltpu.roll(x, shift % x.shape[axis], axis)


def minmod(a, b):
    return jnp.maximum(jnp.minimum(b, 0.0), jnp.minimum(a, jnp.maximum(b, 0.0)))


def inverse(x):
    guess = pl.reciprocal(x, approx=True)
    return guess * (2.0 - x * guess)


def root(x):
    return x * lax.rsqrt(x + 1e-35)


def face_factors(h_l, n_l, h_r, n_r, opened):
    w_l = n_l * inverse(jnp.maximum(h_l, 2.5))
    w_r = n_r * inverse(jnp.maximum(h_r, 2.5))
    c_l = jnp.abs(w_l) + root(0.5 * h_l)
    c_r = jnp.abs(w_r) + root(0.5 * h_r)
    fastest = jnp.maximum(c_l, c_r)
    push = (0.25 * opened) * (h_l * h_l + h_r * h_r)
    return opened * (w_l + fastest), opened * (w_r - fastest), push


def kernel(
    depth, disch, sed, bed, cmap, wetm, factors,
    o_fields, o_fine, o_bed, o_dep,
    params, nat, raw, bedv, pk, rx, strips, band, band2, cn, nbed, sidx, sshift,
    ibuf, rbuf, kbuf, one, two, wet, gx, gy, ox, oy, wd, coef,
    exch, nmain, nside, sel, mhi, mlo, tot, nsum, nrx, rs, wnew,
    in_sem, nb_send, nb_recv, st_send, st_recv, ph_send, ph_recv, ns_send, ns_recv,
):
    R = lax.axis_index("row")
    C = lax.axis_index("col")
    other_half = jnp.where(C < 8, 8, 0)
    barrier = pltpu.get_barrier_semaphore()

    def greet(n, carry):
        c = (n + other_half) & 15
        near = jnp.abs(c - C) <= 1

        @pl.when(c != C)
        def _():
            pl.semaphore_signal(barrier, inc=1, device_id=(R, c), device_id_type=MESH)

        @pl.when(jnp.logical_and(R > 0, jnp.logical_or(near, c >= COLS - 3)))
        def _():
            pl.semaphore_signal(barrier, inc=1, device_id=(R - 1, c), device_id_type=MESH)

        @pl.when(jnp.logical_and(R < ROWS - 1, jnp.logical_or(near, c <= 2)))
        def _():
            pl.semaphore_signal(barrier, inc=1, device_id=(R + 1, c), device_id_type=MESH)

        return carry

    lax.fori_loop(0, COLS, greet, 0)

    mid = pl.ds(8, 64)
    loads = [
        pltpu.make_async_copy(depth, nat.at[0, mid], in_sem.at[0]),
        pltpu.make_async_copy(disch, nat.at[pl.ds(1, 2), mid], in_sem.at[1]),
        pltpu.make_async_copy(sed, nat.at[pl.ds(3, 4), mid], in_sem.at[2]),
        pltpu.make_async_copy(bed, bedv, in_sem.at[3]),
        pltpu.make_async_copy(cmap, raw.at[0], in_sem.at[4]),
        pltpu.make_async_copy(wetm, raw.at[1], in_sem.at[5]),
        pltpu.make_async_copy(factors, params, in_sem.at[6]),
    ]
    for copy in loads:
        copy.start()

    lane = lax.broadcasted_iota(i32, (8, 128), 1)
    sub = lax.broadcasted_iota(i32, (8, 128), 0)
    low_lanes = lane < 64

    far = f32(1 << 20)

    @pl.when(R == 0)
    def _():
        nat[0:8, 0:8, :] = jnp.zeros((8, 8, 128), f32)
        nat[8, 0:8, :] = jnp.full((8, 128), far)
        band[0:3] = jnp.zeros((3, 1, 128), f32)

    @pl.when(R == ROWS - 1)
    def _():
        nat[0:8, 72:80, :] = jnp.zeros((8, 8, 128), f32)
        nat[8, 72:80, :] = jnp.full((8, 128), far)
        band[19:22] = jnp.zeros((3, 1, 128), f32)

    for side, edge in ((0, C == COLS - 1), (1, C == 0)):

        @pl.when(edge)
        def _(side=side):
            rx[side, 0] = jnp.full((8, 128), far)
            rx[side, 1:9] = jnp.zeros((8, 8, 128), f32)

        @pl.when(jnp.logical_or(edge, R == 0))
        def _(side=side):
            rx[side, 9] = jnp.zeros((8, 128), f32)
            rx[side, 10] = jnp.full((8, 128), far)

        @pl.when(jnp.logical_or(edge, R == ROWS - 1))
        def _(side=side):
            rx[side, 11] = jnp.full((8, 128), far)
            rx[side, 12] = jnp.zeros((8, 128), f32)

    @pl.when(C == COLS - 1)
    def _():
        nrx[0] = jnp.zeros((16, 128), f32)

    @pl.when(C == 0)
    def _():
        nrx[1] = jnp.zeros((16, 128), f32)

    wnew[...] = jnp.zeros((24, 128), f32)

    from_col = lax.broadcasted_iota(i32, (128, 128), 0) // 4
    to_lane = lax.broadcasted_iota(i32, (128, 128), 1)
    for d in range(7):
        sel[128 * d : 128 * d + 128, :] = (
            jnp.where(to_lane - from_col == d + 5, 1.0, 0.0).astype(jnp.bfloat16)
        )

    for copy in loads:
        copy.wait()
    for k in range(FRACTIONS):
        erode = 0.002 * jnp.full((8, 128), params[2, k], f32)
        coef[0, k] = 0.05 * jnp.full((8, 128), params[0, k], f32)
        coef[1, k] = erode / (0.05 * jnp.full((8, 128), params[1, k], f32))
        coef[2, k] = erode

    nat[8, 8:72, :] = raw[0].astype(f32)
    nat[7, 8:72, :] = raw[1].astype(f32)

    at = 32 * lax.broadcasted_iota(i32, (16, 128), 0) - 8 + lax.broadcasted_iota(i32, (16, 128), 1)
    window = jnp.zeros((16, 128), f32)
    for q in range(4):
        chunk = jnp.broadcast_to(bedv[:, 128 * q : 128 * q + 128], (16, 128))
        got = jnp.take_along_axis(chunk, at & 127, axis=1, mode="promise_in_bounds")
        window = jnp.where((at >> 7) == q, got, window)
    for t in range(COLS):
        strips[t] = window[t : t + 1, :]

    map_pack = jnp.zeros((8, 128), f32)
    for g in range(8):
        rows = slice(8 + 8 * g, 16 + 8 * g)
        packed = jnp.zeros((8, 128), f32)
        for q in range(8):
            first = (lane >> 3) == 2 * q
            second = (lane >> 3) == 2 * q + 1
            values = nat[q, rows, :]
            packed = jnp.where(first, roll(values, 16 * q, 1), packed)
            packed = jnp.where(second, roll(values, 16 * q + 16, 1), packed)
        pk[1 + g] = packed
        values = nat[8, rows, :]
        map_pack = jnp.where((lane >> 3) == 2 * g, roll(values, 16 * g, 1), map_pack)
        map_pack = jnp.where((lane >> 3) == 2 * g + 1, roll(values, 16 * g + 16, 1), map_pack)
    pk[0] = map_pack
    pk[9] = map_pack

    up, down = R > 0, R < ROWS - 1
    left, right = C > 0, C < COLS - 1
    both = jnp.logical_and
    above = jnp.where(C <= 2, COLS, jnp.where(C == COLS - 1, 2, 3))
    below = jnp.where(C >= COLS - 3, COLS, jnp.where(C == 0, 2, 3))
    expected = COLS - 1 + jnp.where(up, above, 0) + jnp.where(down, below, 0)
    pl.semaphore_wait(barrier, expected)

    def remote(src, dst, send, recv, device):
        return pltpu.make_async_remote_copy(
            src_ref=src, dst_ref=dst, send_sem=send, recv_sem=recv,
            device_id=device, device_id_type=MESH,
        )

    plan = [
        (left, pk.at[pl.ds(0, 9)], rx.at[0, pl.ds(0, 9)], (R, C - 1), right),
        (right, pk.at[pl.ds(0, 9)], rx.at[1, pl.ds(0, 9)], (R, C + 1), left),
        (up, nat.at[:, pl.ds(8, 8)], nat.at[:, pl.ds(72, 8)], (R - 1, C), down),
        (down, nat.at[:, pl.ds(64, 8)], nat.at[:, pl.ds(0, 8)], (R + 1, C), up),
        (both(up, left), pk.at[pl.ds(0, 2)], rx.at[0, pl.ds(11, 2)], (R - 1, C - 1), both(down, right)),
        (both(up, right), pk.at[pl.ds(0, 2)], rx.at[1, pl.ds(11, 2)], (R - 1, C + 1), both(down, left)),
        (both(down, left), pk.at[pl.ds(8, 2)], rx.at[0, pl.ds(9, 2)], (R + 1, C - 1), both(up, right)),
        (both(down, right), pk.at[pl.ds(8, 2)], rx.at[1, pl.ds(9, 2)], (R + 1, C + 1), both(up, left)),
    ]

    def send_to_neighbours(which):
        for n in which:
            sends, src, dst, device, _ = plan[n]

            @pl.when(sends)
            def _(n=n, src=src, dst=dst, device=device):
                remote(src, dst, nb_send.at[n], nb_recv.at[n], device).start()

    def await_neighbours(which):
        for n in which:
            _, src, dst, device, gets = plan[n]

            @pl.when(gets)
            def _(n=n, src=src, dst=dst):
                pltpu.make_async_copy(src, dst, nb_recv.at[n]).wait()

    def send_strips(n, carry):
        t = (n + other_half) & 15

        @pl.when(t != C)
        def _():
            remote(strips.at[t], band.at[3 + C], st_send.at[0], st_recv.at[0], (R, t)).start()

        @pl.when(both(C <= 2, up))
        def _():
            remote(strips.at[t], band.at[19 + C], st_send.at[1], st_recv.at[1], (R - 1, t)).start()

        @pl.when(both(C >= COLS - 3, down))
        def _():
            remote(strips.at[t], band.at[C - 13], st_send.at[1], st_recv.at[2], (R + 1, t)).start()

        return carry

    send_to_neighbours((0, 1))
    lax.fori_loop(0, COLS // 2, send_strips, 0)
    send_to_neighbours(range(2, 8))
    lax.fori_loop(COLS // 2, COLS, send_strips, 0)
    band[3 + C] = strips[C]

    def main_plane(ref, t):
        return ref[pl.ds(t, 8, stride=10), :]

    def side_rows(ref, t):
        return ref[pl.ds(t, 8, stride=5), :], ref[pl.ds(40 + t, 8, stride=5), :]

    def side_inner(ref):
        rows = [side_rows(ref, t) for t in range(5)]
        turned = [(roll(a, 8, 1), roll(a, -72, 1), roll(b, 72, 1), roll(b, -8, 1)) for a, b in rows]
        return [
            jnp.where(low_lanes, jnp.where(lane < 32, a, b), jnp.where(lane < 96, c, d))
            for a, b, c, d in turned
        ]

    first_eight = (lane & 8) == 0
    seam = both(lane >= 56, lane < 72)
    halo_lanes = both(((lane + 8) & 63) < 16, lane >= 0)

    def side_halo(mixed, q, inner):
        turned = [(roll(a, 56 - 16 * q, 1), roll(b, 120 - 16 * q, 1)) for a, b in mixed]
        return [
            jnp.where(halo_lanes, jnp.where(seam, a, b), old) for (a, b), old in zip(turned, inner)
        ]

    def mixed_rows(ref):
        rows = [side_rows(ref, t) for t in range(5)]
        return [(jnp.where(first_eight, a, b), jnp.where(first_eight, b, a)) for a, b in rows]

    def shifted(value, step, side):
        turned = roll(value, step, 0)
        if side:
            turned = jnp.where(sub == (0 if step == 1 else 7), roll(turned, 64, 1), turned)
        return turned

    def around(planes, side):
        return [
            shifted(planes[-2], 1, side), shifted(planes[-1], 1, side),
            shifted(planes[0], -1, side), shifted(planes[1], -1, side),
        ]

    def ghosts(ref, side, channels=range(7)):
        first, count = (SIDE, 5) if side else (MAIN, 10)
        made = [
            around([ref[q, first + n] for n in (0, 1, count - 2, count - 1)], side) for q in channels
        ]
        for q, values in zip(channels, made):
            for slot, value in zip((first - 2, first - 1, first + count, first + count + 1), values):
                ref[q, slot] = value

    def wet_factors(planes, side):
        first, count = (SIDE, 5) if side else (MAIN, 10)
        beyond = around(planes, side)
        padded = [beyond[1]] + planes + [beyond[2]]
        turned = [roll(w, -1, 1) for w in planes]
        for n in range(count + 1):
            ox[first - 1 + n] = 0.05 * padded[n] * padded[n + 1]
        for n in range(count):
            oy[first + n] = 0.05 * planes[n] * turned[n]
            wd[first + n] = 0.2 * planes[n]

    def exchanged(k, mass, s2, settle, w):
        erosion = jnp.maximum(s2 * coef[1, k] - coef[2, k], 0.0)
        return coef[0, k] * mass * settle - erosion * w

    def speeds(h, x, y):
        inv = inverse(jnp.maximum(h, 1.25))
        u, v = x * inv, y * inv
        return inv, u, v, u * u + v * v + 1e-6

    def chunk(src, dst, base, with_bed, start=False, count=True):
        kept, diffs = {}, {}

        def q_at(q, s):
            if (q, s) not in kept:
                kept[q, s] = src[q, base + s]
            return kept[q, s]

        def d_at(q, s):
            if (q, s) not in diffs:
                diffs[q, s] = q_at(q, s + 1) - q_at(q, s)
            return diffs[q, s]

        ahead = {}

        def fetch(p):
            for q in range(7):
                q_at(q, p + 2)
            ahead[p] = [
                tuple(roll(q_at(q, p), step, 1) for step in (1, -1, -2)) for q in range(7)
            ]
            if count and not start:
                ahead[p, "sum"] = [exch[k, base + p] for k in range(FRACTIONS)]

        def finish(p, new, turned, changes):
            for q in range(7):
                dst[q, base + p] = new[q] + turned[q]
            for k, value in enumerate(changes):
                exch[k, base + p] = value

        for s in range(-2, 2):
            for q in range(7):
                q_at(q, s)
        fetch(0)
        lefts, fluxes, twice = {}, {}, {}
        pending = None
        for s in range(-1, 6):
            if 1 <= s < 5:
                fetch(s)
            elif s == 5:
                for q in range(7):
                    q_at(q, 6)
            rights = {}
            for q in range(7):
                slope = minmod(d_at(q, s - 1), d_at(q, s))
                double = q_at(q, s) + q_at(q, s)
                twice[q, s] = double
                lefts[q, s] = double + slope
                rights[q] = double - slope
            if s < 0:
                continue
            a, b, push = face_factors(
                lefts[0, s - 1], lefts[1, s - 1], rights[0], rights[1], ox[base + s - 1]
            )
            for q in range(7):
                flux = lefts[q, s - 1] * a + rights[q] * b
                fluxes[q, s] = flux + push if q == 1 else flux
            if s < 1:
                continue
            p = s - 1
            y_left, y_right = {}, {}
            for q in range(7):
                v = q_at(q, p)
                lower, upper, second = ahead[p][q]
                d = upper - v
                y_left[q] = twice[q, p] + minmod(v - lower, d)
                y_right[q] = upper + upper - minmod(d, second - upper)
            a, b, push = face_factors(y_left[0], y_left[2], y_right[0], y_right[2], oy[base + p])
            new, turned = [], []
            for q in range(7):
                flux = y_left[q] * a + y_right[q] * b
                if q == 2:
                    flux = flux + push
                turned.append(roll(flux, 1, 1))
                new.append(q_at(q, p) - ((fluxes[q, s] - fluxes[q, p]) + flux))
            h = q_at(0, p)
            inv, u, v, s2 = speeds(h, q_at(1, p), q_at(2, p))
            w = wd[base + p]
            drag = (0.02 * w) * root(s2)
            new[1] = new[1] - drag * u
            new[2] = new[2] - drag * v
            if with_bed:
                new[1] = new[1] + h * gx[base + p]
                new[2] = new[2] + h * gy[base + p]
            settle = inv * w
            changes = []
            for k in range(FRACTIONS):
                change = exchanged(k, q_at(3 + k, p), s2, settle, w)
                new[3 + k] = new[3 + k] - change
                if count:
                    changes.append(change if start else ahead[p, "sum"][k] + change)
            if pending is not None:
                finish(*pending)
            pending = (p, new, turned, changes)
        finish(*pending)

    await_neighbours((2, 3))
    wet_main = [main_plane(nat.at[7], t) for t in range(10)]
    wet_factors(wet_main, False)
    for q in range(7):
        planes = [main_plane(nat.at[q], t) for t in range(10)]
        for t in range(10):
            one[q, MAIN + t] = planes[t]
    ghosts(one, False)
    for q in range(8):
        planes = side_inner(nat.at[q])
        for t in range(5):
            if q < 7:
                one[q, SIDE + t] = planes[t]
            else:
                wet[SIDE + t] = planes[t]

    top_half = sub < 4

    def place(values, g):
        cells = values.astype(i32)
        base = 2 * g - 2 + (sub >> 2)
        shift = (cells >> 9) - base + (-16 if g == 0 else (16 if g == 9 else 0))
        return ((cells & 511) - 32 * C + 8) & 127, shift

    places = [place(nat[8, 8 * g : 8 * g + 8, :], g) for g in range(10)]
    for g, (index, shift) in enumerate(places):
        rows = slice(8 * g, 8 * g + 8)
        ibuf[rows, :] = index
        rbuf[rows, :] = shift
        kbuf[rows, :] = (shift + 1) * 7 + (index - 8 - (lane >> 2) + 3)

    def early(c, carry):
        chunk(one, two, MAIN + 5 * c, False, True)
        return carry

    lax.fori_loop(0, 2, early, 0)

    await_neighbours((0, 1, 4, 5, 6, 7))
    groups = [9, *range(1, 9), 12]
    side_values = [jnp.where(first_eight, rx[0, n], rx[1, n]) for n in groups]
    map_side = jnp.where(first_eight, rx[0, 0], rx[1, 0])
    map_top = jnp.where(first_eight, rx[0, 10], rx[1, 10])
    map_low = jnp.where(first_eight, rx[0, 11], rx[1, 11])
    beside = [map_top] + [map_side] * 8 + [map_low]
    beside = [roll(v, -16 * n, 1) for v, n in zip(beside, (7, *range(8), 0))]
    places = [place(values, g) for g, values in enumerate(beside)]
    for g in range(10):
        cn[8 * g : 8 * g + 8, :] = side_values[g]
        sidx[8 * g : 8 * g + 8, :], sshift[8 * g : 8 * g + 8, :] = places[g]
    mixed = mixed_rows(cn)
    wet_side = side_halo(mixed, 7, [wet[SIDE + t] for t in range(5)])
    whole = [side_halo(mixed, q, [one[q, SIDE + t] for t in range(5)]) for q in range(7)]
    wet_factors(wet_side, True)
    for q in range(7):
        for t in range(5):
            one[q, SIDE + t] = whole[q][t]
    ghosts(one, True)
    chunk(one, two, SIDE, False, True)
    ghosts(two, False, (0, 3, 4, 5, 6))
    ghosts(two, True, (0, 3, 4, 5, 6))

    pltpu.make_async_copy(strips.at[pl.ds(0, 15)], band.at[pl.ds(3, 15)], st_recv.at[0]).wait()

    @pl.when(down)
    def _():
        pltpu.make_async_copy(strips.at[pl.ds(0, 3)], band.at[pl.ds(19, 3)], st_recv.at[1]).wait()

    @pl.when(up)
    def _():
        pltpu.make_async_copy(strips.at[pl.ds(0, 3)], band.at[pl.ds(0, 3)], st_recv.at[2]).wait()

    def looked_up(rows, places):
        found = []
        for g, (index, shift) in enumerate(places):
            found.append([
                jnp.take_along_axis(
                    jnp.where(top_half, rows[2 * g + n], rows[2 * g + n + 1]),
                    index, axis=1, mode="promise_in_bounds",
                )
                for n in range(3)
            ])
        return [
            jnp.where(
                shift == -1, got[0],
                jnp.where(shift == 0, got[1], jnp.where(shift == 1, got[2], 0.0)),
            )
            for got, (_, shift) in zip(found, places)
        ]

    rows = [jnp.broadcast_to(band[e], (8, 128)) for e in range(22)]
    groups = [slice(8 * g, 8 * g + 8) for g in range(10)]
    found = looked_up(rows, [(ibuf[r, :], rbuf[r, :]) for r in groups])
    for r, value in zip(groups, found):
        nbed[0, r, :] = value
    found = looked_up(rows, [(sidx[r, :], sshift[r, :]) for r in groups])
    for r, value in zip(groups, found):
        nbed[1, r, :] = value

    bed_main = [main_plane(nbed.at[0], t) for t in range(10)]
    bed_side = side_halo(mixed_rows(nbed.at[1]), 0, side_inner(nbed.at[0]))
    for planes, side in ((bed_main, False), (bed_side, True)):
        first, count = (SIDE, 5) if side else (MAIN, 10)
        beyond = around(planes, side)
        padded = [beyond[1]] + planes + [beyond[2]]
        turned = [(roll(v, -1, 1), roll(v, 1, 1)) for v in planes]
        scale = [-0.5 * wd[first + n] for n in range(count)]
        slope_x = [scale[n] * (padded[n + 2] - padded[n]) for n in range(count)]
        slope_y = [scale[n] * (turned[n][0] - turned[n][1]) for n in range(count)]
        depths = [one[0, first + n] for n in range(count)]
        new_x = [two[1, first + n] + depths[n] * slope_x[n] for n in range(count)]
        new_y = [two[2, first + n] + depths[n] * slope_y[n] for n in range(count)]
        for n in range(count):
            gx[first + n] = slope_x[n]
            gy[first + n] = slope_y[n]
            two[1, first + n] = new_x[n]
            two[2, first + n] = new_y[n]
    ghosts(two, False, (1, 2))
    ghosts(two, True, (1, 2))

    def step(src, dst, count):
        def each(c, carry):
            chunk(src, dst, MAIN + 5 * c + 4 * (c // 2), True, False, count)
            return carry

        lax.fori_loop(0, 3, each, 0)

    states = (one, two)
    for substep in range(1, SUBSTEPS - 1):
        src, dst = states[substep % 2], states[1 - substep % 2]
        step(src, dst, True)
        ghosts(dst, False)
        ghosts(dst, True)
    before_last, after_last = states[(SUBSTEPS - 1) % 2], states[SUBSTEPS % 2]

    slots = [*range(MAIN, MAIN + 10), *range(SIDE, SIDE + 5)]
    totals = {}
    for slot in slots:
        h, x, y, *masses = [before_last[q, slot] for q in range(7)]
        inv, _, _, s2 = speeds(h, x, y)
        w = wd[slot]
        for k in range(FRACTIONS):
            totals[k, slot] = exch[k, slot] + exchanged(k, masses[k], s2, inv * w, w)

    edge = jnp.logical_or(lane < 8, lane >= 120)

    def natural(planes, n):
        mains, sides = planes[:10], planes[10:]
        turned = [tuple(roll(v, step, 1) for step in (-8, 72, -72, 8)) for v in sides]
        for t, value in enumerate(mains):
            nmain[n, pl.ds(t, 8, stride=10), :] = value
        for t, (a, b, c, d) in enumerate(turned):
            nside[n, pl.ds(t, 8, stride=5), :] = jnp.where(low_lanes, a, b)
            nside[n, pl.ds(40 + t, 8, stride=5), :] = jnp.where(low_lanes, c, d)

    for k in range(FRACTIONS):
        natural([totals[k, slot] for slot in slots], k)
    wide_edge = jnp.concatenate([edge, edge], axis=0)

    keys = [kbuf[pl.ds(8 + p, 16, stride=4), :] for p in range(4)]
    fourth = [pl.ds(8 + p, 16, stride=4) for p in range(4)]
    planes = [
        [jnp.where(wide_edge, nside[k, rows, :], nmain[k, rows, :]) for rows in fourth]
        for k in range(FRACTIONS)
    ]
    for r in range(3):
        for d in range(7):
            hits = [keys[p] == r * 7 + d for p in range(4)]
            for k in range(FRACTIONS):
                acc = jnp.where(hits[0], planes[k][0], 0.0)
                for p in range(1, 4):
                    acc = acc + jnp.where(hits[p], planes[k][p], 0.0)
                high = acc.astype(jnp.bfloat16)
                rows = slice(64 * r + 16 * k, 64 * r + 16 * k + 16)
                mhi[rows, 128 * d : 128 * d + 128] = high
                mlo[rows, 128 * d : 128 * d + 128] = (acc - high.astype(f32)).astype(jnp.bfloat16)
    res = jnp.dot(mhi[...], sel[...], preferred_element_type=f32)
    res = res + jnp.dot(mlo[...], sel[...], preferred_element_type=f32)
    parts = []
    for k in range(FRACTIONS):
        part = res[64 + 16 * k : 80 + 16 * k]
        part = part + roll(res[16 * k : 16 * k + 16], -1, 0)
        part = part + roll(res[128 + 16 * k : 144 + 16 * k], 1, 0)
        parts.append(25.0 * part)
    nsum[...] = (parts[0] + parts[1]) + (parts[2] + parts[3])
    for n in range(2):
        pair = parts[2 * n] + roll(parts[2 * n + 1], 64, 1)
        for r in range(COLS):
            tot[r, :, 128 * n : 128 * n + 128] = pair[r : r + 1, :]

    def send_sums(n, carry):
        r = (n + other_half) & 15

        @pl.when(r != C)
        def _():
            remote(tot.at[r], rs.at[C], ph_send, ph_recv, (R, r)).start()

        return carry

    @pl.when(left)
    def _():
        remote(nsum, nrx.at[0], ns_send.at[0], ns_recv.at[0], (R, C - 1)).start()

    @pl.when(right)
    def _():
        remote(nsum, nrx.at[1], ns_send.at[1], ns_recv.at[1], (R, C + 1)).start()

    lax.fori_loop(0, COLS, send_sums, 0)
    rs[C] = tot[C]

    step(before_last, after_last, False)
    for q in range(7):
        natural([after_last[q, s] for s in slots], 4 + q)
    for q in range(7):
        for g in range(1, 9):
            rows = slice(8 * g, 8 * g + 8)
            o_fields[q, rows, :] = jnp.where(edge, nside[4 + q, rows, :], nmain[4 + q, rows, :])

    for n, (sends, src, dst, device, _) in enumerate(plan):

        @pl.when(sends)
        def _(n=n, src=src, dst=dst, device=device):
            remote(src, dst, nb_send.at[n], nb_recv.at[n], device).wait_send()

    pltpu.make_async_copy(strips.at[pl.ds(0, 15)], band.at[pl.ds(0, 15)], st_send.at[0]).wait()

    @pl.when(jnp.logical_or(both(C <= 2, up), both(C >= COLS - 3, down)))
    def _():
        pltpu.make_async_copy(strips, band.at[pl.ds(0, 16)], st_send.at[1]).wait()

    @pl.when(right)
    def _():
        pltpu.make_async_copy(nsum, nrx.at[0], ns_recv.at[0]).wait()

    @pl.when(left)
    def _():
        pltpu.make_async_copy(nsum, nrx.at[1], ns_recv.at[1]).wait()

    for e in range(16):
        band2[e : e + 1, :] = band[3 + e]
    wnew[1:17, :] = band2[...] + (nsum[...] + roll(nrx[0], 32, 1) + roll(nrx[1], -32, 1))
    wide = [jnp.broadcast_to(wnew[n : n + 1, :], (8, 128)) for n in range(18)]
    inner = [slice(8 + 8 * g, 16 + 8 * g) for g in range(8)]
    found = looked_up(wide, [(ibuf[r, :], rbuf[r, :]) for r in inner])
    for g, value in enumerate(found):
        o_fine[8 * g : 8 * g + 8, :] = value

    pltpu.make_async_copy(tot.at[pl.ds(0, 15)], rs.at[pl.ds(0, 15)], ph_recv).wait()
    row_lane = lax.broadcasted_iota(i32, (1, 128), 1)
    row_low = row_lane < 64
    lines = [[jnp.zeros((1, 128), f32) for _ in range(4)] for _ in range(FRACTIONS)]
    for s in range(COLS):
        q, m = divmod(s, 4)
        for n in range(2):
            pair = rs[s, :, 128 * n : 128 * n + 128]
            for half in range(2):
                line = lines[2 * n + half]
                piece = jnp.where(row_low, 0.0, pair) if half else jnp.where(row_low, pair, 0.0)
                piece = roll(piece, 32 * m - 8 - 64 * half, 1)
                if m == 0:
                    line[q] = line[q] + jnp.where(row_low, piece, 0.0)
                    if q > 0:
                        line[q - 1] = line[q - 1] + jnp.where(row_low, 0.0, piece)
                elif m == 3:
                    line[q] = line[q] + jnp.where(row_low, 0.0, piece)
                    if q < 3:
                        line[q + 1] = line[q + 1] + jnp.where(row_low, piece, 0.0)
                else:
                    line[q] = line[q] + piece
    for q in range(4):
        cols = slice(128 * q, 128 * q + 128)
        total = None
        for k in range(FRACTIONS):
            line = lines[k][q]
            o_dep[k, :, cols] = line
            total = line if k == 0 else total + line
        o_bed[:, cols] = bedv[:, cols] + total
    @pl.when(left)
    def _():
        pltpu.make_async_copy(nsum, nrx.at[0], ns_send.at[0]).wait()

    @pl.when(right)
    def _():
        pltpu.make_async_copy(nsum, nrx.at[1], ns_send.at[1]).wait()

    pltpu.make_async_copy(tot.at[pl.ds(0, 15)], rs.at[pl.ds(0, 15)], ph_send).wait()


def handed_on(fields, fine, bed, dep, o_depth, o_disch, o_sed, o_fine, o_bed, o_dep, sem):
    mid = pl.ds(8, 64)
    pairs = (
        (fields.at[0, mid], o_depth),
        (fields.at[pl.ds(1, 2), mid], o_disch),
        (fields.at[pl.ds(3, 4), mid], o_sed),
        (fine, o_fine),
        (bed, o_bed),
        (dep, o_dep),
    )
    copies = [pltpu.make_async_copy(src, dst, sem.at[n]) for n, (src, dst) in enumerate(pairs)]
    for copy in copies:
        copy.start()
    for copy in copies:
        copy.wait()


def local(water_depth, discharge, sediment, bed_level, cell_map, wet_mask, sediment_params):
    hbm = pl.BlockSpec(memory_space=pl.ANY)
    dma = pltpu.SemaphoreType.DMA
    vmem = pl.BlockSpec(memory_space=pltpu.VMEM)
    bf16 = jnp.bfloat16
    plane = (SLOTS, 8, 128)
    scratch = [
        ((9, 80, 128), f32),
        ((2, 64, 128), i32),
        ((1, 512), f32),
        ((10, 8, 128), f32),
        ((2, 13, 8, 128), f32),
        ((16, 1, 128), f32),
        ((22, 1, 128), f32),
        ((16, 128), f32),
        ((80, 128), f32),
        ((2, 80, 128), f32),
        ((80, 128), i32),
        ((80, 128), i32),
        ((80, 128), i32),
        ((80, 128), i32),
        ((80, 128), i32),
        ((7, *plane), f32),
        ((7, *plane), f32),
        (plane, f32),
        (plane, f32),
        (plane, f32),
        (plane, f32),
        (plane, f32),
        (plane, f32),
        ((3, 4, 8, 128), f32),
        ((4, *plane), f32),
        ((11, 80, 128), f32),
        ((11, 80, 128), f32),
        ((896, 128), bf16),
        ((192, 896), bf16),
        ((192, 896), bf16),
        ((16, 1, 256), f32),
        ((16, 128), f32),
        ((2, 16, 128), f32),
        ((16, 1, 256), f32),
        ((24, 128), f32),
    ]
    results = tuple(
        jax.ShapeDtypeStruct(shape, f32)
        for shape in ((64, 128), (2, 64, 128), (4, 64, 128), (64, 128), (1, 512), (4, 1, 512))
    )
    made = pl.pallas_call(
        kernel,
        out_shape=tuple(
            pltpu.VMEM(shape, f32) for shape in ((7, 80, 128), (64, 128), (1, 512), (4, 1, 512))
        ),
        in_specs=[hbm] * 7,
        out_specs=(vmem,) * 4,
        scratch_shapes=[pltpu.SMEM((3, FRACTIONS), f32)]
        + [pltpu.VMEM(shape, dtype) for shape, dtype in scratch]
        + [dma((7,)), dma((8,)), dma((8,)), dma((2,)), dma((3,)), dma(()), dma(()), dma((2,)), dma((2,))],
        compiler_params=pltpu.CompilerParams(
            collective_id=0, has_side_effects=True, vmem_limit_bytes=56 * 1024 * 1024
        ),
    )(water_depth, discharge, sediment, bed_level, cell_map, wet_mask, sediment_params)
    return pl.pallas_call(
        handed_on,
        out_shape=results,
        in_specs=[hbm] * 4,
        out_specs=(hbm,) * 6,
        scratch_shapes=[dma((6,))],
    )(*(pltpu.with_memory_space_constraint(x, pltpu.VMEM) for x in made))


def solution(mesh):
    placed = (
        P("row", "col"),
        P(None, "row", "col"),
        P(None, "row", "col"),
        P(("row", "col"), None),
        P("row", "col"),
        P("row", "col"),
        P(),
    )
    return jax.shard_map(
        local,
        mesh=mesh,
        in_specs=placed,
        out_specs=(
            P("row", "col"),
            P(None, "row", "col"),
            P(None, "row", "col"),
            P("row", "col"),
            P(("row", "col"), None),
            P(None, ("row", "col"), None),
        ),
        check_vma=False,
    )
```

```python
import jax
import jax.numpy as jnp
from jax import lax
from jax.experimental import pallas as pl
from jax.experimental.pallas import tpu as pltpu
from jax.sharding import PartitionSpec as P

FRACTIONS = 4
SUBSTEPS = 4
ROWS = 32
COLS = 16
MAIN, SIDE = 2, 16
SLOTS = 23

MESH = pl.DeviceIdType.MESH
f32 = jnp.float32
i32 = jnp.int32


def roll(x, shift, axis):
    return pltpu.roll(x, shift % x.shape[axis], axis)


def minmod(a, b):
    return jnp.maximum(jnp.minimum(b, 0.0), jnp.minimum(a, jnp.maximum(b, 0.0)))


def inverse(x):
    guess = pl.reciprocal(x, approx=True)
    return guess * (2.0 - x * guess)


def root(x):
    return x * lax.rsqrt(x + 1e-35)


def face_factors(h_l, n_l, h_r, n_r, opened):
    w_l = n_l * inverse(jnp.maximum(h_l, 2.5))
    w_r = n_r * inverse(jnp.maximum(h_r, 2.5))
    c_l = jnp.abs(w_l) + root(0.5 * h_l)
    c_r = jnp.abs(w_r) + root(0.5 * h_r)
    fastest = jnp.maximum(c_l, c_r)
    push = (0.25 * opened) * (h_l * h_l + h_r * h_r)
    return opened * (w_l + fastest), opened * (w_r - fastest), push


def kernel(
    depth, disch, sed, bed, cmap, wetm, factors,
    o_fields, o_fine, o_bed, o_dep,
    params, nat, raw, bedv, pk, rx, strips, band, band2, cn, nbed, sidx, sshift,
    ibuf, rbuf, kbuf, one, two, wet, gx, gy, ox, oy, wd, coef,
    exch, nmain, nside, sel, mhi, mlo, tot, nsum, nrx, rs, wnew,
    in_sem, nb_send, nb_recv, st_send, st_recv, ph_send, ph_recv, ns_send, ns_recv,
):
    R = lax.axis_index("row")
    C = lax.axis_index("col")
    other_half = jnp.where(C < 8, 8, 0)
    barrier = pltpu.get_barrier_semaphore()

    others = [other_half + (((C & 7) + k) & 7) for k in (4, 5, 3, 6, 2, 7, 1, 0)]
    mates = [8 - other_half + (((C & 7) + k) & 7) for k in range(1, 8)]
    up, down = R > 0, R < ROWS - 1
    left, right = C > 0, C < COLS - 1
    both = jnp.logical_and

    def greet(row, c):
        pl.semaphore_signal(barrier, inc=1, device_id=(row, c), device_id_type=MESH)

    for c in others:
        greet(R, c)

    @pl.when(down)
    def _():
        for c in range(3):
            greet(R + 1, c)

    @pl.when(up)
    def _():
        for c in range(COLS - 3, COLS):
            greet(R - 1, c)

    for c in mates:
        greet(R, c)
    for step in (-1, 0, 1):

        @pl.when(both(down, both(C + step > 2, C + step < COLS)))
        def _(step=step):
            greet(R + 1, C + step)

        @pl.when(both(up, both(C + step >= 0, C + step < COLS - 3)))
        def _(step=step):
            greet(R - 1, C + step)

    mid = pl.ds(8, 64)
    loads = [
        pltpu.make_async_copy(depth, nat.at[0, mid], in_sem.at[0]),
        pltpu.make_async_copy(disch, nat.at[pl.ds(1, 2), mid], in_sem.at[1]),
        pltpu.make_async_copy(sed, nat.at[pl.ds(3, 4), mid], in_sem.at[2]),
        pltpu.make_async_copy(bed, bedv, in_sem.at[3]),
        pltpu.make_async_copy(cmap, raw.at[0], in_sem.at[4]),
        pltpu.make_async_copy(wetm, raw.at[1], in_sem.at[5]),
        pltpu.make_async_copy(factors, params, in_sem.at[6]),
    ]
    for copy in loads:
        copy.start()

    lane = lax.broadcasted_iota(i32, (8, 128), 1)
    sub = lax.broadcasted_iota(i32, (8, 128), 0)
    low_lanes = lane < 64

    far = f32(1 << 20)

    @pl.when(R == 0)
    def _():
        nat[0:8, 0:8, :] = jnp.zeros((8, 8, 128), f32)
        nat[8, 0:8, :] = jnp.full((8, 128), far)
        band[0:3] = jnp.zeros((3, 1, 128), f32)

    @pl.when(R == ROWS - 1)
    def _():
        nat[0:8, 72:80, :] = jnp.zeros((8, 8, 128), f32)
        nat[8, 72:80, :] = jnp.full((8, 128), far)
        band[19:22] = jnp.zeros((3, 1, 128), f32)

    for side, edge in ((0, C == COLS - 1), (1, C == 0)):

        @pl.when(edge)
        def _(side=side):
            rx[side, 0] = jnp.full((8, 128), far)
            rx[side, 1:9] = jnp.zeros((8, 8, 128), f32)

        @pl.when(jnp.logical_or(edge, R == 0))
        def _(side=side):
            rx[side, 9] = jnp.zeros((8, 128), f32)
            rx[side, 10] = jnp.full((8, 128), far)

        @pl.when(jnp.logical_or(edge, R == ROWS - 1))
        def _(side=side):
            rx[side, 11] = jnp.full((8, 128), far)
            rx[side, 12] = jnp.zeros((8, 128), f32)

    @pl.when(C == COLS - 1)
    def _():
        nrx[0] = jnp.zeros((16, 128), f32)

    @pl.when(C == 0)
    def _():
        nrx[1] = jnp.zeros((16, 128), f32)

    wnew[...] = jnp.zeros((24, 128), f32)

    from_col = lax.broadcasted_iota(i32, (128, 128), 0) // 4
    to_lane = lax.broadcasted_iota(i32, (128, 128), 1)
    for d in range(7):
        sel[128 * d : 128 * d + 128, :] = (
            jnp.where(to_lane - from_col == d + 5, 1.0, 0.0).astype(jnp.bfloat16)
        )

    for copy in loads:
        copy.wait()
    for k in range(FRACTIONS):
        erode = 0.002 * jnp.full((8, 128), params[2, k], f32)
        coef[0, k] = 0.05 * jnp.full((8, 128), params[0, k], f32)
        coef[1, k] = erode / (0.05 * jnp.full((8, 128), params[1, k], f32))
        coef[2, k] = erode

    nat[8, 8:72, :] = raw[0].astype(f32)
    nat[7, 8:72, :] = raw[1].astype(f32)

    at = 32 * lax.broadcasted_iota(i32, (16, 128), 0) - 8 + lax.broadcasted_iota(i32, (16, 128), 1)
    window = jnp.zeros((16, 128), f32)
    for q in range(4):
        chunk = jnp.broadcast_to(bedv[:, 128 * q : 128 * q + 128], (16, 128))
        got = jnp.take_along_axis(chunk, at & 127, axis=1, mode="promise_in_bounds")
        window = jnp.where((at >> 7) == q, got, window)
    for t in range(COLS):
        strips[t] = window[t : t + 1, :]

    map_pack = jnp.zeros((8, 128), f32)
    for g in range(8):
        rows = slice(8 + 8 * g, 16 + 8 * g)
        packed = jnp.zeros((8, 128), f32)
        for q in range(8):
            first = (lane >> 3) == 2 * q
            second = (lane >> 3) == 2 * q + 1
            values = nat[q, rows, :]
            packed = jnp.where(first, roll(values, 16 * q, 1), packed)
            packed = jnp.where(second, roll(values, 16 * q + 16, 1), packed)
        pk[1 + g] = packed
        values = nat[8, rows, :]
        map_pack = jnp.where((lane >> 3) == 2 * g, roll(values, 16 * g, 1), map_pack)
        map_pack = jnp.where((lane >> 3) == 2 * g + 1, roll(values, 16 * g + 16, 1), map_pack)
    pk[0] = map_pack
    pk[9] = map_pack

    above = jnp.where(C <= 2, COLS, jnp.where(C == COLS - 1, 2, 3))
    below = jnp.where(C >= COLS - 3, COLS, jnp.where(C == 0, 2, 3))
    expected = COLS - 1 + jnp.where(up, above, 0) + jnp.where(down, below, 0)
    pl.semaphore_wait(barrier, expected)

    def remote(src, dst, send, recv, device):
        return pltpu.make_async_remote_copy(
            src_ref=src, dst_ref=dst, send_sem=send, recv_sem=recv,
            device_id=device, device_id_type=MESH,
        )

    plan = [
        (left, pk.at[pl.ds(0, 9)], rx.at[0, pl.ds(0, 9)], (R, C - 1), right),
        (right, pk.at[pl.ds(0, 9)], rx.at[1, pl.ds(0, 9)], (R, C + 1), left),
        (up, nat.at[:, pl.ds(8, 8)], nat.at[:, pl.ds(72, 8)], (R - 1, C), down),
        (down, nat.at[:, pl.ds(64, 8)], nat.at[:, pl.ds(0, 8)], (R + 1, C), up),
        (both(up, left), pk.at[pl.ds(0, 2)], rx.at[0, pl.ds(11, 2)], (R - 1, C - 1), both(down, right)),
        (both(up, right), pk.at[pl.ds(0, 2)], rx.at[1, pl.ds(11, 2)], (R - 1, C + 1), both(down, left)),
        (both(down, left), pk.at[pl.ds(8, 2)], rx.at[0, pl.ds(9, 2)], (R + 1, C - 1), both(up, right)),
        (both(down, right), pk.at[pl.ds(8, 2)], rx.at[1, pl.ds(9, 2)], (R + 1, C + 1), both(up, left)),
    ]

    def send_to_neighbours(which):
        for n in which:
            sends, src, dst, device, _ = plan[n]

            @pl.when(sends)
            def _(n=n, src=src, dst=dst, device=device):
                remote(src, dst, nb_send.at[n], nb_recv.at[n], device).start()

    def await_neighbours(which):
        for n in which:
            _, src, dst, device, gets = plan[n]

            @pl.when(gets)
            def _(n=n, src=src, dst=dst):
                pltpu.make_async_copy(src, dst, nb_recv.at[n]).wait()

    def send_strip(t):
        remote(strips.at[t], band.at[3 + C], st_send.at[0], st_recv.at[0], (R, t)).start()

    send_to_neighbours((0, 1))
    for t in others:
        send_strip(t)

    @pl.when(both(C <= 2, up))
    def _():
        def send_up(n, carry):
            t = (n + other_half) & 15
            remote(strips.at[t], band.at[19 + C], st_send.at[1], st_recv.at[1], (R - 1, t)).start()
            return carry

        lax.fori_loop(0, COLS, send_up, 0)

    @pl.when(both(C >= COLS - 3, down))
    def _():
        def send_down(n, carry):
            t = (n + other_half) & 15
            remote(strips.at[t], band.at[C - 13], st_send.at[1], st_recv.at[2], (R + 1, t)).start()
            return carry

        lax.fori_loop(0, COLS, send_down, 0)

    send_to_neighbours(range(2, 8))
    for t in mates:
        send_strip(t)
    band[3 + C] = strips[C]

    def main_plane(ref, t):
        return ref[pl.ds(t, 8, stride=10), :]

    def side_rows(ref, t):
        return ref[pl.ds(t, 8, stride=5), :], ref[pl.ds(40 + t, 8, stride=5), :]

    def side_inner(ref):
        rows = [side_rows(ref, t) for t in range(5)]
        turned = [(roll(a, 8, 1), roll(a, -72, 1), roll(b, 72, 1), roll(b, -8, 1)) for a, b in rows]
        return [
            jnp.where(low_lanes, jnp.where(lane < 32, a, b), jnp.where(lane < 96, c, d))
            for a, b, c, d in turned
        ]

    first_eight = (lane & 8) == 0
    seam = both(lane >= 56, lane < 72)
    halo_lanes = both(((lane + 8) & 63) < 16, lane >= 0)

    def side_halo(mixed, q, inner):
        turned = [(roll(a, 56 - 16 * q, 1), roll(b, 120 - 16 * q, 1)) for a, b in mixed]
        return [
            jnp.where(halo_lanes, jnp.where(seam, a, b), old) for (a, b), old in zip(turned, inner)
        ]

    def mixed_rows(ref):
        rows = [side_rows(ref, t) for t in range(5)]
        return [(jnp.where(first_eight, a, b), jnp.where(first_eight, b, a)) for a, b in rows]

    def shifted(value, step, side):
        turned = roll(value, step, 0)
        if side:
            turned = jnp.where(sub == (0 if step == 1 else 7), roll(turned, 64, 1), turned)
        return turned

    def around(planes, side):
        return [
            shifted(planes[-2], 1, side), shifted(planes[-1], 1, side),
            shifted(planes[0], -1, side), shifted(planes[1], -1, side),
        ]

    def ghosts(ref, side, channels=range(7)):
        first, count = (SIDE, 5) if side else (MAIN, 10)
        made = [
            around([ref[q, first + n] for n in (0, 1, count - 2, count - 1)], side) for q in channels
        ]
        for q, values in zip(channels, made):
            for slot, value in zip((first - 2, first - 1, first + count, first + count + 1), values):
                ref[q, slot] = value

    def wet_factors(planes, side):
        first, count = (SIDE, 5) if side else (MAIN, 10)
        beyond = around(planes, side)
        padded = [beyond[1]] + planes + [beyond[2]]
        turned = [roll(w, -1, 1) for w in planes]
        for n in range(count + 1):
            ox[first - 1 + n] = 0.05 * padded[n] * padded[n + 1]
        for n in range(count):
            oy[first + n] = 0.05 * planes[n] * turned[n]
            wd[first + n] = 0.2 * planes[n]

    def exchanged(k, mass, s2, settle, w):
        erosion = jnp.maximum(s2 * coef[1, k] - coef[2, k], 0.0)
        return coef[0, k] * mass * settle - erosion * w

    def speeds(h, x, y):
        inv = inverse(jnp.maximum(h, 1.25))
        u, v = x * inv, y * inv
        return inv, u, v, u * u + v * v + 1e-6

    def chunk(src, dst, base, with_bed, start=False, count=True):
        kept, diffs = {}, {}

        def q_at(q, s):
            if (q, s) not in kept:
                kept[q, s] = src[q, base + s]
            return kept[q, s]

        def d_at(q, s):
            if (q, s) not in diffs:
                diffs[q, s] = q_at(q, s + 1) - q_at(q, s)
            return diffs[q, s]

        ahead = {}

        def fetch(p):
            for q in range(7):
                q_at(q, p + 2)
            ahead[p] = [
                tuple(roll(q_at(q, p), step, 1) for step in (1, -1, -2)) for q in range(7)
            ]
            if count and not start:
                ahead[p, "sum"] = [exch[k, base + p] for k in range(FRACTIONS)]

        def finish(p, new, turned, changes):
            for q in range(7):
                dst[q, base + p] = new[q] + turned[q]
            for k, value in enumerate(changes):
                exch[k, base + p] = value

        for s in range(-2, 2):
            for q in range(7):
                q_at(q, s)
        fetch(0)
        lefts, fluxes, twice = {}, {}, {}
        pending = None
        for s in range(-1, 6):
            if 1 <= s < 5:
                fetch(s)
            elif s == 5:
                for q in range(7):
                    q_at(q, 6)
            rights = {}
            for q in range(7):
                slope = minmod(d_at(q, s - 1), d_at(q, s))
                double = q_at(q, s) + q_at(q, s)
                twice[q, s] = double
                lefts[q, s] = double + slope
                rights[q] = double - slope
            if s < 0:
                continue
            a, b, push = face_factors(
                lefts[0, s - 1], lefts[1, s - 1], rights[0], rights[1], ox[base + s - 1]
            )
            for q in range(7):
                flux = lefts[q, s - 1] * a + rights[q] * b
                fluxes[q, s] = flux + push if q == 1 else flux
            if s < 1:
                continue
            p = s - 1
            y_left, y_right = {}, {}
            for q in range(7):
                v = q_at(q, p)
                lower, upper, second = ahead[p][q]
                d = upper - v
                y_left[q] = twice[q, p] + minmod(v - lower, d)
                y_right[q] = upper + upper - minmod(d, second - upper)
            a, b, push = face_factors(y_left[0], y_left[2], y_right[0], y_right[2], oy[base + p])
            new, turned = [], []
            for q in range(7):
                flux = y_left[q] * a + y_right[q] * b
                if q == 2:
                    flux = flux + push
                turned.append(roll(flux, 1, 1))
                new.append(q_at(q, p) - ((fluxes[q, s] - fluxes[q, p]) + flux))
            h = q_at(0, p)
            inv, u, v, s2 = speeds(h, q_at(1, p), q_at(2, p))
            w = wd[base + p]
            drag = (0.02 * w) * root(s2)
            new[1] = new[1] - drag * u
            new[2] = new[2] - drag * v
            if with_bed:
                new[1] = new[1] + h * gx[base + p]
                new[2] = new[2] + h * gy[base + p]
            settle = inv * w
            changes = []
            for k in range(FRACTIONS):
                change = exchanged(k, q_at(3 + k, p), s2, settle, w)
                new[3 + k] = new[3 + k] - change
                if count:
                    changes.append(change if start else ahead[p, "sum"][k] + change)
            if pending is not None:
                finish(*pending)
            pending = (p, new, turned, changes)
        finish(*pending)

    await_neighbours((2, 3))
    wet_main = [main_plane(nat.at[7], t) for t in range(10)]
    wet_factors(wet_main, False)
    for q in range(7):
        planes = [main_plane(nat.at[q], t) for t in range(10)]
        for t in range(10):
            one[q, MAIN + t] = planes[t]
    ghosts(one, False)
    for q in range(8):
        planes = side_inner(nat.at[q])
        for t in range(5):
            if q < 7:
                one[q, SIDE + t] = planes[t]
            else:
                wet[SIDE + t] = planes[t]

    top_half = sub < 4

    def place(values, g):
        cells = values.astype(i32)
        base = 2 * g - 2 + (sub >> 2)
        shift = (cells >> 9) - base + (-16 if g == 0 else (16 if g == 9 else 0))
        return ((cells & 511) - 32 * C + 8) & 127, shift

    places = [place(nat[8, 8 * g : 8 * g + 8, :], g) for g in range(10)]
    for g, (index, shift) in enumerate(places):
        rows = slice(8 * g, 8 * g + 8)
        ibuf[rows, :] = index
        rbuf[rows, :] = shift
        kbuf[rows, :] = (shift + 1) * 7 + (index - 8 - (lane >> 2) + 3)

    def early(c, carry):
        chunk(one, two, MAIN + 5 * c, False, True)
        return carry

    lax.fori_loop(0, 2, early, 0)

    await_neighbours((0, 1, 4, 5, 6, 7))
    groups = [9, *range(1, 9), 12]
    side_values = [jnp.where(first_eight, rx[0, n], rx[1, n]) for n in groups]
    map_side = jnp.where(first_eight, rx[0, 0], rx[1, 0])
    map_top = jnp.where(first_eight, rx[0, 10], rx[1, 10])
    map_low = jnp.where(first_eight, rx[0, 11], rx[1, 11])
    beside = [map_top] + [map_side] * 8 + [map_low]
    beside = [roll(v, -16 * n, 1) for v, n in zip(beside, (7, *range(8), 0))]
    places = [place(values, g) for g, values in enumerate(beside)]
    for g in range(10):
        cn[8 * g : 8 * g + 8, :] = side_values[g]
        sidx[8 * g : 8 * g + 8, :], sshift[8 * g : 8 * g + 8, :] = places[g]
    mixed = mixed_rows(cn)
    wet_side = side_halo(mixed, 7, [wet[SIDE + t] for t in range(5)])
    whole = [side_halo(mixed, q, [one[q, SIDE + t] for t in range(5)]) for q in range(7)]
    wet_factors(wet_side, True)
    for q in range(7):
        for t in range(5):
            one[q, SIDE + t] = whole[q][t]
    ghosts(one, True)
    chunk(one, two, SIDE, False, True)
    ghosts(two, False, (0, 3, 4, 5, 6))
    ghosts(two, True, (0, 3, 4, 5, 6))

    pltpu.make_async_copy(strips.at[pl.ds(0, 15)], band.at[pl.ds(3, 15)], st_recv.at[0]).wait()

    def looked_up(rows, places):
        found = []
        for g, index, shift in places:
            found.append([
                jnp.take_along_axis(
                    jnp.where(top_half, rows[2 * g + n], rows[2 * g + n + 1]),
                    index, axis=1, mode="promise_in_bounds",
                )
                for n in range(3)
            ])
        return [
            jnp.where(
                shift == -1, got[0],
                jnp.where(shift == 0, got[1], jnp.where(shift == 1, got[2], 0.0)),
            )
            for got, (_, _, shift) in zip(found, places)
        ]

    def bed_of(groups, rows):
        span = [slice(8 * g, 8 * g + 8) for g in groups]
        mains = looked_up(rows, [(g, ibuf[r, :], rbuf[r, :]) for g, r in zip(groups, span)])
        sides = looked_up(rows, [(g, sidx[r, :], sshift[r, :]) for g, r in zip(groups, span)])
        for r, a, b in zip(span, mains, sides):
            nbed[0, r, :] = a
            nbed[1, r, :] = b

    rows = {e: jnp.broadcast_to(band[e], (8, 128)) for e in range(3, 19)}
    rows[2], rows[19] = rows[3], rows[18]
    bed_of(range(1, 9), rows)

    @pl.when(down)
    def _():
        pltpu.make_async_copy(strips.at[pl.ds(0, 3)], band.at[pl.ds(19, 3)], st_recv.at[1]).wait()

    @pl.when(up)
    def _():
        pltpu.make_async_copy(strips.at[pl.ds(0, 3)], band.at[pl.ds(0, 3)], st_recv.at[2]).wait()

    rows = {e: jnp.broadcast_to(band[e], (8, 128)) for e in (0, 1, 2, 3, 18, 19, 20, 21)}
    bed_of((0, 9), rows)

    bed_main = [main_plane(nbed.at[0], t) for t in range(10)]
    bed_side = side_halo(mixed_rows(nbed.at[1]), 0, side_inner(nbed.at[0]))
    for planes, side in ((bed_main, False), (bed_side, True)):
        first, count = (SIDE, 5) if side else (MAIN, 10)
        beyond = around(planes, side)
        padded = [beyond[1]] + planes + [beyond[2]]
        turned = [(roll(v, -1, 1), roll(v, 1, 1)) for v in planes]
        scale = [-0.5 * wd[first + n] for n in range(count)]
        slope_x = [scale[n] * (padded[n + 2] - padded[n]) for n in range(count)]
        slope_y = [scale[n] * (turned[n][0] - turned[n][1]) for n in range(count)]
        depths = [one[0, first + n] for n in range(count)]
        new_x = [two[1, first + n] + depths[n] * slope_x[n] for n in range(count)]
        new_y = [two[2, first + n] + depths[n] * slope_y[n] for n in range(count)]
        for n in range(count):
            gx[first + n] = slope_x[n]
            gy[first + n] = slope_y[n]
            two[1, first + n] = new_x[n]
            two[2, first + n] = new_y[n]
    ghosts(two, False, (1, 2))
    ghosts(two, True, (1, 2))

    def step(src, dst, count):
        def each(c, carry):
            chunk(src, dst, MAIN + 5 * c + 4 * (c // 2), True, False, count)
            return carry

        lax.fori_loop(0, 3, each, 0)

    states = (one, two)
    for substep in range(1, SUBSTEPS - 1):
        src, dst = states[substep % 2], states[1 - substep % 2]
        step(src, dst, True)
        ghosts(dst, False)
        ghosts(dst, True)
    before_last, after_last = states[(SUBSTEPS - 1) % 2], states[SUBSTEPS % 2]

    slots = [*range(MAIN, MAIN + 10), *range(SIDE, SIDE + 5)]
    totals = {}
    for slot in slots:
        h, x, y, *masses = [before_last[q, slot] for q in range(7)]
        inv, _, _, s2 = speeds(h, x, y)
        w = wd[slot]
        for k in range(FRACTIONS):
            totals[k, slot] = exch[k, slot] + exchanged(k, masses[k], s2, inv * w, w)

    edge = jnp.logical_or(lane < 8, lane >= 120)

    def natural(planes, n):
        mains, sides = planes[:10], planes[10:]
        turned = [tuple(roll(v, step, 1) for step in (-8, 72, -72, 8)) for v in sides]
        for t, value in enumerate(mains):
            nmain[n, pl.ds(t, 8, stride=10), :] = value
        for t, (a, b, c, d) in enumerate(turned):
            nside[n, pl.ds(t, 8, stride=5), :] = jnp.where(low_lanes, a, b)
            nside[n, pl.ds(40 + t, 8, stride=5), :] = jnp.where(low_lanes, c, d)

    for k in range(FRACTIONS):
        natural([totals[k, slot] for slot in slots], k)
    wide_edge = jnp.concatenate([edge, edge], axis=0)

    keys = [kbuf[pl.ds(8 + p, 16, stride=4), :] for p in range(4)]
    fourth = [pl.ds(8 + p, 16, stride=4) for p in range(4)]
    planes = [
        [jnp.where(wide_edge, nside[k, rows, :], nmain[k, rows, :]) for rows in fourth]
        for k in range(FRACTIONS)
    ]
    for d in range(7):
        kept = [0.0] * FRACTIONS
        for r in range(3):
            hits = [keys[p] == r * 7 + d for p in range(4)]
            for k in range(FRACTIONS):
                acc = jnp.where(hits[0], planes[k][0], 0.0)
                for p in range(1, 4):
                    acc = acc + jnp.where(hits[p], planes[k][p], 0.0)
                kept[k] = kept[k] + (acc if r == 1 else roll(acc, r - 1, 0))
        for k in range(FRACTIONS):
            high = kept[k].astype(jnp.bfloat16)
            rows = slice(16 * k, 16 * k + 16)
            mhi[rows, 128 * d : 128 * d + 128] = high
            mlo[rows, 128 * d : 128 * d + 128] = (kept[k] - high.astype(f32)).astype(jnp.bfloat16)
    res = jnp.dot(mhi[...], sel[...], preferred_element_type=f32)
    res = 25.0 * (res + jnp.dot(mlo[...], sel[...], preferred_element_type=f32))
    parts = [res[16 * k : 16 * k + 16] for k in range(FRACTIONS)]
    nsum[...] = (parts[0] + parts[1]) + (parts[2] + parts[3])
    for n in range(2):
        pair = parts[2 * n] + roll(parts[2 * n + 1], 64, 1)
        for r in range(COLS):
            tot[r, :, 128 * n : 128 * n + 128] = pair[r : r + 1, :]

    def send_sum(r):
        remote(tot.at[r], rs.at[C], ph_send, ph_recv, (R, r)).start()

    for r in others:
        send_sum(r)

    @pl.when(left)
    def _():
        remote(nsum, nrx.at[0], ns_send.at[0], ns_recv.at[0], (R, C - 1)).start()

    @pl.when(right)
    def _():
        remote(nsum, nrx.at[1], ns_send.at[1], ns_recv.at[1], (R, C + 1)).start()

    for r in mates:
        send_sum(r)
    rs[C] = tot[C]

    step(before_last, after_last, False)
    for q in range(7):
        natural([after_last[q, s] for s in slots], 4 + q)
    for q in range(7):
        for g in range(1, 9):
            rows = slice(8 * g, 8 * g + 8)
            o_fields[q, rows, :] = jnp.where(edge, nside[4 + q, rows, :], nmain[4 + q, rows, :])

    for n, (sends, src, dst, device, _) in enumerate(plan):

        @pl.when(sends)
        def _(n=n, src=src, dst=dst, device=device):
            remote(src, dst, nb_send.at[n], nb_recv.at[n], device).wait_send()

    pltpu.make_async_copy(strips.at[pl.ds(0, 15)], band.at[pl.ds(0, 15)], st_send.at[0]).wait()

    @pl.when(jnp.logical_or(both(C <= 2, up), both(C >= COLS - 3, down)))
    def _():
        pltpu.make_async_copy(strips, band.at[pl.ds(0, 16)], st_send.at[1]).wait()

    @pl.when(right)
    def _():
        pltpu.make_async_copy(nsum, nrx.at[0], ns_recv.at[0]).wait()

    @pl.when(left)
    def _():
        pltpu.make_async_copy(nsum, nrx.at[1], ns_recv.at[1]).wait()

    for e in range(16):
        band2[e : e + 1, :] = band[3 + e]
    wnew[1:17, :] = band2[...] + (nsum[...] + roll(nrx[0], 32, 1) + roll(nrx[1], -32, 1))
    wide = [jnp.broadcast_to(wnew[n : n + 1, :], (8, 128)) for n in range(18)]
    inner = [slice(8 + 8 * g, 16 + 8 * g) for g in range(8)]
    found = looked_up(wide, [(g, ibuf[r, :], rbuf[r, :]) for g, r in enumerate(inner)])
    for g, value in enumerate(found):
        o_fine[8 * g : 8 * g + 8, :] = value

    pltpu.make_async_copy(tot.at[pl.ds(0, 15)], rs.at[pl.ds(0, 15)], ph_recv).wait()
    row_lane = lax.broadcasted_iota(i32, (1, 128), 1)
    row_low = row_lane < 64
    lines = [[jnp.zeros((1, 128), f32) for _ in range(4)] for _ in range(FRACTIONS)]
    for s in range(COLS):
        q, m = divmod(s, 4)
        for n in range(2):
            pair = rs[s, :, 128 * n : 128 * n + 128]
            for half in range(2):
                line = lines[2 * n + half]
                piece = jnp.where(row_low, 0.0, pair) if half else jnp.where(row_low, pair, 0.0)
                piece = roll(piece, 32 * m - 8 - 64 * half, 1)
                if m == 0:
                    line[q] = line[q] + jnp.where(row_low, piece, 0.0)
                    if q > 0:
                        line[q - 1] = line[q - 1] + jnp.where(row_low, 0.0, piece)
                elif m == 3:
                    line[q] = line[q] + jnp.where(row_low, 0.0, piece)
                    if q < 3:
                        line[q + 1] = line[q + 1] + jnp.where(row_low, piece, 0.0)
                else:
                    line[q] = line[q] + piece
    for q in range(4):
        cols = slice(128 * q, 128 * q + 128)
        total = None
        for k in range(FRACTIONS):
            line = lines[k][q]
            o_dep[k, :, cols] = line
            total = line if k == 0 else total + line
        o_bed[:, cols] = bedv[:, cols] + total
    @pl.when(left)
    def _():
        pltpu.make_async_copy(nsum, nrx.at[0], ns_send.at[0]).wait()

    @pl.when(right)
    def _():
        pltpu.make_async_copy(nsum, nrx.at[1], ns_send.at[1]).wait()

    pltpu.make_async_copy(tot.at[pl.ds(0, 15)], rs.at[pl.ds(0, 15)], ph_send).wait()


def handed_on(fields, fine, bed, dep, o_depth, o_disch, o_sed, o_fine, o_bed, o_dep, sem):
    mid = pl.ds(8, 64)
    pairs = (
        (fields.at[0, mid], o_depth),
        (fields.at[pl.ds(1, 2), mid], o_disch),
        (fields.at[pl.ds(3, 4), mid], o_sed),
        (fine, o_fine),
        (bed, o_bed),
        (dep, o_dep),
    )
    copies = [pltpu.make_async_copy(src, dst, sem.at[n]) for n, (src, dst) in enumerate(pairs)]
    for copy in copies:
        copy.start()
    for copy in copies:
        copy.wait()


def local(water_depth, discharge, sediment, bed_level, cell_map, wet_mask, sediment_params):
    hbm = pl.BlockSpec(memory_space=pl.ANY)
    dma = pltpu.SemaphoreType.DMA
    vmem = pl.BlockSpec(memory_space=pltpu.VMEM)
    bf16 = jnp.bfloat16
    plane = (SLOTS, 8, 128)
    scratch = [
        ((9, 80, 128), f32),
        ((2, 64, 128), i32),
        ((1, 512), f32),
        ((10, 8, 128), f32),
        ((2, 13, 8, 128), f32),
        ((16, 1, 128), f32),
        ((22, 1, 128), f32),
        ((16, 128), f32),
        ((80, 128), f32),
        ((2, 80, 128), f32),
        ((80, 128), i32),
        ((80, 128), i32),
        ((80, 128), i32),
        ((80, 128), i32),
        ((80, 128), i32),
        ((7, *plane), f32),
        ((7, *plane), f32),
        (plane, f32),
        (plane, f32),
        (plane, f32),
        (plane, f32),
        (plane, f32),
        (plane, f32),
        ((3, 4, 8, 128), f32),
        ((4, *plane), f32),
        ((11, 80, 128), f32),
        ((11, 80, 128), f32),
        ((896, 128), bf16),
        ((64, 896), bf16),
        ((64, 896), bf16),
        ((16, 1, 256), f32),
        ((16, 128), f32),
        ((2, 16, 128), f32),
        ((16, 1, 256), f32),
        ((24, 128), f32),
    ]
    results = tuple(
        jax.ShapeDtypeStruct(shape, f32)
        for shape in ((64, 128), (2, 64, 128), (4, 64, 128), (64, 128), (1, 512), (4, 1, 512))
    )
    made = pl.pallas_call(
        kernel,
        out_shape=tuple(
            pltpu.VMEM(shape, f32) for shape in ((7, 80, 128), (64, 128), (1, 512), (4, 1, 512))
        ),
        in_specs=[hbm] * 7,
        out_specs=(vmem,) * 4,
        scratch_shapes=[pltpu.SMEM((3, FRACTIONS), f32)]
        + [pltpu.VMEM(shape, dtype) for shape, dtype in scratch]
        + [dma((7,)), dma((8,)), dma((8,)), dma((2,)), dma((3,)), dma(()), dma(()), dma((2,)), dma((2,))],
        compiler_params=pltpu.CompilerParams(
            collective_id=0, has_side_effects=True, vmem_limit_bytes=56 * 1024 * 1024
        ),
    )(water_depth, discharge, sediment, bed_level, cell_map, wet_mask, sediment_params)
    return pl.pallas_call(
        handed_on,
        out_shape=results,
        in_specs=[hbm] * 4,
        out_specs=(hbm,) * 6,
        scratch_shapes=[dma((6,))],
    )(*(pltpu.with_memory_space_constraint(x, pltpu.VMEM) for x in made))


def solution(mesh):
    placed = (
        P("row", "col"),
        P(None, "row", "col"),
        P(None, "row", "col"),
        P(("row", "col"), None),
        P("row", "col"),
        P("row", "col"),
        P(),
    )
    return jax.shard_map(
        local,
        mesh=mesh,
        in_specs=placed,
        out_specs=(
            P("row", "col"),
            P(None, "row", "col"),
            P(None, "row", "col"),
            P("row", "col"),
            P(("row", "col"), None),
            P(None, ("row", "col"), None),
        ),
        check_vma=False,
    )
```

```python
import jax
import jax.numpy as jnp
from jax import lax
from jax.experimental import pallas as pl
from jax.experimental.pallas import tpu as pltpu
from jax.sharding import PartitionSpec as P

FRACTIONS = 4
SUBSTEPS = 4
ROWS = 32
COLS = 16
MAIN, SIDE = 2, 16
SLOTS = 23

MESH = pl.DeviceIdType.MESH
f32 = jnp.float32
i32 = jnp.int32


def roll(x, shift, axis):
    return pltpu.roll(x, shift % x.shape[axis], axis)


def minmod(a, b):
    return jnp.maximum(jnp.minimum(b, 0.0), jnp.minimum(a, jnp.maximum(b, 0.0)))


def inverse(x):
    guess = pl.reciprocal(x, approx=True)
    return guess * (2.0 - x * guess)


def root(x):
    return x * lax.rsqrt(x + 1e-35)


def face_factors(h_l, n_l, h_r, n_r, opened):
    w_l = n_l * inverse(jnp.maximum(h_l, 2.5))
    w_r = n_r * inverse(jnp.maximum(h_r, 2.5))
    c_l = jnp.abs(w_l) + root(0.5 * h_l)
    c_r = jnp.abs(w_r) + root(0.5 * h_r)
    fastest = jnp.maximum(c_l, c_r)
    push = (0.25 * opened) * (h_l * h_l + h_r * h_r)
    return opened * (w_l + fastest), opened * (w_r - fastest), push


def kernel(
    depth, disch, sed, bed, cmap, wetm, factors,
    o_fields, o_fine, o_bed, o_dep,
    params, nat, raw, bedv, pk, rx, strips, band, band2, cn, nbed, sidx, sshift,
    ibuf, rbuf, kbuf, one, two, wet, gx, gy, ox, oy, wd, coef,
    exch, nmain, nside, sel, mhi, mlo, tot, nsum, nrx, rs, wnew,
    in_sem, nb_send, nb_recv, st_send, st_recv, ph_send, ph_recv, ns_send, ns_recv,
):
    R = lax.axis_index("row")
    C = lax.axis_index("col")
    other_half = jnp.where(C < 8, 8, 0)
    barrier = pltpu.get_barrier_semaphore()

    others = [other_half + (((C & 7) + k) & 7) for k in (4, 5, 3, 6, 2, 7, 1, 0)]
    mates = [8 - other_half + (((C & 7) + k) & 7) for k in range(1, 8)]
    up, down = R > 0, R < ROWS - 1
    left, right = C > 0, C < COLS - 1
    both = jnp.logical_and

    def greet(row, c):
        pl.semaphore_signal(barrier, inc=1, device_id=(row, c), device_id_type=MESH)

    for c in others:
        greet(R, c)

    @pl.when(down)
    def _():
        for c in range(3):
            greet(R + 1, c)

    @pl.when(up)
    def _():
        for c in range(COLS - 3, COLS):
            greet(R - 1, c)

    for c in mates:
        greet(R, c)
    for step in (-1, 0, 1):

        @pl.when(both(down, both(C + step > 2, C + step < COLS)))
        def _(step=step):
            greet(R + 1, C + step)

        @pl.when(both(up, both(C + step >= 0, C + step < COLS - 3)))
        def _(step=step):
            greet(R - 1, C + step)

    mid = pl.ds(8, 64)
    loads = [
        pltpu.make_async_copy(depth, nat.at[0, mid], in_sem.at[0]),
        pltpu.make_async_copy(disch, nat.at[pl.ds(1, 2), mid], in_sem.at[1]),
        pltpu.make_async_copy(sed, nat.at[pl.ds(3, 4), mid], in_sem.at[2]),
        pltpu.make_async_copy(bed, bedv, in_sem.at[3]),
        pltpu.make_async_copy(cmap, raw.at[0], in_sem.at[4]),
        pltpu.make_async_copy(wetm, raw.at[1], in_sem.at[5]),
        pltpu.make_async_copy(factors, params, in_sem.at[6]),
    ]
    for copy in loads:
        copy.start()

    lane = lax.broadcasted_iota(i32, (8, 128), 1)
    sub = lax.broadcasted_iota(i32, (8, 128), 0)
    low_lanes = lane < 64

    far = f32(1 << 20)

    @pl.when(R == 0)
    def _():
        nat[0:8, 0:8, :] = jnp.zeros((8, 8, 128), f32)
        nat[8, 0:8, :] = jnp.full((8, 128), far)
        band[0:3] = jnp.zeros((3, 1, 128), f32)

    @pl.when(R == ROWS - 1)
    def _():
        nat[0:8, 72:80, :] = jnp.zeros((8, 8, 128), f32)
        nat[8, 72:80, :] = jnp.full((8, 128), far)
        band[19:22] = jnp.zeros((3, 1, 128), f32)

    for side, edge in ((0, C == COLS - 1), (1, C == 0)):

        @pl.when(edge)
        def _(side=side):
            rx[side, 0] = jnp.full((8, 128), far)
            rx[side, 1:9] = jnp.zeros((8, 8, 128), f32)

        @pl.when(jnp.logical_or(edge, R == 0))
        def _(side=side):
            rx[side, 9] = jnp.zeros((8, 128), f32)
            rx[side, 10] = jnp.full((8, 128), far)

        @pl.when(jnp.logical_or(edge, R == ROWS - 1))
        def _(side=side):
            rx[side, 11] = jnp.full((8, 128), far)
            rx[side, 12] = jnp.zeros((8, 128), f32)

    @pl.when(C == COLS - 1)
    def _():
        nrx[0] = jnp.zeros((16, 128), f32)

    @pl.when(C == 0)
    def _():
        nrx[1] = jnp.zeros((16, 128), f32)

    wnew[...] = jnp.zeros((24, 128), f32)

    from_col = lax.broadcasted_iota(i32, (128, 128), 0) // 4
    to_lane = lax.broadcasted_iota(i32, (128, 128), 1)
    for d in range(7):
        sel[128 * d : 128 * d + 128, :] = (
            jnp.where(to_lane - from_col == d + 5, 1.0, 0.0).astype(jnp.bfloat16)
        )

    for copy in loads:
        copy.wait()
    for k in range(FRACTIONS):
        erode = 0.002 * jnp.full((8, 128), params[2, k], f32)
        coef[0, k] = 0.05 * jnp.full((8, 128), params[0, k], f32)
        coef[1, k] = erode / (0.05 * jnp.full((8, 128), params[1, k], f32))
        coef[2, k] = erode

    nat[8, 8:72, :] = raw[0].astype(f32)
    nat[7, 8:72, :] = raw[1].astype(f32)

    at = 32 * lax.broadcasted_iota(i32, (16, 128), 0) - 8 + lax.broadcasted_iota(i32, (16, 128), 1)
    window = jnp.zeros((16, 128), f32)
    for q in range(4):
        chunk = jnp.broadcast_to(bedv[:, 128 * q : 128 * q + 128], (16, 128))
        got = jnp.take_along_axis(chunk, at & 127, axis=1, mode="promise_in_bounds")
        window = jnp.where((at >> 7) == q, got, window)
    for t in range(COLS):
        strips[t] = window[t : t + 1, :]

    map_pack = jnp.zeros((8, 128), f32)
    for g in range(8):
        rows = slice(8 + 8 * g, 16 + 8 * g)
        packed = jnp.zeros((8, 128), f32)
        for q in range(8):
            first = (lane >> 3) == 2 * q
            second = (lane >> 3) == 2 * q + 1
            values = nat[q, rows, :]
            packed = jnp.where(first, roll(values, 16 * q, 1), packed)
            packed = jnp.where(second, roll(values, 16 * q + 16, 1), packed)
        pk[1 + g] = packed
        values = nat[8, rows, :]
        map_pack = jnp.where((lane >> 3) == 2 * g, roll(values, 16 * g, 1), map_pack)
        map_pack = jnp.where((lane >> 3) == 2 * g + 1, roll(values, 16 * g + 16, 1), map_pack)
    pk[0] = map_pack
    pk[9] = map_pack

    above = jnp.where(C <= 2, COLS, jnp.where(C == COLS - 1, 2, 3))
    below = jnp.where(C >= COLS - 3, COLS, jnp.where(C == 0, 2, 3))
    expected = COLS - 1 + jnp.where(up, above, 0) + jnp.where(down, below, 0)
    pl.semaphore_wait(barrier, expected)

    def remote(src, dst, send, recv, device):
        return pltpu.make_async_remote_copy(
            src_ref=src, dst_ref=dst, send_sem=send, recv_sem=recv,
            device_id=device, device_id_type=MESH,
        )

    plan = [
        (left, pk.at[pl.ds(0, 9)], rx.at[0, pl.ds(0, 9)], (R, C - 1), right),
        (right, pk.at[pl.ds(0, 9)], rx.at[1, pl.ds(0, 9)], (R, C + 1), left),
        (up, nat.at[:, pl.ds(8, 8)], nat.at[:, pl.ds(72, 8)], (R - 1, C), down),
        (down, nat.at[:, pl.ds(64, 8)], nat.at[:, pl.ds(0, 8)], (R + 1, C), up),
        (both(up, left), pk.at[pl.ds(0, 2)], rx.at[0, pl.ds(11, 2)], (R - 1, C - 1), both(down, right)),
        (both(up, right), pk.at[pl.ds(0, 2)], rx.at[1, pl.ds(11, 2)], (R - 1, C + 1), both(down, left)),
        (both(down, left), pk.at[pl.ds(8, 2)], rx.at[0, pl.ds(9, 2)], (R + 1, C - 1), both(up, right)),
        (both(down, right), pk.at[pl.ds(8, 2)], rx.at[1, pl.ds(9, 2)], (R + 1, C + 1), both(up, left)),
    ]

    def send_to_neighbours(which):
        for n in which:
            sends, src, dst, device, _ = plan[n]

            @pl.when(sends)
            def _(n=n, src=src, dst=dst, device=device):
                remote(src, dst, nb_send.at[n], nb_recv.at[n], device).start()

    def await_neighbours(which):
        for n in which:
            _, src, dst, device, gets = plan[n]

            @pl.when(gets)
            def _(n=n, src=src, dst=dst):
                pltpu.make_async_copy(src, dst, nb_recv.at[n]).wait()

    def send_strip(t):
        remote(strips.at[t], band.at[3 + C], st_send.at[0], st_recv.at[0], (R, t)).start()

    send_to_neighbours((0, 1))
    for t in others:
        send_strip(t)

    def send_beyond(targets):
        @pl.when(both(C <= 2, up))
        def _():
            for t in targets:
                remote(
                    strips.at[t], band.at[19 + C], st_send.at[1], st_recv.at[1], (R - 1, t)
                ).start()

        @pl.when(both(C >= COLS - 3, down))
        def _():
            for t in targets:
                remote(
                    strips.at[t], band.at[C - 13], st_send.at[1], st_recv.at[2], (R + 1, t)
                ).start()

    send_beyond(others)
    send_to_neighbours(range(2, 8))
    for t in mates:
        send_strip(t)
    send_beyond([*mates, C])
    band[3 + C] = strips[C]

    def main_plane(ref, t):
        return ref[pl.ds(t, 8, stride=10), :]

    def side_rows(ref, t):
        return ref[pl.ds(t, 8, stride=5), :], ref[pl.ds(40 + t, 8, stride=5), :]

    def side_inner(ref):
        rows = [side_rows(ref, t) for t in range(5)]
        turned = [(roll(a, 8, 1), roll(a, -72, 1), roll(b, 72, 1), roll(b, -8, 1)) for a, b in rows]
        return [
            jnp.where(low_lanes, jnp.where(lane < 32, a, b), jnp.where(lane < 96, c, d))
            for a, b, c, d in turned
        ]

    first_eight = (lane & 8) == 0
    seam = both(lane >= 56, lane < 72)
    halo_lanes = both(((lane + 8) & 63) < 16, lane >= 0)

    def side_halo(mixed, q, inner):
        turned = [(roll(a, 56 - 16 * q, 1), roll(b, 120 - 16 * q, 1)) for a, b in mixed]
        return [
            jnp.where(halo_lanes, jnp.where(seam, a, b), old) for (a, b), old in zip(turned, inner)
        ]

    def mixed_rows(ref):
        rows = [side_rows(ref, t) for t in range(5)]
        return [(jnp.where(first_eight, a, b), jnp.where(first_eight, b, a)) for a, b in rows]

    def shifted(value, step, side):
        turned = roll(value, step, 0)
        if side:
            turned = jnp.where(sub == (0 if step == 1 else 7), roll(turned, 64, 1), turned)
        return turned

    def around(planes, side):
        return [
            shifted(planes[-2], 1, side), shifted(planes[-1], 1, side),
            shifted(planes[0], -1, side), shifted(planes[1], -1, side),
        ]

    def ghosts(ref, side, channels=range(7)):
        first, count = (SIDE, 5) if side else (MAIN, 10)
        made = [
            around([ref[q, first + n] for n in (0, 1, count - 2, count - 1)], side) for q in channels
        ]
        for q, values in zip(channels, made):
            for slot, value in zip((first - 2, first - 1, first + count, first + count + 1), values):
                ref[q, slot] = value

    def wet_factors(planes, side):
        first, count = (SIDE, 5) if side else (MAIN, 10)
        beyond = around(planes, side)
        padded = [beyond[1]] + planes + [beyond[2]]
        turned = [roll(w, -1, 1) for w in planes]
        for n in range(count + 1):
            ox[first - 1 + n] = 0.05 * padded[n] * padded[n + 1]
        for n in range(count):
            oy[first + n] = 0.05 * planes[n] * turned[n]
            wd[first + n] = 0.2 * planes[n]

    def exchanged(k, mass, s2, settle, w):
        erosion = jnp.maximum(s2 * coef[1, k] - coef[2, k], 0.0)
        return coef[0, k] * mass * settle - erosion * w

    def speeds(h, x, y):
        inv = inverse(jnp.maximum(h, 1.25))
        u, v = x * inv, y * inv
        return inv, u, v, u * u + v * v + 1e-6

    def chunk(src, dst, base, with_bed, start=False, count=True):
        kept, diffs = {}, {}

        def q_at(q, s):
            if (q, s) not in kept:
                kept[q, s] = src[q, base + s]
            return kept[q, s]

        def d_at(q, s):
            if (q, s) not in diffs:
                diffs[q, s] = q_at(q, s + 1) - q_at(q, s)
            return diffs[q, s]

        ahead = {}

        def fetch(p):
            for q in range(7):
                q_at(q, p + 2)
            ahead[p] = [
                tuple(roll(q_at(q, p), step, 1) for step in (1, -1, -2)) for q in range(7)
            ]
            if count and not start:
                ahead[p, "sum"] = [exch[k, base + p] for k in range(FRACTIONS)]

        def finish(p, new, turned, changes):
            for q in range(7):
                dst[q, base + p] = new[q] + turned[q]
            for k, value in enumerate(changes):
                exch[k, base + p] = value

        for s in range(-2, 2):
            for q in range(7):
                q_at(q, s)
        fetch(0)
        lefts, fluxes, twice = {}, {}, {}
        pending = None
        for s in range(-1, 6):
            if 1 <= s < 5:
                fetch(s)
            elif s == 5:
                for q in range(7):
                    q_at(q, 6)
            rights = {}
            for q in range(7):
                slope = minmod(d_at(q, s - 1), d_at(q, s))
                double = q_at(q, s) + q_at(q, s)
                twice[q, s] = double
                lefts[q, s] = double + slope
                rights[q] = double - slope
            if s < 0:
                continue
            a, b, push = face_factors(
                lefts[0, s - 1], lefts[1, s - 1], rights[0], rights[1], ox[base + s - 1]
            )
            for q in range(7):
                flux = lefts[q, s - 1] * a + rights[q] * b
                fluxes[q, s] = flux + push if q == 1 else flux
            if s < 1:
                continue
            p = s - 1
            y_left, y_right = {}, {}
            for q in range(7):
                v = q_at(q, p)
                lower, upper, second = ahead[p][q]
                d = upper - v
                y_left[q] = twice[q, p] + minmod(v - lower, d)
                y_right[q] = upper + upper - minmod(d, second - upper)
            a, b, push = face_factors(y_left[0], y_left[2], y_right[0], y_right[2], oy[base + p])
            new, turned = [], []
            for q in range(7):
                flux = y_left[q] * a + y_right[q] * b
                if q == 2:
                    flux = flux + push
                turned.append(roll(flux, 1, 1))
                new.append(q_at(q, p) - ((fluxes[q, s] - fluxes[q, p]) + flux))
            h = q_at(0, p)
            inv, u, v, s2 = speeds(h, q_at(1, p), q_at(2, p))
            w = wd[base + p]
            drag = (0.02 * w) * root(s2)
            new[1] = new[1] - drag * u
            new[2] = new[2] - drag * v
            if with_bed:
                new[1] = new[1] + h * gx[base + p]
                new[2] = new[2] + h * gy[base + p]
            settle = inv * w
            changes = []
            for k in range(FRACTIONS):
                change = exchanged(k, q_at(3 + k, p), s2, settle, w)
                new[3 + k] = new[3 + k] - change
                if count:
                    changes.append(change if start else ahead[p, "sum"][k] + change)
            if pending is not None:
                finish(*pending)
            pending = (p, new, turned, changes)
        finish(*pending)

    await_neighbours((2, 3))
    wet_main = [main_plane(nat.at[7], t) for t in range(10)]
    wet_factors(wet_main, False)
    for q in range(7):
        planes = [main_plane(nat.at[q], t) for t in range(10)]
        for t in range(10):
            one[q, MAIN + t] = planes[t]
    ghosts(one, False)
    for q in range(8):
        planes = side_inner(nat.at[q])
        for t in range(5):
            if q < 7:
                one[q, SIDE + t] = planes[t]
            else:
                wet[SIDE + t] = planes[t]

    top_half = sub < 4

    def place(values, g):
        cells = values.astype(i32)
        base = 2 * g - 2 + (sub >> 2)
        shift = (cells >> 9) - base + (-16 if g == 0 else (16 if g == 9 else 0))
        return ((cells & 511) - 32 * C + 8) & 127, shift

    places = [place(nat[8, 8 * g : 8 * g + 8, :], g) for g in range(10)]
    for g, (index, shift) in enumerate(places):
        rows = slice(8 * g, 8 * g + 8)
        ibuf[rows, :] = index
        rbuf[rows, :] = shift
        kbuf[rows, :] = (shift + 1) * 7 + (index - 8 - (lane >> 2) + 3)

    def early(c, carry):
        chunk(one, two, MAIN + 5 * c, False, True)
        return carry

    lax.fori_loop(0, 2, early, 0)

    await_neighbours((0, 1, 4, 5, 6, 7))
    groups = [9, *range(1, 9), 12]
    side_values = [jnp.where(first_eight, rx[0, n], rx[1, n]) for n in groups]
    map_side = jnp.where(first_eight, rx[0, 0], rx[1, 0])
    map_top = jnp.where(first_eight, rx[0, 10], rx[1, 10])
    map_low = jnp.where(first_eight, rx[0, 11], rx[1, 11])
    beside = [map_top] + [map_side] * 8 + [map_low]
    beside = [roll(v, -16 * n, 1) for v, n in zip(beside, (7, *range(8), 0))]
    places = [place(values, g) for g, values in enumerate(beside)]
    for g in range(10):
        cn[8 * g : 8 * g + 8, :] = side_values[g]
        sidx[8 * g : 8 * g + 8, :], sshift[8 * g : 8 * g + 8, :] = places[g]
    mixed = mixed_rows(cn)
    wet_side = side_halo(mixed, 7, [wet[SIDE + t] for t in range(5)])
    whole = [side_halo(mixed, q, [one[q, SIDE + t] for t in range(5)]) for q in range(7)]
    wet_factors(wet_side, True)
    for q in range(7):
        for t in range(5):
            one[q, SIDE + t] = whole[q][t]
    ghosts(one, True)
    chunk(one, two, SIDE, False, True)
    ghosts(two, False, (0, 3, 4, 5, 6))
    ghosts(two, True, (0, 3, 4, 5, 6))

    pltpu.make_async_copy(strips.at[pl.ds(0, 15)], band.at[pl.ds(3, 15)], st_recv.at[0]).wait()

    def looked_up(rows, places):
        found = []
        for g, index, shift in places:
            found.append([
                jnp.take_along_axis(
                    jnp.where(top_half, rows[2 * g + n], rows[2 * g + n + 1]),
                    index, axis=1, mode="promise_in_bounds",
                )
                for n in range(3)
            ])
        return [
            jnp.where(
                shift == -1, got[0],
                jnp.where(shift == 0, got[1], jnp.where(shift == 1, got[2], 0.0)),
            )
            for got, (_, _, shift) in zip(found, places)
        ]

    def bed_of(groups, rows):
        span = [slice(8 * g, 8 * g + 8) for g in groups]
        mains = looked_up(rows, [(g, ibuf[r, :], rbuf[r, :]) for g, r in zip(groups, span)])
        sides = looked_up(rows, [(g, sidx[r, :], sshift[r, :]) for g, r in zip(groups, span)])
        for r, a, b in zip(span, mains, sides):
            nbed[0, r, :] = a
            nbed[1, r, :] = b

    rows = {e: jnp.broadcast_to(band[e], (8, 128)) for e in range(3, 19)}
    rows[2], rows[19] = rows[3], rows[18]
    bed_of(range(1, 9), rows)

    @pl.when(down)
    def _():
        pltpu.make_async_copy(strips.at[pl.ds(0, 3)], band.at[pl.ds(19, 3)], st_recv.at[1]).wait()

    @pl.when(up)
    def _():
        pltpu.make_async_copy(strips.at[pl.ds(0, 3)], band.at[pl.ds(0, 3)], st_recv.at[2]).wait()

    rows = {e: jnp.broadcast_to(band[e], (8, 128)) for e in (0, 1, 2, 3, 18, 19, 20, 21)}
    bed_of((0, 9), rows)

    bed_main = [main_plane(nbed.at[0], t) for t in range(10)]
    bed_side = side_halo(mixed_rows(nbed.at[1]), 0, side_inner(nbed.at[0]))
    for planes, side in ((bed_main, False), (bed_side, True)):
        first, count = (SIDE, 5) if side else (MAIN, 10)
        beyond = around(planes, side)
        padded = [beyond[1]] + planes + [beyond[2]]
        turned = [(roll(v, -1, 1), roll(v, 1, 1)) for v in planes]
        scale = [-0.5 * wd[first + n] for n in range(count)]
        slope_x = [scale[n] * (padded[n + 2] - padded[n]) for n in range(count)]
        slope_y = [scale[n] * (turned[n][0] - turned[n][1]) for n in range(count)]
        depths = [one[0, first + n] for n in range(count)]
        new_x = [two[1, first + n] + depths[n] * slope_x[n] for n in range(count)]
        new_y = [two[2, first + n] + depths[n] * slope_y[n] for n in range(count)]
        for n in range(count):
            gx[first + n] = slope_x[n]
            gy[first + n] = slope_y[n]
            two[1, first + n] = new_x[n]
            two[2, first + n] = new_y[n]
    ghosts(two, False, (1, 2))
    ghosts(two, True, (1, 2))

    def step(src, dst, count):
        def each(c, carry):
            chunk(src, dst, MAIN + 5 * c + 4 * (c // 2), True, False, count)
            return carry

        lax.fori_loop(0, 3, each, 0)

    states = (one, two)
    for substep in range(1, SUBSTEPS - 1):
        src, dst = states[substep % 2], states[1 - substep % 2]
        step(src, dst, True)
        ghosts(dst, False)
        ghosts(dst, True)
    before_last, after_last = states[(SUBSTEPS - 1) % 2], states[SUBSTEPS % 2]

    slots = [*range(MAIN, MAIN + 10), *range(SIDE, SIDE + 5)]
    totals = {}
    for slot in slots:
        h, x, y, *masses = [before_last[q, slot] for q in range(7)]
        inv, _, _, s2 = speeds(h, x, y)
        w = wd[slot]
        for k in range(FRACTIONS):
            totals[k, slot] = exch[k, slot] + exchanged(k, masses[k], s2, inv * w, w)

    edge = jnp.logical_or(lane < 8, lane >= 120)

    def natural(planes, n):
        mains, sides = planes[:10], planes[10:]
        turned = [tuple(roll(v, step, 1) for step in (-8, 72, -72, 8)) for v in sides]
        for t, value in enumerate(mains):
            nmain[n, pl.ds(t, 8, stride=10), :] = value
        for t, (a, b, c, d) in enumerate(turned):
            nside[n, pl.ds(t, 8, stride=5), :] = jnp.where(low_lanes, a, b)
            nside[n, pl.ds(40 + t, 8, stride=5), :] = jnp.where(low_lanes, c, d)

    for k in range(FRACTIONS):
        natural([totals[k, slot] for slot in slots], k)
    wide_edge = jnp.concatenate([edge, edge], axis=0)

    keys = [kbuf[pl.ds(8 + p, 16, stride=4), :] for p in range(4)]
    fourth = [pl.ds(8 + p, 16, stride=4) for p in range(4)]
    planes = [
        [jnp.where(wide_edge, nside[k, rows, :], nmain[k, rows, :]) for rows in fourth]
        for k in range(FRACTIONS)
    ]
    for d in range(7):
        kept = [0.0] * FRACTIONS
        for r in range(3):
            hits = [keys[p] == r * 7 + d for p in range(4)]
            for k in range(FRACTIONS):
                acc = jnp.where(hits[0], planes[k][0], 0.0)
                for p in range(1, 4):
                    acc = acc + jnp.where(hits[p], planes[k][p], 0.0)
                kept[k] = kept[k] + (acc if r == 1 else roll(acc, r - 1, 0))
        for k in range(FRACTIONS):
            high = kept[k].astype(jnp.bfloat16)
            rows = slice(16 * k, 16 * k + 16)
            mhi[rows, 128 * d : 128 * d + 128] = high
            mlo[rows, 128 * d : 128 * d + 128] = (kept[k] - high.astype(f32)).astype(jnp.bfloat16)
    res = jnp.dot(mhi[...], sel[...], preferred_element_type=f32)
    res = 25.0 * (res + jnp.dot(mlo[...], sel[...], preferred_element_type=f32))
    parts = [res[16 * k : 16 * k + 16] for k in range(FRACTIONS)]
    nsum[...] = (parts[0] + parts[1]) + (parts[2] + parts[3])
    for n in range(2):
        pair = parts[2 * n] + roll(parts[2 * n + 1], 64, 1)
        for r in range(COLS):
            tot[r, :, 128 * n : 128 * n + 128] = pair[r : r + 1, :]

    def send_sum(r):
        remote(tot.at[r], rs.at[C], ph_send, ph_recv, (R, r)).start()

    for r in others:
        send_sum(r)

    @pl.when(left)
    def _():
        remote(nsum, nrx.at[0], ns_send.at[0], ns_recv.at[0], (R, C - 1)).start()

    @pl.when(right)
    def _():
        remote(nsum, nrx.at[1], ns_send.at[1], ns_recv.at[1], (R, C + 1)).start()

    for r in mates:
        send_sum(r)
    rs[C] = tot[C]

    step(before_last, after_last, False)
    for q in range(7):
        natural([after_last[q, s] for s in slots], 4 + q)
    for q in range(7):
        for g in range(1, 9):
            rows = slice(8 * g, 8 * g + 8)
            o_fields[q, rows, :] = jnp.where(edge, nside[4 + q, rows, :], nmain[4 + q, rows, :])

    for n, (sends, src, dst, device, _) in enumerate(plan):

        @pl.when(sends)
        def _(n=n, src=src, dst=dst, device=device):
            remote(src, dst, nb_send.at[n], nb_recv.at[n], device).wait_send()

    pltpu.make_async_copy(strips.at[pl.ds(0, 15)], band.at[pl.ds(0, 15)], st_send.at[0]).wait()

    @pl.when(jnp.logical_or(both(C <= 2, up), both(C >= COLS - 3, down)))
    def _():
        pltpu.make_async_copy(strips, band.at[pl.ds(0, 16)], st_send.at[1]).wait()

    @pl.when(right)
    def _():
        pltpu.make_async_copy(nsum, nrx.at[0], ns_recv.at[0]).wait()

    @pl.when(left)
    def _():
        pltpu.make_async_copy(nsum, nrx.at[1], ns_recv.at[1]).wait()

    for e in range(16):
        band2[e : e + 1, :] = band[3 + e]
    wnew[1:17, :] = band2[...] + (nsum[...] + roll(nrx[0], 32, 1) + roll(nrx[1], -32, 1))
    wide = [jnp.broadcast_to(wnew[n : n + 1, :], (8, 128)) for n in range(18)]
    inner = [slice(8 + 8 * g, 16 + 8 * g) for g in range(8)]
    found = looked_up(wide, [(g, ibuf[r, :], rbuf[r, :]) for g, r in enumerate(inner)])
    for g, value in enumerate(found):
        o_fine[8 * g : 8 * g + 8, :] = value

    pltpu.make_async_copy(tot.at[pl.ds(0, 15)], rs.at[pl.ds(0, 15)], ph_recv).wait()
    row_lane = lax.broadcasted_iota(i32, (1, 128), 1)
    row_low = row_lane < 64
    lines = [[jnp.zeros((1, 128), f32) for _ in range(4)] for _ in range(FRACTIONS)]
    for s in range(COLS):
        q, m = divmod(s, 4)
        for n in range(2):
            pair = rs[s, :, 128 * n : 128 * n + 128]
            for half in range(2):
                line = lines[2 * n + half]
                piece = jnp.where(row_low, 0.0, pair) if half else jnp.where(row_low, pair, 0.0)
                piece = roll(piece, 32 * m - 8 - 64 * half, 1)
                if m == 0:
                    line[q] = line[q] + jnp.where(row_low, piece, 0.0)
                    if q > 0:
                        line[q - 1] = line[q - 1] + jnp.where(row_low, 0.0, piece)
                elif m == 3:
                    line[q] = line[q] + jnp.where(row_low, 0.0, piece)
                    if q < 3:
                        line[q + 1] = line[q + 1] + jnp.where(row_low, piece, 0.0)
                else:
                    line[q] = line[q] + piece
    for q in range(4):
        cols = slice(128 * q, 128 * q + 128)
        total = None
        for k in range(FRACTIONS):
            line = lines[k][q]
            o_dep[k, :, cols] = line
            total = line if k == 0 else total + line
        o_bed[:, cols] = bedv[:, cols] + total
    @pl.when(left)
    def _():
        pltpu.make_async_copy(nsum, nrx.at[0], ns_send.at[0]).wait()

    @pl.when(right)
    def _():
        pltpu.make_async_copy(nsum, nrx.at[1], ns_send.at[1]).wait()

    pltpu.make_async_copy(tot.at[pl.ds(0, 15)], rs.at[pl.ds(0, 15)], ph_send).wait()


def handed_on(fields, fine, bed, dep, o_depth, o_disch, o_sed, o_fine, o_bed, o_dep, sem):
    mid = pl.ds(8, 64)
    pairs = (
        (fields.at[0, mid], o_depth),
        (fields.at[pl.ds(1, 2), mid], o_disch),
        (fields.at[pl.ds(3, 4), mid], o_sed),
        (fine, o_fine),
        (bed, o_bed),
        (dep, o_dep),
    )
    copies = [pltpu.make_async_copy(src, dst, sem.at[n]) for n, (src, dst) in enumerate(pairs)]
    for copy in copies:
        copy.start()
    for copy in copies:
        copy.wait()


def local(water_depth, discharge, sediment, bed_level, cell_map, wet_mask, sediment_params):
    hbm = pl.BlockSpec(memory_space=pl.ANY)
    dma = pltpu.SemaphoreType.DMA
    vmem = pl.BlockSpec(memory_space=pltpu.VMEM)
    bf16 = jnp.bfloat16
    plane = (SLOTS, 8, 128)
    scratch = [
        ((9, 80, 128), f32),
        ((2, 64, 128), i32),
        ((1, 512), f32),
        ((10, 8, 128), f32),
        ((2, 13, 8, 128), f32),
        ((16, 1, 128), f32),
        ((22, 1, 128), f32),
        ((16, 128), f32),
        ((80, 128), f32),
        ((2, 80, 128), f32),
        ((80, 128), i32),
        ((80, 128), i32),
        ((80, 128), i32),
        ((80, 128), i32),
        ((80, 128), i32),
        ((7, *plane), f32),
        ((7, *plane), f32),
        (plane, f32),
        (plane, f32),
        (plane, f32),
        (plane, f32),
        (plane, f32),
        (plane, f32),
        ((3, 4, 8, 128), f32),
        ((4, *plane), f32),
        ((11, 80, 128), f32),
        ((11, 80, 128), f32),
        ((896, 128), bf16),
        ((64, 896), bf16),
        ((64, 896), bf16),
        ((16, 1, 256), f32),
        ((16, 128), f32),
        ((2, 16, 128), f32),
        ((16, 1, 256), f32),
        ((24, 128), f32),
    ]
    results = tuple(
        jax.ShapeDtypeStruct(shape, f32)
        for shape in ((64, 128), (2, 64, 128), (4, 64, 128), (64, 128), (1, 512), (4, 1, 512))
    )
    made = pl.pallas_call(
        kernel,
        out_shape=tuple(
            pltpu.VMEM(shape, f32) for shape in ((7, 80, 128), (64, 128), (1, 512), (4, 1, 512))
        ),
        in_specs=[hbm] * 7,
        out_specs=(vmem,) * 4,
        scratch_shapes=[pltpu.SMEM((3, FRACTIONS), f32)]
        + [pltpu.VMEM(shape, dtype) for shape, dtype in scratch]
        + [dma((7,)), dma((8,)), dma((8,)), dma((2,)), dma((3,)), dma(()), dma(()), dma((2,)), dma((2,))],
        compiler_params=pltpu.CompilerParams(
            collective_id=0, has_side_effects=True, vmem_limit_bytes=56 * 1024 * 1024
        ),
    )(water_depth, discharge, sediment, bed_level, cell_map, wet_mask, sediment_params)
    return pl.pallas_call(
        handed_on,
        out_shape=results,
        in_specs=[hbm] * 4,
        out_specs=(hbm,) * 6,
        scratch_shapes=[dma((6,))],
    )(*(pltpu.with_memory_space_constraint(x, pltpu.VMEM) for x in made))


def solution(mesh):
    placed = (
        P("row", "col"),
        P(None, "row", "col"),
        P(None, "row", "col"),
        P(("row", "col"), None),
        P("row", "col"),
        P("row", "col"),
        P(),
    )
    return jax.shard_map(
        local,
        mesh=mesh,
        in_specs=placed,
        out_specs=(
            P("row", "col"),
            P(None, "row", "col"),
            P(None, "row", "col"),
            P("row", "col"),
            P(("row", "col"), None),
            P(None, ("row", "col"), None),
        ),
        check_vma=False,
    )
```
